32 devices in a mesh: parts: 2 (over y), node: 4 (over x, core), local: 4 (over z).
Axes of the slice: x: 2, y: 2, z: 4, core: 2. Of those that a mesh axis runs over, the one named last changes fastest.
Arguments:
- tokens: bfloat16 [256, 7168], P(('parts', 'node', 'local')), parts along dimension 0, may hold values from -6 to 6
- expert_ids: int32 [256, 4], P(('parts', 'node', 'local')), parts along dimension 0, may hold values from 0 to 7, all different within a row; in each aligned block of 8 rows (0 to 7, 8 to 15, ...) at most 8 rows name the same one
- route_weights: float32 [256, 4], P(('parts', 'node', 'local')), parts along dimension 0, may hold values from 0.05 to 1
- expert_slot: int32 [8], replicated, may hold values from 0 to 7, each once
- w_gate: bfloat16 [8, 7168, 2048], P('node', None, 'local'), may hold values from -0.0625 to 0.0625
- w_up: bfloat16 [8, 7168, 2048], P('node', None, 'local'), may hold values from -0.0625 to 0.0625
- w_down: bfloat16 [8, 2048, 7168], P('node', 'local'), may hold values from -0.125 to 0.125
Outputs:
- combined: bfloat16 [256, 7168], P(('parts', 'node', 'local')), parts along dimension 0
The draws below stay inside these ranges and needn't reach their ends.
There are 2 independent parts, one for each index of `parts`. The reference program is written for one: setup_inputs(seed, part) draws one part's arguments, and reference() takes and returns one part's arrays. A program takes and returns all parts, laid end to end along the dimension named above; an argument that names none is the same for every part. Nothing has to cross between parts.
Inputs may be any that keep to these rules, and one draw needn't show every extreme that they name: `expert_ids`: each row names 4 different experts. Among the 8 rows of one device at most 8 name any one expert, a bound that some block reaches. Every expert is named somewhere. `expert_slot`: each slot holds exactly one expert.
All inputs are finite; a program needn't handle non-finite values.
Results may differ from the reference program's by a relative error of at most 0.013.
Values may be sent and summed in bfloat16 or wider, within the bound.
No kernel may reach another device: no remote copies, remote signals or barrier semaphores. Data moves between devices by JAX's collectives and lax.ppermute only.
A program may use at most 128 MiB of HBM per device.

```python
import math
import jax
import jax.numpy as jnp
import numpy as np
from jax import lax

D = 7168
FF = 2048
TOK_DEV = 8
TOPK = 4
EXPERTS = 8
CAP = 8
HID_DEV = 512
TOKENS = 128
N_LOCAL = 4


def level_of(own_key, shape, pieces, smallest, largest):
    gain = 1.0
    for axis_at, shards_of in pieces:
        steps = jax.random.uniform(jax.random.fold_in(jax.random.fold_in(own_key, 6), axis_at), (shards_of,), jnp.float32, smallest / len(pieces), largest / len(pieces))
        gain = gain * jnp.repeat(jnp.exp(steps), shape[axis_at] // shards_of).reshape((-1,) + (1,) * (len(shape) - 1 - axis_at))
    return gain


def deal_out(rng, own, number, rows, number_of, top, limit, lean):
    ranking = jax.random.permutation(rng, number_of)
    crowded, usual = load_shares(number_of, rows * top, limit, lean, True), load_shares(number_of, rows * top, limit, lean, False)
    places = jnp.arange(number_of)

    def named(sizes, turn):
        used = int((sizes > 0).sum())
        fixed = max(1, used // 4)
        passed = fixed + (places - fixed + turn * (used - fixed)) % max(1, number_of - fixed)
        return jnp.zeros((number_of,), jnp.int32).at[ranking[jnp.where(places < fixed, places, passed)]].set(jnp.asarray(sizes, jnp.int32))

    sizes = jnp.where(number % 4 == 0, named(crowded, number // 4), named(usual, number - number // 4 - 1))
    mixed = jax.random.permutation(jax.random.fold_in(own, 3), number_of)
    donor, receiver = mixed[0:number_of // 2 * 2:2], mixed[1:number_of // 2 * 2:2]
    slack = jnp.minimum(sizes[donor] - 1, limit - sizes[receiver]) // 2
    slack = jnp.where((donor == ranking[0]) | (receiver == ranking[0]) | (sizes[receiver] == 0), 0, jnp.maximum(slack, 0))
    passed = jax.random.randint(jax.random.fold_in(own, 4), (number_of // 2,), 0, 1 << 20) % (slack + 1)
    sizes = sizes.at[donor].add(-passed).at[receiver].add(passed)
    labels = jnp.searchsorted(jnp.cumsum(sizes), jnp.arange(rows * top), side="right").astype(jnp.int32)
    listing = labels.reshape(top, rows).T
    listing = listing[jax.random.permutation(jax.random.fold_in(own, 1), rows)]
    turn = jax.random.randint(jax.random.fold_in(own, 2), (rows, 1), 0, top)
    return jnp.take_along_axis(listing, (jnp.arange(top)[None, :] + turn) % top, axis=1)


def load_shares(amount, total, reach, slope, full):
    weights = [(1 << 20) // math.isqrt(grade ** slope) + 1 for grade in range(1, amount + 1)]
    largest = reach if full else min(reach, max(-(-total // amount), total * weights[0] // sum(weights)))
    least = 1 if total - largest >= amount - 1 else 0
    given, rest = [largest] + [least] * (amount - 1), total - largest - least * (amount - 1)
    while rest > 0:
        free = [i for i in range(1, amount) if given[i] < largest] or [i for i in range(1, amount) if given[i] < reach]
        mass, budget = sum([weights[i] for i in free]), rest
        for i in free:
            more = min(reach - given[i], max(1, budget * weights[i] // mass), rest)
            given[i] = given[i] + more
            rest = rest - more
    return np.array(given)


def gaussian(rng, shape, deviation, reach, split=(), kind=jnp.bfloat16):
    values = jax.random.normal(rng, shape, jnp.float32) * deviation
    if len(split) > 0:
        values = level_of(rng, shape, split, -0.22, 0.18) * values
    return jnp.clip(values, min=-reach, max=reach).astype(kind)


def setup_inputs(seed: int = 0, part: int = 0) -> dict:
    splits = jax.random.split(jax.random.key(seed), 8)
    part_splits = jax.random.split(jax.random.fold_in(splits[7], part), 8)
    tokens = gaussian(part_splits[0], (TOKENS, D), 1.0, 6.0, ((0, 16),))
    expert_ids_keys = jax.random.split(jax.random.fold_in(part_splits[1], 1), TOKENS // TOK_DEV)
    expert_ids_turns = jax.random.permutation(jax.random.fold_in(part_splits[1], 3), TOKENS // TOK_DEV)
    expert_ids = jax.vmap(lambda own, number: deal_out(jax.random.fold_in(part_splits[1], 2), own, number, TOK_DEV, EXPERTS, TOPK, CAP, 2))(expert_ids_keys, expert_ids_turns).reshape((TOKENS, TOPK))
    route_weights = jnp.clip(0.05 + 0.95 * jax.random.uniform(part_splits[2], (TOKENS, TOPK), jnp.float32) ** level_of(part_splits[2], (TOKENS, TOPK), ((0, 16),), -0.2, 0.2), 0.05, 1.0)
    expert_slot = jax.random.permutation(splits[3], EXPERTS).astype(jnp.int32)
    w_gate = gaussian(splits[4], (EXPERTS, D, FF), D ** -0.5, 0.0625, ((0, 4), (2, 4)))
    w_up = gaussian(splits[5], (EXPERTS, D, FF), D ** -0.5, 0.0625, ((0, 4), (2, 4)))
    w_down = gaussian(splits[6], (EXPERTS, FF, D), FF ** -0.5, 0.125, ((0, 4), (1, 4)))
    return dict(tokens=tokens, expert_ids=expert_ids, route_weights=route_weights, expert_slot=expert_slot, w_gate=w_gate, w_up=w_up, w_down=w_down)


def apply_expert(operands):
    rows_in, gate_w, up_w, down_w = operands
    rows_f = rows_in.astype(jnp.float32)
    gate_act = jnp.dot(rows_f, gate_w.astype(jnp.float32))
    up_act = jnp.dot(rows_f, up_w.astype(jnp.float32))
    hidden = (jax.nn.silu(gate_act) * up_act).astype(jnp.bfloat16)
    hidden = lax.optimization_barrier(hidden).astype(jnp.float32)
    partials = jnp.einsum('rph,phd->rpd', hidden.reshape(-1, N_LOCAL, HID_DEV),
                          down_w.astype(jnp.float32).reshape(N_LOCAL, HID_DEV, D))
    partials = lax.optimization_barrier(partials.astype(jnp.bfloat16)).astype(jnp.float32)
    return jnp.sum(partials, axis=1).astype(jnp.bfloat16)


def reference(tokens, expert_ids, route_weights, expert_slot, w_gate, w_up, w_down):
    blocks = TOKENS // TOK_DEV
    slot_of = expert_slot[expert_ids].astype(jnp.int32)
    onehot = (slot_of[..., None] == jnp.arange(EXPERTS, dtype=jnp.int32)).astype(jnp.int32)
    per_token = jnp.sum(onehot, axis=1).reshape(blocks, TOK_DEV, EXPERTS)
    earlier = (jnp.cumsum(per_token, axis=1) - per_token).reshape(TOKENS, EXPERTS)
    position = jnp.sum(onehot * earlier[:, None, :], axis=-1).astype(jnp.int32)
    owner_block = (jnp.arange(TOKENS, dtype=jnp.int32) // TOK_DEV)[:, None]
    row_of = (owner_block * CAP + position).astype(jnp.int32)
    filled = jnp.zeros((EXPERTS, blocks * CAP, D), tokens.dtype)
    filled = filled.at[slot_of, row_of].set(jnp.broadcast_to(tokens[:, None, :], (TOKENS, TOPK, D)))
    expert_out = lax.map(apply_expert, (filled, w_gate, w_up, w_down))
    picked = expert_out[slot_of, row_of].astype(jnp.float32)
    combined = jnp.sum(route_weights[..., None].astype(jnp.float32) * picked, axis=1)
    return combined.astype(jnp.bfloat16)
```

```python
import jax
import jax.numpy as jnp
from jax import lax
from jax.sharding import PartitionSpec as P

LANES = 128


def slot_weights(expert_ids, route_weights, expert_slot):
    experts = expert_slot.shape[0]
    slots = jnp.arange(experts, dtype=jnp.int32)
    lookup = expert_ids[..., None] == slots
    slot_ids = jnp.sum(jnp.where(lookup, expert_slot, 0), axis=-1)
    hit = slot_ids[..., None] == slots
    return jnp.sum(jnp.where(hit, route_weights[..., None], 0.0), axis=1)


def three_pieces(values):
    first = lax.reduce_precision(values, 8, 7)
    rest = values - first
    second = lax.reduce_precision(rest, 8, 7)
    third = rest - second
    return [piece.astype(jnp.bfloat16) for piece in (first, second, third)]


def per_device(tokens, expert_ids, route_weights, expert_slot, w_gate, w_up, w_down):
    members, width, hid = w_gate.shape
    slots = expert_slot.shape[0]
    weights = slot_weights(expert_ids, route_weights, expert_slot)
    pieces = three_pieces(weights)
    packed = jnp.concatenate([tokens] + pieces, axis=1)
    packed = jnp.pad(packed, ((0, 0), (0, -packed.shape[1] % LANES)))
    gathered = lax.all_gather(packed, ("node", "local"), axis=0, tiled=True)
    rows = gathered[:, :width]
    tail = gathered[:, width : width + 3 * slots].astype(jnp.float32)
    mine = tail[:, :slots] + tail[:, slots : 2 * slots] + tail[:, 2 * slots :]
    mine = lax.dynamic_slice_in_dim(mine, lax.axis_index("node") * members, members, axis=1)
    gate = jnp.einsum("td,edh->eth", rows, w_gate, preferred_element_type=jnp.float32)
    up = jnp.einsum("td,edh->eth", rows, w_up, preferred_element_type=jnp.float32)
    hidden = (jax.nn.silu(gate) * up * mine.T[..., None]).astype(jnp.bfloat16)
    result = jnp.einsum("eth,ehd->td", hidden, w_down, preferred_element_type=jnp.float32)
    return lax.psum_scatter(
        result.astype(jnp.bfloat16), ("node", "local"), scatter_dimension=0, tiled=True
    )


def solution(mesh):
    rows = P(("parts", "node", "local"), None)
    in_specs = (
        rows,
        rows,
        rows,
        P(),
        P("node", None, "local"),
        P("node", None, "local"),
        P("node", "local", None),
    )
    return jax.shard_map(
        per_device, mesh=mesh, in_specs=in_specs, out_specs=rows, check_vma=False
    )
```

```python
import functools

import jax
import jax.numpy as jnp
from jax import lax
from jax.experimental import pallas as pl
from jax.experimental.pallas import tpu as pltpu
from jax.sharding import PartitionSpec as P

LANES = 128
MAX_BLOCKS = 16
K_TILE = 512
N_TILE = 512
OUT_CHUNKS = 2
VMEM_LIMIT = 30 * 2**20


def pack_kernel(slot_ref, tokens_ref, ids_ref, route_ref, out_ref):
    rows, width = tokens_ref.shape
    experts = slot_ref.shape[0]
    column = lax.broadcasted_iota(jnp.int32, (rows, LANES), 1)
    weights = jnp.zeros((rows, LANES), jnp.float32)
    for expert in range(experts):
        at_slot = lax.rem(column, experts) == slot_ref[expert]
        for k in range(ids_ref.shape[1]):
            named = ids_ref[:, k : k + 1] == expert
            weights += jnp.where(at_slot & named, route_ref[:, k : k + 1], 0.0)
    first = weights.astype(jnp.bfloat16).astype(jnp.float32)
    second = (weights - first).astype(jnp.bfloat16).astype(jnp.float32)
    third = weights - first - second
    tail = jnp.where(column < experts, first, jnp.where(column < 2 * experts, second, third))
    out_ref[:, :width] = tokens_ref[...]
    out_ref[:, width:] = jnp.where(column < 3 * experts, tail, 0.0).astype(jnp.bfloat16)


def pack(tokens, expert_ids, route_weights, expert_slot):
    rows, width = tokens.shape
    vmem = pl.BlockSpec(memory_space=pltpu.VMEM)
    return pl.pallas_call(
        pack_kernel,
        out_shape=jax.ShapeDtypeStruct((rows, width + LANES), jnp.bfloat16),
        in_specs=[pl.BlockSpec(memory_space=pltpu.SMEM), vmem, vmem, vmem],
        out_specs=vmem,
        name="pack",
    )(expert_slot, tokens, expert_ids, route_weights)


def hidden_kernel(experts, *refs):
    *pieces, gate_ref, up_ref, out_ref, gate_acc, up_acc = refs
    step = pl.program_id(0)
    members, k_tile, hid = gate_ref.shape
    width = pieces[0].shape[1] - LANES
    columns = pl.ds(pl.multiple_of(step * k_tile, LANES), k_tile)
    x = jnp.concatenate([piece[:, columns] for piece in pieces], axis=0)

    @pl.when(step == 0)
    def _():
        gate_acc[...] = jnp.zeros_like(gate_acc)
        up_acc[...] = jnp.zeros_like(up_acc)

    for member in range(members):
        for ref, acc in ((gate_ref, gate_acc), (up_ref, up_acc)):
            acc[member] += jnp.dot(x, ref[member], preferred_element_type=jnp.float32)

    @pl.when(step == pl.num_programs(0) - 1)
    def _():
        tail = jnp.concatenate([piece[:, width:] for piece in pieces], axis=0)
        tail = tail.astype(jnp.float32)
        column = lax.broadcasted_iota(jnp.int32, tail.shape, 1)
        for member in range(members):
            slot = lax.axis_index("node") * members + member
            mine = (lax.rem(column, experts) == slot) & (column < 3 * experts)
            weight = jnp.sum(jnp.where(mine, tail, 0.0), axis=1, keepdims=True)
            gate = gate_acc[member]
            hidden = gate / (1.0 + jnp.exp(-gate)) * up_acc[member] * weight
            out_ref[:, member * hid : (member + 1) * hid] = hidden.astype(jnp.bfloat16)


def hidden_units(pieces, w_gate, w_up, experts):
    members, width, hid = w_gate.shape
    rows = sum(piece.shape[0] for piece in pieces)
    whole = pl.BlockSpec(memory_space=pltpu.VMEM)
    weights = pl.BlockSpec((members, K_TILE, hid), lambda k: (0, k, 0))
    return pl.pallas_call(
        functools.partial(hidden_kernel, experts),
        grid=(width // K_TILE,),
        out_shape=jax.ShapeDtypeStruct((rows, members * hid), jnp.bfloat16),
        in_specs=[whole] * len(pieces) + [weights, weights],
        out_specs=pl.BlockSpec((rows, members * hid), lambda k: (0, 0)),
        scratch_shapes=[pltpu.VMEM((members, rows, hid), jnp.float32)] * 2,
        compiler_params=pltpu.CompilerParams(vmem_limit_bytes=VMEM_LIMIT),
        cost_estimate=pl.CostEstimate(
            flops=4 * rows * members * width * hid,
            bytes_accessed=4 * members * width * hid,
            transcendentals=rows * members * hid,
        ),
        name="hidden",
    )(*pieces, w_gate, w_up)


def down_kernel(hidden_ref, down_ref, keep_ref, send_ref):
    members, hid, _ = down_ref.shape
    half = keep_ref.shape[0]
    total = sum(
        jnp.dot(
            hidden_ref[:, member * hid : (member + 1) * hid],
            down_ref[member],
            preferred_element_type=jnp.float32,
        )
        for member in range(members)
    ).astype(jnp.bfloat16)
    keep_ref[...] = total[:half]
    send_ref[...] = total[half:]


def down(hidden, w_down, chunk, chunks):
    members, hid, width = w_down.shape
    rows = hidden.shape[0]
    steps = width // chunks // N_TILE
    half = pl.BlockSpec((rows // 2, N_TILE), lambda j: (0, j))
    return pl.pallas_call(
        down_kernel,
        grid=(steps,),
        out_shape=[jax.ShapeDtypeStruct((rows // 2, width // chunks), jnp.bfloat16)] * 2,
        in_specs=[
            pl.BlockSpec((rows, members * hid), lambda j: (0, 0)),
            pl.BlockSpec((members, hid, N_TILE), lambda j: (0, 0, chunk * steps + j)),
        ],
        out_specs=[half, half],
        compiler_params=pltpu.CompilerParams(vmem_limit_bytes=VMEM_LIMIT),
        cost_estimate=pl.CostEstimate(
            flops=2 * rows * members * hid * width // chunks,
            bytes_accessed=2 * members * hid * width // chunks,
            transcendentals=0,
        ),
        name="down",
    )(hidden, w_down)


def swap(value, axis, bits):
    size = lax.axis_size(axis)
    return lax.ppermute(value, axis, [(i, i ^ bits) for i in range(size)])


def gather_blocks(own):
    chips = lax.axis_size("node") // 2
    along = [own] + [swap(own, "local", dz) for dz in range(1, lax.axis_size("local"))]
    chip = along + [swap(piece, "node", 2 * dx) for dx in range(1, chips) for piece in along]
    return chip + [swap(piece, "node", 1) for piece in chip]


def add(*terms):
    return sum(term.astype(jnp.float32) for term in terms).astype(jnp.bfloat16)


def reduce_blocks(keep, send, rows):
    places = lax.axis_size("local")
    chips = lax.axis_size("node") // 2
    chip = add(keep, swap(send, "node", 1)).reshape(chips, places * rows, -1)
    along = add(chip[0], *[swap(chip[dx], "node", 2 * dx) for dx in range(1, chips)])
    along = along.reshape(places, rows, -1)
    return add(along[0], *[swap(along[dz], "local", dz) for dz in range(1, places)])


def by_permutes(tokens, expert_ids, route_weights, expert_slot, w_gate, w_up, w_down):
    rows = tokens.shape[0]
    pieces = gather_blocks(pack(tokens, expert_ids, route_weights, expert_slot))
    hidden = hidden_units(pieces, w_gate, w_up, expert_slot.shape[0])
    outs = []
    for chunk in range(OUT_CHUNKS):
        keep, send = down(hidden, w_down, chunk, OUT_CHUNKS)
        outs.append(reduce_blocks(keep, send, rows))
    return jnp.concatenate(outs, axis=1)


def by_collectives(tokens, expert_ids, route_weights, expert_slot, w_gate, w_up, w_down):
    members, width, _ = w_gate.shape
    experts = expert_slot.shape[0]
    packed = pack(tokens, expert_ids, route_weights, expert_slot)
    gathered = lax.all_gather(packed, ("node", "local"), axis=0, tiled=True)
    rows = gathered[:, :width]
    tail = gathered[:, width : width + 3 * experts].astype(jnp.float32)
    weights = tail.reshape(-1, 3, experts).sum(axis=1)
    mine = lax.dynamic_slice_in_dim(weights, lax.axis_index("node") * members, members, axis=1)
    gate = jnp.einsum("td,edh->eth", rows, w_gate, preferred_element_type=jnp.float32)
    up = jnp.einsum("td,edh->eth", rows, w_up, preferred_element_type=jnp.float32)
    hidden = (jax.nn.silu(gate) * up * mine.T[..., None]).astype(jnp.bfloat16)
    result = jnp.einsum("eth,ehd->td", hidden, w_down, preferred_element_type=jnp.float32)
    return lax.psum_scatter(
        result.astype(jnp.bfloat16), ("node", "local"), scatter_dimension=0, tiled=True
    )


def per_device(*args):
    blocks = lax.axis_size("node") * lax.axis_size("local")
    return (by_permutes if blocks <= MAX_BLOCKS else by_collectives)(*args)


def solution(mesh):
    rows = P(("parts", "node", "local"), None)
    in_specs = (
        rows,
        rows,
        rows,
        P(),
        P("node", None, "local"),
        P("node", None, "local"),
        P("node", "local", None),
    )
    return jax.shard_map(
        per_device, mesh=mesh, in_specs=in_specs, out_specs=rows, check_vma=False
    )
```

```python
import functools

import jax
import jax.numpy as jnp
from jax import lax
from jax.experimental import pallas as pl
from jax.experimental.pallas import tpu as pltpu
from jax.sharding import PartitionSpec as P

LANES = 128
K_TILE = 1024
N_TILE = 512
OUT_CHUNKS = 1
VMEM_LIMIT = 8 * 2**20


def pack_kernel(slot_ref, ids_ref, route_ref, tokens_ref, out_ref):
    rows, width = tokens_ref.shape
    experts = slot_ref.shape[0]
    row = lax.broadcasted_iota(jnp.int32, (rows, LANES), 0)
    column = lax.broadcasted_iota(jnp.int32, (rows, LANES), 1)
    slot = lax.rem(column, experts)
    weights = jnp.zeros((rows, LANES), jnp.float32)
    for k in range(ids_ref.shape[0]):
        for token in range(rows):
            named = (row == token) & (slot == slot_ref[ids_ref[k, token]])
            weights = jnp.where(named, route_ref[k, token], weights)
    first = weights.astype(jnp.bfloat16).astype(jnp.float32)
    second = (weights - first).astype(jnp.bfloat16).astype(jnp.float32)
    third = weights - first - second
    tail = jnp.where(column < experts, first, jnp.where(column < 2 * experts, second, third))
    out_ref[:, :width] = tokens_ref[...]
    out_ref[:, width:] = jnp.where(column < 3 * experts, tail, 0.0).astype(jnp.bfloat16)


def pack(tokens, expert_ids, route_weights, expert_slot):
    rows, width = tokens.shape
    vmem = pl.BlockSpec(memory_space=pltpu.VMEM)
    smem = pl.BlockSpec(memory_space=pltpu.SMEM)
    return pl.pallas_call(
        pack_kernel,
        out_shape=jax.ShapeDtypeStruct((rows, width + LANES), jnp.bfloat16),
        in_specs=[smem, smem, smem, vmem],
        out_specs=vmem,
        compiler_params=pltpu.CompilerParams(vmem_limit_bytes=VMEM_LIMIT),
        name="pack",
    )(expert_slot, expert_ids.T, route_weights.T, tokens)


def fetch_kernel(weights_ref, out_ref):
    del weights_ref
    out_ref[...] = jnp.zeros_like(out_ref)


def fetch(weights):
    return pl.pallas_call(
        fetch_kernel,
        out_shape=jax.ShapeDtypeStruct((8, LANES), jnp.float32),
        in_specs=[pl.BlockSpec(memory_space=pl.ANY)],
        out_specs=pl.BlockSpec(memory_space=pltpu.VMEM),
        compiler_params=pltpu.CompilerParams(vmem_limit_bytes=VMEM_LIMIT, has_side_effects=True),
        name="fetch",
    )(weights)


def hidden_kernel(experts, *refs):
    *pieces, gate_ref, up_ref, out_ref, x_ref, gate_acc, up_acc = refs
    members, width, hid = gate_ref.shape
    steps = width // K_TILE

    def add_product(step, ref, acc):
        at = pl.ds(pl.multiple_of(step * K_TILE, K_TILE), K_TILE)
        for member in range(members):
            acc[member] += jnp.dot(
                x_ref[:, at], ref[member, at], preferred_element_type=jnp.float32
            )

    gate_acc[...] = jnp.zeros_like(gate_acc)
    up_acc[...] = jnp.zeros_like(up_acc)

    @pl.loop(0, steps)
    def _(step):
        at = pl.ds(pl.multiple_of(step * K_TILE, K_TILE), K_TILE)
        x_ref[:, at] = jnp.concatenate([piece[:, at] for piece in pieces], axis=0)
        add_product(step, gate_ref, gate_acc)

    @pl.loop(0, steps)
    def _(step):
        add_product(step, up_ref, up_acc)

    tail = jnp.concatenate([piece[:, width:] for piece in pieces], axis=0)
    tail = tail.astype(jnp.float32)
    column = lax.broadcasted_iota(jnp.int32, tail.shape, 1)
    for member in range(members):
        slot = lax.axis_index("node") * members + member
        mine = (lax.rem(column, experts) == slot) & (column < 3 * experts)
        weight = jnp.sum(jnp.where(mine, tail, 0.0), axis=1, keepdims=True)
        gate = gate_acc[member]
        hidden = gate / (1.0 + jnp.exp(-gate)) * up_acc[member] * weight
        out_ref[:, member * hid : (member + 1) * hid] = hidden.astype(jnp.bfloat16)


def hidden_units(pieces, w_gate, w_up, experts):
    members, width, hid = w_gate.shape
    rows = sum(piece.shape[0] for piece in pieces)
    vmem = pl.BlockSpec(memory_space=pltpu.VMEM)
    return pl.pallas_call(
        functools.partial(hidden_kernel, experts),
        out_shape=jax.ShapeDtypeStruct((rows, members * hid), jnp.bfloat16),
        in_specs=[vmem] * (len(pieces) + 2),
        out_specs=vmem,
        scratch_shapes=[
            pltpu.VMEM((rows, width), jnp.bfloat16),
            pltpu.VMEM((members, rows, hid), jnp.float32),
            pltpu.VMEM((members, rows, hid), jnp.float32),
        ],
        compiler_params=pltpu.CompilerParams(vmem_limit_bytes=VMEM_LIMIT),
        cost_estimate=pl.CostEstimate(
            flops=4 * rows * members * width * hid,
            bytes_accessed=4 * members * width * hid,
            transcendentals=rows * members * hid,
        ),
        name="hidden",
    )(*pieces, w_gate, w_up)


def down_kernel(chunk, hidden_ref, down_ref, keep_ref, send_ref):
    members, hid, _ = down_ref.shape
    half, width = keep_ref.shape

    @pl.loop(0, width // N_TILE)
    def _(step):
        here = pl.ds(pl.multiple_of(step * N_TILE, N_TILE), N_TILE)
        there = pl.ds(pl.multiple_of(chunk * width + step * N_TILE, N_TILE), N_TILE)
        total = sum(
            jnp.dot(
                hidden_ref[:, member * hid : (member + 1) * hid],
                down_ref[member, :, there],
                preferred_element_type=jnp.float32,
            )
            for member in range(members)
        ).astype(jnp.bfloat16)
        keep_ref[:, here] = total[:half]
        send_ref[:, here] = total[half:]


def down(hidden, w_down, chunk, chunks):
    members, hid, width = w_down.shape
    rows = hidden.shape[0]
    vmem = pl.BlockSpec(memory_space=pltpu.VMEM)
    return pl.pallas_call(
        functools.partial(down_kernel, chunk),
        out_shape=[jax.ShapeDtypeStruct((rows // 2, width // chunks), jnp.bfloat16)] * 2,
        in_specs=[vmem, vmem],
        out_specs=[vmem, vmem],
        compiler_params=pltpu.CompilerParams(vmem_limit_bytes=VMEM_LIMIT),
        cost_estimate=pl.CostEstimate(
            flops=2 * rows * members * hid * width // chunks,
            bytes_accessed=2 * members * hid * width // chunks,
            transcendentals=0,
        ),
        name="down",
    )(hidden, w_down)


CHIPS, PLACES = 2, 4


def to_core(value):
    return lax.ppermute(value, "node", [(i, i ^ 1) for i in range(2 * CHIPS)])


def to_chip(value):
    return lax.ppermute(value, "node", [(i, i ^ 2) for i in range(2 * CHIPS)])


def to_place(value, bits):
    return lax.ppermute(value, "local", [(i, i ^ bits) for i in range(PLACES)])


def gather_blocks(own, meanwhile):
    third = to_place(own, 3)
    first = to_place(own, 1)
    third, _ = lax.optimization_barrier((third, meanwhile()))
    along = [own, first, to_place(third, 1), third]
    chip = along + [to_chip(piece) for piece in along]
    return chip + [to_core(piece) for piece in chip]


def add(*terms):
    return sum(term.astype(jnp.float32) for term in terms).astype(jnp.bfloat16)


def reduce_blocks(keep, send, rows):
    half = PLACES * rows
    far = add(keep[half:], to_core(send[half:])).reshape(PLACES, rows, -1)
    near = add(keep[:half], to_core(send[:half])).reshape(PLACES, rows, -1)
    own, first, second, third = [
        add(near[place], to_chip(far[place])) for place in range(PLACES)
    ]
    third = add(third, to_place(second, 1))
    return add(own, to_place(first, 1), to_place(third, 3))


def by_permutes(tokens, expert_ids, route_weights, expert_slot, w_gate, w_up, w_down):
    rows = tokens.shape[0]
    own = pack(tokens, expert_ids, route_weights, expert_slot)
    pieces = gather_blocks(own, lambda: fetch(w_gate))
    hidden = hidden_units(pieces, w_gate, w_up, expert_slot.shape[0])
    outs = []
    for chunk in range(OUT_CHUNKS):
        keep, send = down(hidden, w_down, chunk, OUT_CHUNKS)
        outs.append(reduce_blocks(keep, send, rows))
    return jnp.concatenate(outs, axis=1)


def by_collectives(tokens, expert_ids, route_weights, expert_slot, w_gate, w_up, w_down):
    members, width, _ = w_gate.shape
    experts = expert_slot.shape[0]
    packed = pack(tokens, expert_ids, route_weights, expert_slot)
    gathered = lax.all_gather(packed, ("node", "local"), axis=0, tiled=True)
    rows = gathered[:, :width]
    tail = gathered[:, width : width + 3 * experts].astype(jnp.float32)
    weights = tail.reshape(-1, 3, experts).sum(axis=1)
    mine = lax.dynamic_slice_in_dim(weights, lax.axis_index("node") * members, members, axis=1)
    gate = jnp.einsum("td,edh->eth", rows, w_gate, preferred_element_type=jnp.float32)
    up = jnp.einsum("td,edh->eth", rows, w_up, preferred_element_type=jnp.float32)
    hidden = (jax.nn.silu(gate) * up * mine.T[..., None]).astype(jnp.bfloat16)
    result = jnp.einsum("eth,ehd->td", hidden, w_down, preferred_element_type=jnp.float32)
    return lax.psum_scatter(
        result.astype(jnp.bfloat16), ("node", "local"), scatter_dimension=0, tiled=True
    )


def per_device(*args):
    small = (lax.axis_size("node"), lax.axis_size("local")) == (2 * CHIPS, PLACES)
    return (by_permutes if small else by_collectives)(*args)


def solution(mesh):
    rows = P(("parts", "node", "local"), None)
    in_specs = (
        rows,
        rows,
        rows,
        P(),
        P("node", None, "local"),
        P("node", None, "local"),
        P("node", "local", None),
    )
    return jax.shard_map(
        per_device, mesh=mesh, in_specs=in_specs, out_specs=rows, check_vma=False
    )
```

```python
import functools

import jax
import jax.numpy as jnp
from jax import lax
from jax.experimental import pallas as pl
from jax.experimental.pallas import tpu as pltpu
from jax.sharding import PartitionSpec as P

LANES = 128
N_TILE = 256
OUT_CHUNKS = 1
VMEM_LIMIT = 4 * 2**20


def pack_kernel(*refs):
    inputs, out_ref, local, sems = refs[:4], refs[-6], refs[-5:-1], refs[-1]
    copies = [
        pltpu.make_async_copy(here, there, sems.at[i])
        for i, (here, there) in enumerate(zip(inputs, local))
    ]
    for copy in copies:
        copy.start()
    for copy in copies:
        copy.wait()
    tokens_ref, ids_ref, route_ref, slot_ref = local
    rows, width = tokens_ref.shape
    experts = slot_ref.shape[0]
    row = lax.broadcasted_iota(jnp.int32, (rows, LANES), 0)
    column = lax.broadcasted_iota(jnp.int32, (rows, LANES), 1)
    slot = lax.rem(column, experts)
    weights = jnp.zeros((rows, LANES), jnp.float32)
    for k in range(ids_ref.shape[0]):
        for token in range(rows):
            named = (row == token) & (slot == slot_ref[ids_ref[k, token]])
            weights = jnp.where(named, route_ref[k, token], weights)
    first = weights.astype(jnp.bfloat16).astype(jnp.float32)
    second = (weights - first).astype(jnp.bfloat16).astype(jnp.float32)
    third = weights - first - second
    tail = jnp.where(column < experts, first, jnp.where(column < 2 * experts, second, third))
    out_ref[:, :width] = tokens_ref[...]
    out_ref[:, width:] = jnp.where(column < 3 * experts, tail, 0.0).astype(jnp.bfloat16)


def pack(tokens, expert_ids, route_weights, expert_slot, *weights):
    rows, width = tokens.shape
    inputs = (tokens, expert_ids.T, route_weights.T, expert_slot)
    held = [pltpu.with_memory_space_constraint(each, pltpu.HBM) for each in inputs + weights]
    return pl.pallas_call(
        pack_kernel,
        out_shape=jax.ShapeDtypeStruct((rows, width + LANES), jnp.bfloat16),
        in_specs=[pl.BlockSpec(memory_space=pl.ANY)] * len(held),
        out_specs=pl.BlockSpec(memory_space=pltpu.VMEM),
        scratch_shapes=[
            pltpu.VMEM(tokens.shape, tokens.dtype),
            *[pltpu.SMEM(each.shape, each.dtype) for each in inputs[1:]],
            pltpu.SemaphoreType.DMA((len(inputs),)),
        ],
        compiler_params=pltpu.CompilerParams(vmem_limit_bytes=VMEM_LIMIT),
        name="pack",
    )(*held)


def hidden_kernel(experts, *refs):
    *pieces, gate_ref, up_ref, out_ref, x_ref, weight_ref = refs
    members, width, hid = gate_ref.shape
    x_ref[...] = jnp.concatenate([piece[:, :width] for piece in pieces], axis=0)
    tail = jnp.concatenate([piece[:, width:] for piece in pieces], axis=0)
    tail = tail.astype(jnp.float32)
    column = lax.broadcasted_iota(jnp.int32, tail.shape, 1)
    for member in range(members):
        slot = lax.axis_index("node") * members + member
        mine = (lax.rem(column, experts) == slot) & (column < 3 * experts)
        weight_ref[member] = jnp.sum(jnp.where(mine, tail, 0.0), axis=1, keepdims=True)
    tiles = hid // N_TILE

    @pl.loop(0, members * tiles)
    def _(step):
        member = step // tiles
        at = pl.ds(pl.multiple_of(lax.rem(step, tiles) * N_TILE, N_TILE), N_TILE)
        gate, up = [
            jnp.dot(x_ref[...], ref[member, :, at], preferred_element_type=jnp.float32)
            for ref in (gate_ref, up_ref)
        ]
        hidden = gate / (1.0 + jnp.exp(-gate)) * up * weight_ref[member]
        to = pl.ds(pl.multiple_of(step * N_TILE, N_TILE), N_TILE)
        out_ref[:, to] = hidden.astype(jnp.bfloat16)


def hidden_units(pieces, w_gate, w_up, experts):
    members, width, hid = w_gate.shape
    rows = sum(piece.shape[0] for piece in pieces)
    vmem = pl.BlockSpec(memory_space=pltpu.VMEM)
    return pl.pallas_call(
        functools.partial(hidden_kernel, experts),
        out_shape=jax.ShapeDtypeStruct((rows, members * hid), jnp.bfloat16),
        in_specs=[vmem] * (len(pieces) + 2),
        out_specs=vmem,
        scratch_shapes=[
            pltpu.VMEM((rows, width), jnp.bfloat16),
            pltpu.VMEM((members, rows, 1), jnp.float32),
        ],
        compiler_params=pltpu.CompilerParams(vmem_limit_bytes=VMEM_LIMIT),
        cost_estimate=pl.CostEstimate(
            flops=4 * rows * members * width * hid,
            bytes_accessed=4 * members * width * hid,
            transcendentals=rows * members * hid,
        ),
        name="hidden",
    )(*pieces, w_gate, w_up)


def down_kernel(chunk, hidden_ref, down_ref, far_ref, near_ref, *keep_refs):
    members, hid, _ = down_ref.shape
    width = far_ref.shape[1]
    part = far_ref.shape[0]
    outs = (*keep_refs, near_ref, far_ref)

    @pl.loop(0, width // N_TILE)
    def _(step):
        here = pl.ds(pl.multiple_of(step * N_TILE, N_TILE), N_TILE)
        there = pl.ds(pl.multiple_of(chunk * width + step * N_TILE, N_TILE), N_TILE)
        total = jnp.dot(
            hidden_ref[...],
            down_ref[:, :, there].reshape(members * hid, N_TILE),
            preferred_element_type=jnp.float32,
        ).astype(jnp.bfloat16)
        for i, ref in enumerate(outs):
            ref[:, here] = total[i * part : (i + 1) * part]


def down(hidden, w_down, chunk, chunks):
    members, hid, width = w_down.shape
    rows = hidden.shape[0]
    vmem = pl.BlockSpec(memory_space=pltpu.VMEM)
    return pl.pallas_call(
        functools.partial(down_kernel, chunk),
        out_shape=[jax.ShapeDtypeStruct((rows // 4, width // chunks), jnp.bfloat16)] * 4,
        in_specs=[vmem, vmem],
        out_specs=[vmem] * 4,
        compiler_params=pltpu.CompilerParams(vmem_limit_bytes=VMEM_LIMIT),
        cost_estimate=pl.CostEstimate(
            flops=2 * rows * members * hid * width // chunks,
            bytes_accessed=2 * members * hid * width // chunks,
            transcendentals=0,
        ),
        name="down",
    )(hidden, w_down)


CHIPS, PLACES = 2, 4


def to_core(value):
    return lax.ppermute(value, "node", [(i, i ^ 1) for i in range(2 * CHIPS)])


def to_chip(value):
    return lax.ppermute(value, "node", [(i, i ^ 2) for i in range(2 * CHIPS)])


def to_place(value, bits):
    return lax.ppermute(value, "local", [(i, i ^ bits) for i in range(PLACES)])


def gather_blocks(own):
    third = to_place(own, 3)
    first = to_place(own, 1)
    along = [own, first, to_place(third, 1), third]
    chip = along + [to_chip(piece) for piece in along]
    return chip + [to_core(piece) for piece in chip]


def add(*terms):
    return sum(term.astype(jnp.float32) for term in terms).astype(jnp.bfloat16)


def after(value, *others):
    return lax.optimization_barrier((value, *others))[0]


def reduce_blocks(other_far, other_near, near, far, rows):
    far = add(far, to_core(other_far)).reshape(PLACES, rows, -1)
    near = add(near, to_core(other_near)).reshape(PLACES, rows, -1)
    far_second = to_place(far[2], 1)
    first = add(near[1], to_chip(far[1]))
    far_third = add(far[3], far_second)
    near_second = to_place(after(near[2], far_second), 1)
    third = add(near[3], near_second, to_chip(far_third))
    third_here = to_place(third, 3)
    own = add(near[0], to_chip(after(far[0], third)))
    return add(own, to_place(after(first, third), 1), third_here)


def by_permutes(tokens, expert_ids, route_weights, expert_slot, w_gate, w_up, w_down):
    rows = tokens.shape[0]
    own = pack(tokens, expert_ids, route_weights, expert_slot, w_gate, w_up, w_down)
    hidden = hidden_units(gather_blocks(own), w_gate, w_up, expert_slot.shape[0])
    outs = []
    for chunk in range(OUT_CHUNKS):
        outs.append(reduce_blocks(*down(hidden, w_down, chunk, OUT_CHUNKS), rows))
    return jnp.concatenate(outs, axis=1)


def by_collectives(tokens, expert_ids, route_weights, expert_slot, w_gate, w_up, w_down):
    members, width, _ = w_gate.shape
    experts = expert_slot.shape[0]
    packed = pack(tokens, expert_ids, route_weights, expert_slot)
    gathered = lax.all_gather(packed, ("node", "local"), axis=0, tiled=True)
    rows = gathered[:, :width]
    tail = gathered[:, width : width + 3 * experts].astype(jnp.float32)
    weights = tail.reshape(-1, 3, experts).sum(axis=1)
    mine = lax.dynamic_slice_in_dim(weights, lax.axis_index("node") * members, members, axis=1)
    gate = jnp.einsum("td,edh->eth", rows, w_gate, preferred_element_type=jnp.float32)
    up = jnp.einsum("td,edh->eth", rows, w_up, preferred_element_type=jnp.float32)
    hidden = (jax.nn.silu(gate) * up * mine.T[..., None]).astype(jnp.bfloat16)
    result = jnp.einsum("eth,ehd->td", hidden, w_down, preferred_element_type=jnp.float32)
    return lax.psum_scatter(
        result.astype(jnp.bfloat16), ("node", "local"), scatter_dimension=0, tiled=True
    )


def per_device(*args):
    small = (lax.axis_size("node"), lax.axis_size("local")) == (2 * CHIPS, PLACES)
    return (by_permutes if small else by_collectives)(*args)


def solution(mesh):
    rows = P(("parts", "node", "local"), None)
    in_specs = (
        rows,
        rows,
        rows,
        P(),
        P("node", None, "local"),
        P("node", None, "local"),
        P("node", "local", None),
    )
    return jax.shard_map(
        per_device, mesh=mesh, in_specs=in_specs, out_specs=rows, check_vma=False
    )
```

```python
import functools

import jax
import jax.numpy as jnp
from jax import lax
from jax.experimental import pallas as pl
from jax.experimental.pallas import tpu as pltpu
from jax.sharding import PartitionSpec as P

LANES = 128
N_TILE = 256
DOWN_TILE = 1792
OUT_CHUNKS = 1
VMEM_LIMIT = 4 * 2**20


def pack_kernel(*refs):
    inputs, out_ref, local, sems = refs[:4], refs[-6], refs[-5:-1], refs[-1]
    copies = [
        pltpu.make_async_copy(here, there, sems.at[i])
        for i, (here, there) in enumerate(zip(inputs, local))
    ]
    for copy in copies:
        copy.start()
    for copy in copies:
        copy.wait()
    tokens_ref, ids_ref, route_ref, slot_ref = local
    rows, width = tokens_ref.shape
    experts = slot_ref.shape[0]
    row = lax.broadcasted_iota(jnp.int32, (rows, LANES), 0)
    column = lax.broadcasted_iota(jnp.int32, (rows, LANES), 1)
    slot = lax.rem(column, experts)
    weights = jnp.zeros((rows, LANES), jnp.float32)
    for k in range(ids_ref.shape[0]):
        for token in range(rows):
            named = (row == token) & (slot == slot_ref[ids_ref[k, token]])
            weights = jnp.where(named, route_ref[k, token], weights)
    first = weights.astype(jnp.bfloat16).astype(jnp.float32)
    second = (weights - first).astype(jnp.bfloat16).astype(jnp.float32)
    third = weights - first - second
    tail = jnp.where(column < experts, first, jnp.where(column < 2 * experts, second, third))
    out_ref[:, :width] = tokens_ref[...]
    out_ref[:, width:] = jnp.where(column < 3 * experts, tail, 0.0).astype(jnp.bfloat16)


def pack(tokens, expert_ids, route_weights, expert_slot, *weights):
    rows, width = tokens.shape
    inputs = (tokens, expert_ids.T, route_weights.T, expert_slot)
    held = [pltpu.with_memory_space_constraint(each, pltpu.HBM) for each in inputs + weights]
    return pl.pallas_call(
        pack_kernel,
        out_shape=jax.ShapeDtypeStruct((rows, width + LANES), jnp.bfloat16),
        in_specs=[pl.BlockSpec(memory_space=pl.ANY)] * len(held),
        out_specs=pl.BlockSpec(memory_space=pltpu.VMEM),
        scratch_shapes=[
            pltpu.VMEM(tokens.shape, tokens.dtype),
            *[pltpu.SMEM(each.shape, each.dtype) for each in inputs[1:]],
            pltpu.SemaphoreType.DMA((len(inputs),)),
        ],
        compiler_params=pltpu.CompilerParams(vmem_limit_bytes=VMEM_LIMIT),
        name="pack",
    )(*held)


def hidden_kernel(experts, *refs):
    *pieces, gate_ref, up_ref, out_ref, x_ref, weight_ref = refs
    members, width, hid = gate_ref.shape
    x_ref[...] = jnp.concatenate([piece[:, :width] for piece in pieces], axis=0)
    tail = jnp.concatenate([piece[:, width:] for piece in pieces], axis=0)
    tail = tail.astype(jnp.float32)
    column = lax.broadcasted_iota(jnp.int32, tail.shape, 1)
    for member in range(members):
        slot = lax.axis_index("node") * members + member
        mine = (lax.rem(column, experts) == slot) & (column < 3 * experts)
        weight_ref[member] = jnp.sum(jnp.where(mine, tail, 0.0), axis=1, keepdims=True)
    tiles = hid // N_TILE

    @pl.loop(0, members * tiles)
    def _(step):
        member = step // tiles
        at = pl.ds(pl.multiple_of(lax.rem(step, tiles) * N_TILE, N_TILE), N_TILE)
        gate, up = [
            jnp.dot(x_ref[...], ref[member, :, at], preferred_element_type=jnp.float32)
            for ref in (gate_ref, up_ref)
        ]
        hidden = gate / (1.0 + jnp.exp(-gate)) * up * weight_ref[member]
        to = pl.ds(pl.multiple_of(step * N_TILE, N_TILE), N_TILE)
        out_ref[:, to] = hidden.astype(jnp.bfloat16)


def hidden_units(pieces, w_gate, w_up, experts):
    members, width, hid = w_gate.shape
    rows = sum(piece.shape[0] for piece in pieces)
    vmem = pl.BlockSpec(memory_space=pltpu.VMEM)
    return pl.pallas_call(
        functools.partial(hidden_kernel, experts),
        out_shape=jax.ShapeDtypeStruct((rows, members * hid), jnp.bfloat16),
        in_specs=[vmem] * (len(pieces) + 2),
        out_specs=vmem,
        scratch_shapes=[
            pltpu.VMEM((rows, width), jnp.bfloat16),
            pltpu.VMEM((members, rows, 1), jnp.float32),
        ],
        compiler_params=pltpu.CompilerParams(vmem_limit_bytes=VMEM_LIMIT),
        cost_estimate=pl.CostEstimate(
            flops=4 * rows * members * width * hid,
            bytes_accessed=4 * members * width * hid,
            transcendentals=rows * members * hid,
        ),
        name="hidden",
    )(*pieces, w_gate, w_up)


def down_kernel(chunk, hidden_ref, down_ref, far_ref, near_ref, *keep_refs):
    part, width = far_ref.shape
    outs = (*keep_refs, near_ref, far_ref)

    @pl.loop(0, width // DOWN_TILE)
    def _(step):
        here = pl.ds(pl.multiple_of(step * DOWN_TILE, DOWN_TILE), DOWN_TILE)
        there = pl.ds(pl.multiple_of(chunk * width + step * DOWN_TILE, DOWN_TILE), DOWN_TILE)
        total = jnp.dot(
            hidden_ref[...], down_ref[:, there], preferred_element_type=jnp.float32
        ).astype(jnp.bfloat16)
        for i, ref in enumerate(outs):
            ref[:, here] = total[i * part : (i + 1) * part]


def down(hidden, w_down, chunk, chunks):
    units, width = w_down.shape
    rows = hidden.shape[0]
    vmem = pl.BlockSpec(memory_space=pltpu.VMEM)
    return pl.pallas_call(
        functools.partial(down_kernel, chunk),
        out_shape=[jax.ShapeDtypeStruct((rows // 4, width // chunks), jnp.bfloat16)] * 4,
        in_specs=[vmem, vmem],
        out_specs=[vmem] * 4,
        compiler_params=pltpu.CompilerParams(vmem_limit_bytes=VMEM_LIMIT),
        cost_estimate=pl.CostEstimate(
            flops=2 * rows * units * width // chunks,
            bytes_accessed=2 * units * width // chunks,
            transcendentals=0,
        ),
        name="down",
    )(hidden, w_down)


CHIPS, PLACES = 2, 4


def to_core(value):
    return lax.ppermute(value, "node", [(i, i ^ 1) for i in range(2 * CHIPS)])


def to_chip(value):
    return lax.ppermute(value, "node", [(i, i ^ 2) for i in range(2 * CHIPS)])


def to_place(value, bits):
    return lax.ppermute(value, "local", [(i, i ^ bits) for i in range(PLACES)])


def to_both(value, bits):
    count = 2 * CHIPS * PLACES
    perm = [(i, i ^ (2 * PLACES + bits)) for i in range(count)]
    return lax.ppermute(value, ("node", "local"), perm)


def add(*terms):
    return sum(term.astype(jnp.float32) for term in terms).astype(jnp.bfloat16)


def after(value, *others):
    return lax.optimization_barrier((value, *others))[0]


def gather_blocks(own):
    second = to_place(own, 2)
    first = to_place(own, 1)
    far_own = to_chip(own)
    far_second, far_third, third = to_chip(second), to_both(second, 1), to_place(second, 1)
    far_first = to_chip(after(first, second))
    chip = [own, first, second, third, far_own, far_first, far_second, far_third]
    ready = [own, first, after(second, third), third, *chip[PLACES:]]
    return chip + [to_core(piece) for piece in ready]


def reduce_blocks(other_far, other_near, near, far, rows):
    far = add(far, to_core(other_far)).reshape(PLACES, rows, -1)
    near = add(near, to_core(other_near)).reshape(PLACES, rows, -1)
    second = add(near[2], to_both(far[3], 1), to_chip(far[2]), to_place(near[3], 1))
    second_here = to_place(second, 2)
    first = add(near[1], to_chip(after(far[1], second)))
    own = add(near[0], to_chip(after(far[0], second)))
    return add(own, to_place(first, 1), second_here)


def by_permutes(tokens, expert_ids, route_weights, expert_slot, w_gate, w_up, w_down):
    rows = tokens.shape[0]
    own = pack(tokens, expert_ids, route_weights, expert_slot, w_gate, w_up, w_down)
    hidden = hidden_units(gather_blocks(own), w_gate, w_up, expert_slot.shape[0])
    matrix = w_down.reshape(-1, w_down.shape[-1])
    outs = []
    for chunk in range(OUT_CHUNKS):
        outs.append(reduce_blocks(*down(hidden, matrix, chunk, OUT_CHUNKS), rows))
    return jnp.concatenate(outs, axis=1)


def by_collectives(tokens, expert_ids, route_weights, expert_slot, w_gate, w_up, w_down):
    members, width, _ = w_gate.shape
    experts = expert_slot.shape[0]
    packed = pack(tokens, expert_ids, route_weights, expert_slot)
    gathered = lax.all_gather(packed, ("node", "local"), axis=0, tiled=True)
    rows = gathered[:, :width]
    tail = gathered[:, width : width + 3 * experts].astype(jnp.float32)
    weights = tail.reshape(-1, 3, experts).sum(axis=1)
    mine = lax.dynamic_slice_in_dim(weights, lax.axis_index("node") * members, members, axis=1)
    gate = jnp.einsum("td,edh->eth", rows, w_gate, preferred_element_type=jnp.float32)
    up = jnp.einsum("td,edh->eth", rows, w_up, preferred_element_type=jnp.float32)
    hidden = (jax.nn.silu(gate) * up * mine.T[..., None]).astype(jnp.bfloat16)
    result = jnp.einsum("eth,ehd->td", hidden, w_down, preferred_element_type=jnp.float32)
    return lax.psum_scatter(
        result.astype(jnp.bfloat16), ("node", "local"), scatter_dimension=0, tiled=True
    )


def per_device(*args):
    small = (lax.axis_size("node"), lax.axis_size("local")) == (2 * CHIPS, PLACES)
    return (by_permutes if small else by_collectives)(*args)


def solution(mesh):
    rows = P(("parts", "node", "local"), None)
    in_specs = (
        rows,
        rows,
        rows,
        P(),
        P("node", None, "local"),
        P("node", None, "local"),
        P("node", "local", None),
    )
    return jax.shard_map(
        per_device, mesh=mesh, in_specs=in_specs, out_specs=rows, check_vma=False
    )
```

```python
import functools

import jax
import jax.numpy as jnp
from jax import lax
from jax.experimental import pallas as pl
from jax.experimental.pallas import tpu as pltpu
from jax.sharding import PartitionSpec as P

LANES = 128
N_TILE = 256
DOWN_TILE = 1792
OUT_CHUNKS = 1
VMEM_LIMIT = 4 * 2**20


def pack_kernel(*refs):
    inputs, out_ref, local, sems = refs[:4], refs[-6], refs[-5:-1], refs[-1]
    copies = [
        pltpu.make_async_copy(here, there, sems.at[i])
        for i, (here, there) in enumerate(zip(inputs, local))
    ]
    for copy in copies:
        copy.start()
    for copy in copies:
        copy.wait()
    tokens_ref, ids_ref, route_ref, slot_ref = local
    rows, width = tokens_ref.shape
    experts = slot_ref.shape[0]
    row = lax.broadcasted_iota(jnp.int32, (rows, LANES), 0)
    column = lax.broadcasted_iota(jnp.int32, (rows, LANES), 1)
    slot = lax.rem(column, experts)
    weights = jnp.zeros((rows, LANES), jnp.float32)
    for k in range(ids_ref.shape[0]):
        for token in range(rows):
            named = (row == token) & (slot == slot_ref[ids_ref[k, token]])
            weights = jnp.where(named, route_ref[k, token], weights)
    first = weights.astype(jnp.bfloat16).astype(jnp.float32)
    second = (weights - first).astype(jnp.bfloat16).astype(jnp.float32)
    third = weights - first - second
    tail = jnp.where(column < experts, first, jnp.where(column < 2 * experts, second, third))
    out_ref[:, :width] = tokens_ref[...]
    out_ref[:, width:] = jnp.where(column < 3 * experts, tail, 0.0).astype(jnp.bfloat16)


def pack(tokens, expert_ids, route_weights, expert_slot, *weights):
    rows, width = tokens.shape
    inputs = (tokens, expert_ids.T, route_weights.T, expert_slot)
    held = [pltpu.with_memory_space_constraint(each, pltpu.HBM) for each in inputs + weights]
    return pl.pallas_call(
        pack_kernel,
        out_shape=jax.ShapeDtypeStruct((rows, width + LANES), jnp.bfloat16),
        in_specs=[pl.BlockSpec(memory_space=pl.ANY)] * len(held),
        out_specs=pl.BlockSpec(memory_space=pltpu.VMEM),
        scratch_shapes=[
            pltpu.VMEM(tokens.shape, tokens.dtype),
            *[pltpu.SMEM(each.shape, each.dtype) for each in inputs[1:]],
            pltpu.SemaphoreType.DMA((len(inputs),)),
        ],
        compiler_params=pltpu.CompilerParams(vmem_limit_bytes=VMEM_LIMIT),
        name="pack",
    )(*held)


def hidden_kernel(experts, *refs):
    *pieces, gate_ref, up_ref, out_ref, x_ref, weight_ref = refs
    members, width, hid = gate_ref.shape
    x_ref[...] = jnp.concatenate([piece[:, :width] for piece in pieces], axis=0)
    tail = jnp.concatenate([piece[:, width:] for piece in pieces], axis=0)
    tail = tail.astype(jnp.float32)
    column = lax.broadcasted_iota(jnp.int32, tail.shape, 1)
    for member in range(members):
        slot = lax.axis_index("node") * members + member
        mine = (lax.rem(column, experts) == slot) & (column < 3 * experts)
        weight_ref[member] = jnp.sum(jnp.where(mine, tail, 0.0), axis=1, keepdims=True)
    tiles = hid // N_TILE

    @pl.loop(0, members * tiles)
    def _(step):
        member = step // tiles
        at = pl.ds(pl.multiple_of(lax.rem(step, tiles) * N_TILE, N_TILE), N_TILE)
        gate, up = [
            jnp.dot(x_ref[...], ref[member, :, at], preferred_element_type=jnp.float32)
            for ref in (gate_ref, up_ref)
        ]
        hidden = gate / (1.0 + jnp.exp(-gate)) * up * weight_ref[member]
        to = pl.ds(pl.multiple_of(step * N_TILE, N_TILE), N_TILE)
        out_ref[:, to] = hidden.astype(jnp.bfloat16)


def hidden_units(pieces, w_gate, w_up, experts):
    members, width, hid = w_gate.shape
    rows = sum(piece.shape[0] for piece in pieces)
    vmem = pl.BlockSpec(memory_space=pltpu.VMEM)
    return pl.pallas_call(
        functools.partial(hidden_kernel, experts),
        out_shape=jax.ShapeDtypeStruct((rows, members * hid), jnp.bfloat16),
        in_specs=[vmem] * (len(pieces) + 2),
        out_specs=vmem,
        scratch_shapes=[
            pltpu.VMEM((rows, width), jnp.bfloat16),
            pltpu.VMEM((members, rows, 1), jnp.float32),
        ],
        compiler_params=pltpu.CompilerParams(vmem_limit_bytes=VMEM_LIMIT),
        cost_estimate=pl.CostEstimate(
            flops=4 * rows * members * width * hid,
            bytes_accessed=4 * members * width * hid,
            transcendentals=rows * members * hid,
        ),
        name="hidden",
    )(*pieces, w_gate, w_up)


def down_kernel(chunk, hidden_ref, down_ref, other_ref, here_ref):
    half, width = here_ref.shape

    @pl.loop(0, width // DOWN_TILE)
    def _(step):
        at = pl.ds(pl.multiple_of(step * DOWN_TILE, DOWN_TILE), DOWN_TILE)
        there = pl.ds(pl.multiple_of(chunk * width + step * DOWN_TILE, DOWN_TILE), DOWN_TILE)
        total = jnp.dot(
            hidden_ref[...], down_ref[:, there], preferred_element_type=jnp.float32
        ).astype(jnp.bfloat16)
        here_ref[:, at] = total[:half]
        other_ref[:, at] = total[half:]


def down(hidden, w_down, chunk, chunks):
    units, width = w_down.shape
    rows = hidden.shape[0]
    vmem = pl.BlockSpec(memory_space=pltpu.VMEM)
    return pl.pallas_call(
        functools.partial(down_kernel, chunk),
        out_shape=[jax.ShapeDtypeStruct((rows // 2, width // chunks), jnp.bfloat16)] * 2,
        in_specs=[vmem, vmem],
        out_specs=[vmem, vmem],
        compiler_params=pltpu.CompilerParams(vmem_limit_bytes=VMEM_LIMIT),
        cost_estimate=pl.CostEstimate(
            flops=2 * rows * units * width // chunks,
            bytes_accessed=2 * units * width // chunks,
            transcendentals=0,
        ),
        name="down",
    )(hidden, w_down)


CHIPS, PLACES = 2, 4
GATHER_ORDER = (0, 2, 4, 5, 1, 3, 6, 7)


def to_core(value):
    return lax.ppermute(value, "node", [(i, i ^ 1) for i in range(2 * CHIPS)])


def to_chip(value):
    return lax.ppermute(value, "node", [(i, i ^ 2) for i in range(2 * CHIPS)])


def to_place(value, bits):
    return lax.ppermute(value, "local", [(i, i ^ bits) for i in range(PLACES)])


def to_both(value, bits):
    count = 2 * CHIPS * PLACES
    perm = [(i, i ^ (2 * PLACES + bits)) for i in range(count)]
    return lax.ppermute(value, ("node", "local"), perm)


def after(value, *others):
    return lax.optimization_barrier((value, *others))[0]


def gather_blocks(own):
    second, far_own = to_place(own, 2), to_chip(own)
    far_first, first = to_both(own, 1), to_place(own, 1)
    other = [to_core(own), to_core(far_own), to_core(first)]
    far_second, far_third, third = to_chip(second), to_both(second, 1), to_place(second, 1)
    other += [to_core(after(piece, third)) for piece in (far_first, second)]
    other += [to_core(piece) for piece in (third, far_second, far_third)]
    chip = [own, far_own, first, far_first, second, third, far_second, far_third]
    return [chip[i] for i in GATHER_ORDER] + [other[i] for i in GATHER_ORDER]


def total(*terms):
    return sum(term.astype(jnp.float32) for term in terms)


def reduce_blocks(other, here, rows):
    sums = total(here, to_core(other)).astype(jnp.bfloat16).reshape(2 * PLACES, rows, -1)
    near, far = sums[:PLACES], sums[PLACES:]
    second = total(near[2], to_chip(far[2]), to_both(far[3], 1), to_place(near[3], 1))
    second = second.astype(jnp.bfloat16)
    own = total(near[0], after(to_place(near[1], 1), second))
    far_own, far_first = to_chip(after(far[0], own)), to_both(after(far[1], own), 1)
    return total(own, to_place(second, 2), far_own, far_first).astype(jnp.bfloat16)


def by_permutes(tokens, expert_ids, route_weights, expert_slot, w_gate, w_up, w_down):
    rows = tokens.shape[0]
    own = pack(tokens, expert_ids, route_weights, expert_slot, w_gate, w_up, w_down)
    hidden = hidden_units(gather_blocks(own), w_gate, w_up, expert_slot.shape[0])
    matrix = w_down.reshape(-1, w_down.shape[-1])
    outs = []
    for chunk in range(OUT_CHUNKS):
        outs.append(reduce_blocks(*down(hidden, matrix, chunk, OUT_CHUNKS), rows))
    return jnp.concatenate(outs, axis=1)


def by_collectives(tokens, expert_ids, route_weights, expert_slot, w_gate, w_up, w_down):
    members, width, _ = w_gate.shape
    experts = expert_slot.shape[0]
    packed = pack(tokens, expert_ids, route_weights, expert_slot)
    gathered = lax.all_gather(packed, ("node", "local"), axis=0, tiled=True)
    rows = gathered[:, :width]
    tail = gathered[:, width : width + 3 * experts].astype(jnp.float32)
    weights = tail.reshape(-1, 3, experts).sum(axis=1)
    mine = lax.dynamic_slice_in_dim(weights, lax.axis_index("node") * members, members, axis=1)
    gate = jnp.einsum("td,edh->eth", rows, w_gate, preferred_element_type=jnp.float32)
    up = jnp.einsum("td,edh->eth", rows, w_up, preferred_element_type=jnp.float32)
    hidden = (jax.nn.silu(gate) * up * mine.T[..., None]).astype(jnp.bfloat16)
    result = jnp.einsum("eth,ehd->td", hidden, w_down, preferred_element_type=jnp.float32)
    return lax.psum_scatter(
        result.astype(jnp.bfloat16), ("node", "local"), scatter_dimension=0, tiled=True
    )


def per_device(*args):
    small = (lax.axis_size("node"), lax.axis_size("local")) == (2 * CHIPS, PLACES)
    return (by_permutes if small else by_collectives)(*args)


def solution(mesh):
    rows = P(("parts", "node", "local"), None)
    in_specs = (
        rows,
        rows,
        rows,
        P(),
        P("node", None, "local"),
        P("node", None, "local"),
        P("node", "local", None),
    )
    return jax.shard_map(
        per_device, mesh=mesh, in_specs=in_specs, out_specs=rows, check_vma=False
    )
```

```python
import functools

import jax
import jax.numpy as jnp
from jax import lax
from jax.experimental import pallas as pl
from jax.experimental.pallas import tpu as pltpu
from jax.sharding import PartitionSpec as P

LANES = 128
N_TILE = 256
DOWN_TILE = 1792
OUT_CHUNKS = 1
VMEM_LIMIT = 4 * 2**20


def pack_kernel(*refs):
    inputs, out_ref, local, sems = refs[:4], refs[-6], refs[-5:-1], refs[-1]
    copies = [
        pltpu.make_async_copy(here, there, sems.at[i])
        for i, (here, there) in enumerate(zip(inputs, local))
    ]
    for copy in copies:
        copy.start()
    for copy in copies:
        copy.wait()
    tokens_ref, ids_ref, route_ref, slot_ref = local
    rows, width = tokens_ref.shape
    experts = slot_ref.shape[0]
    row = lax.broadcasted_iota(jnp.int32, (rows, LANES), 0)
    column = lax.broadcasted_iota(jnp.int32, (rows, LANES), 1)
    slot = lax.rem(column, experts)
    weights = jnp.zeros((rows, LANES), jnp.float32)
    for k in range(ids_ref.shape[0]):
        for token in range(rows):
            named = (row == token) & (slot == slot_ref[ids_ref[k, token]])
            weights = jnp.where(named, route_ref[k, token], weights)
    first = weights.astype(jnp.bfloat16).astype(jnp.float32)
    second = (weights - first).astype(jnp.bfloat16).astype(jnp.float32)
    third = weights - first - second
    tail = jnp.where(column < experts, first, jnp.where(column < 2 * experts, second, third))
    out_ref[:, :width] = tokens_ref[...]
    out_ref[:, width:] = jnp.where(column < 3 * experts, tail, 0.0).astype(jnp.bfloat16)


def pack(tokens, expert_ids, route_weights, expert_slot, *weights):
    rows, width = tokens.shape
    inputs = (tokens, expert_ids.T, route_weights.T, expert_slot)
    held = [pltpu.with_memory_space_constraint(each, pltpu.HBM) for each in inputs + weights]
    return pl.pallas_call(
        pack_kernel,
        out_shape=jax.ShapeDtypeStruct((rows, width + LANES), jnp.bfloat16),
        in_specs=[pl.BlockSpec(memory_space=pl.ANY)] * len(held),
        out_specs=pl.BlockSpec(memory_space=pltpu.VMEM),
        scratch_shapes=[
            pltpu.VMEM(tokens.shape, tokens.dtype),
            *[pltpu.SMEM(each.shape, each.dtype) for each in inputs[1:]],
            pltpu.SemaphoreType.DMA((len(inputs),)),
        ],
        compiler_params=pltpu.CompilerParams(vmem_limit_bytes=VMEM_LIMIT),
        name="pack",
    )(*held)


def hidden_kernel(experts, *refs):
    *pieces, gate_ref, up_ref, out_ref, x_ref, weight_ref = refs
    members, width, hid = gate_ref.shape
    x_ref[...] = jnp.concatenate([piece[:, :width] for piece in pieces], axis=0)
    tail = jnp.concatenate([piece[:, width:] for piece in pieces], axis=0)
    tail = tail.astype(jnp.float32)
    column = lax.broadcasted_iota(jnp.int32, tail.shape, 1)
    for member in range(members):
        slot = lax.axis_index("node") * members + member
        mine = (lax.rem(column, experts) == slot) & (column < 3 * experts)
        weight_ref[member] = jnp.sum(jnp.where(mine, tail, 0.0), axis=1, keepdims=True)
    tiles = hid // N_TILE

    @pl.loop(0, members * tiles)
    def _(step):
        member = step // tiles
        at = pl.ds(pl.multiple_of(lax.rem(step, tiles) * N_TILE, N_TILE), N_TILE)
        gate, up = [
            jnp.dot(x_ref[...], ref[member, :, at], preferred_element_type=jnp.float32)
            for ref in (gate_ref, up_ref)
        ]
        hidden = gate / (1.0 + jnp.exp(-gate)) * up * weight_ref[member]
        to = pl.ds(pl.multiple_of(step * N_TILE, N_TILE), N_TILE)
        out_ref[:, to] = hidden.astype(jnp.bfloat16)


def hidden_units(pieces, w_gate, w_up, experts):
    members, width, hid = w_gate.shape
    rows = sum(piece.shape[0] for piece in pieces)
    vmem = pl.BlockSpec(memory_space=pltpu.VMEM)
    return pl.pallas_call(
        functools.partial(hidden_kernel, experts),
        out_shape=jax.ShapeDtypeStruct((rows, members * hid), jnp.bfloat16),
        in_specs=[vmem] * (len(pieces) + 2),
        out_specs=vmem,
        scratch_shapes=[
            pltpu.VMEM((rows, width), jnp.bfloat16),
            pltpu.VMEM((members, rows, 1), jnp.float32),
        ],
        compiler_params=pltpu.CompilerParams(vmem_limit_bytes=VMEM_LIMIT),
        cost_estimate=pl.CostEstimate(
            flops=4 * rows * members * width * hid,
            bytes_accessed=4 * members * width * hid,
            transcendentals=rows * members * hid,
        ),
        name="hidden",
    )(*pieces, w_gate, w_up)


def down_kernel(chunk, hidden_ref, down_ref, *outs):
    part, width = outs[0].shape

    @pl.loop(0, width // DOWN_TILE)
    def _(step):
        at = pl.ds(pl.multiple_of(step * DOWN_TILE, DOWN_TILE), DOWN_TILE)
        there = pl.ds(pl.multiple_of(chunk * width + step * DOWN_TILE, DOWN_TILE), DOWN_TILE)
        total = jnp.dot(
            hidden_ref[...], down_ref[:, there], preferred_element_type=jnp.float32
        ).astype(jnp.bfloat16)
        for i, ref in enumerate(outs):
            ref[:, at] = total[i * part : (i + 1) * part]


def down(hidden, w_down, chunk, chunks):
    units, width = w_down.shape
    rows = hidden.shape[0]
    vmem = pl.BlockSpec(memory_space=pltpu.VMEM)
    return pl.pallas_call(
        functools.partial(down_kernel, chunk),
        out_shape=[jax.ShapeDtypeStruct((rows // 4, width // chunks), jnp.bfloat16)] * 4,
        in_specs=[vmem, vmem],
        out_specs=[vmem] * 4,
        compiler_params=pltpu.CompilerParams(vmem_limit_bytes=VMEM_LIMIT),
        cost_estimate=pl.CostEstimate(
            flops=2 * rows * units * width // chunks,
            bytes_accessed=2 * units * width // chunks,
            transcendentals=0,
        ),
        name="down",
    )(hidden, w_down)


CHIPS, PLACES = 2, 4
GATHER_ORDER = (0, 2, 4, 5, 1, 3, 6, 7)


def to_core(value):
    return lax.ppermute(value, "node", [(i, i ^ 1) for i in range(2 * CHIPS)])


def to_chip(value):
    return lax.ppermute(value, "node", [(i, i ^ 2) for i in range(2 * CHIPS)])


def to_place(value, bits):
    return lax.ppermute(value, "local", [(i, i ^ bits) for i in range(PLACES)])


def to_both(value, bits):
    count = 2 * CHIPS * PLACES
    perm = [(i, i ^ (2 * PLACES + bits)) for i in range(count)]
    return lax.ppermute(value, ("node", "local"), perm)


def after(value, *others):
    return lax.optimization_barrier((value, *others))[0]


def gather_blocks(own):
    second, first, far_own = to_place(own, 2), to_place(own, 1), to_chip(own)
    far_first = to_chip(first)
    other = [to_core(after(own, first)), to_core(after(far_own, first)), to_core(first)]
    ready = after(second, far_first, far_own, other[0])
    far_second, far_third, third = to_chip(ready), to_both(ready, 1), to_place(ready, 1)
    other += [to_core(after(piece, third)) for piece in (far_first, second)]
    other += [to_core(piece) for piece in (third, far_second, far_third)]
    chip = [own, far_own, first, far_first, second, third, far_second, far_third]
    return [chip[i] for i in GATHER_ORDER] + [other[i] for i in GATHER_ORDER]


def total(*terms):
    return sum(term.astype(jnp.float32) for term in terms)


def reduce_blocks(near, far, other_near, other_far, rows):
    other_far = to_core(other_far)
    other_near = to_core(after(other_near, other_far))
    far = total(far, other_far).astype(jnp.bfloat16).reshape(PLACES, rows, -1)
    second, third = to_chip(far[2]), to_both(far[3], 1)
    near = total(near, other_near).astype(jnp.bfloat16).reshape(PLACES, rows, -1)
    second = total(near[2], second, third, to_place(near[3], 1)).astype(jnp.bfloat16)
    own = total(near[0], after(to_place(near[1], 1), second))
    far_own, far_first = to_chip(after(far[0], own)), to_both(after(far[1], own), 1)
    return total(own, to_place(second, 2), far_own, far_first).astype(jnp.bfloat16)


def by_permutes(tokens, expert_ids, route_weights, expert_slot, w_gate, w_up, w_down):
    rows = tokens.shape[0]
    own = pack(tokens, expert_ids, route_weights, expert_slot, w_gate, w_up, w_down)
    hidden = hidden_units(gather_blocks(own), w_gate, w_up, expert_slot.shape[0])
    matrix = w_down.reshape(-1, w_down.shape[-1])
    outs = []
    for chunk in range(OUT_CHUNKS):
        outs.append(reduce_blocks(*down(hidden, matrix, chunk, OUT_CHUNKS), rows))
    return jnp.concatenate(outs, axis=1)


def by_collectives(tokens, expert_ids, route_weights, expert_slot, w_gate, w_up, w_down):
    members, width, _ = w_gate.shape
    experts = expert_slot.shape[0]
    packed = pack(tokens, expert_ids, route_weights, expert_slot)
    gathered = lax.all_gather(packed, ("node", "local"), axis=0, tiled=True)
    rows = gathered[:, :width]
    tail = gathered[:, width : width + 3 * experts].astype(jnp.float32)
    weights = tail.reshape(-1, 3, experts).sum(axis=1)
    mine = lax.dynamic_slice_in_dim(weights, lax.axis_index("node") * members, members, axis=1)
    gate = jnp.einsum("td,edh->eth", rows, w_gate, preferred_element_type=jnp.float32)
    up = jnp.einsum("td,edh->eth", rows, w_up, preferred_element_type=jnp.float32)
    hidden = (jax.nn.silu(gate) * up * mine.T[..., None]).astype(jnp.bfloat16)
    result = jnp.einsum("eth,ehd->td", hidden, w_down, preferred_element_type=jnp.float32)
    return lax.psum_scatter(
        result.astype(jnp.bfloat16), ("node", "local"), scatter_dimension=0, tiled=True
    )


def per_device(*args):
    small = (lax.axis_size("node"), lax.axis_size("local")) == (2 * CHIPS, PLACES)
    return (by_permutes if small else by_collectives)(*args)


def solution(mesh):
    rows = P(("parts", "node", "local"), None)
    in_specs = (
        rows,
        rows,
        rows,
        P(),
        P("node", None, "local"),
        P("node", None, "local"),
        P("node", "local", None),
    )
    return jax.shard_map(
        per_device, mesh=mesh, in_specs=in_specs, out_specs=rows, check_vma=False
    )
```

```python
import functools

import jax
import jax.numpy as jnp
from jax import lax
from jax.experimental import pallas as pl
from jax.experimental.pallas import tpu as pltpu
from jax.sharding import PartitionSpec as P

LANES = 128
N_TILE = 256
DOWN_TILE = 1792
VMEM_LIMIT = 4 * 2**20


def pack_kernel(*refs):
    inputs, out_ref, local, sems = refs[:4], refs[-6], refs[-5:-1], refs[-1]
    copies = [
        pltpu.make_async_copy(here, there, sems.at[i])
        for i, (here, there) in enumerate(zip(inputs, local))
    ]
    for copy in copies:
        copy.start()
    for copy in copies:
        copy.wait()
    tokens_ref, ids_ref, route_ref, slot_ref = local
    rows, width = tokens_ref.shape
    experts = slot_ref.shape[0]
    row = lax.broadcasted_iota(jnp.int32, (rows, LANES), 0)
    column = lax.broadcasted_iota(jnp.int32, (rows, LANES), 1)
    slot = lax.rem(column, experts)
    weights = jnp.zeros((rows, LANES), jnp.float32)
    for k in range(ids_ref.shape[0]):
        for token in range(rows):
            named = (row == token) & (slot == slot_ref[ids_ref[k, token]])
            weights = jnp.where(named, route_ref[k, token], weights)
    first = weights.astype(jnp.bfloat16).astype(jnp.float32)
    second = (weights - first).astype(jnp.bfloat16).astype(jnp.float32)
    third = weights - first - second
    tail = jnp.where(column < experts, first, jnp.where(column < 2 * experts, second, third))
    out_ref[:, :width] = tokens_ref[...]
    out_ref[:, width:] = jnp.where(column < 3 * experts, tail, 0.0).astype(jnp.bfloat16)


def pack(tokens, expert_ids, route_weights, expert_slot, *weights):
    rows, width = tokens.shape
    inputs = (tokens, expert_ids.T, route_weights.T, expert_slot)
    held = [pltpu.with_memory_space_constraint(each, pltpu.HBM) for each in inputs + weights]
    return pl.pallas_call(
        pack_kernel,
        out_shape=jax.ShapeDtypeStruct((rows, width + LANES), jnp.bfloat16),
        in_specs=[pl.BlockSpec(memory_space=pl.ANY)] * len(held),
        out_specs=pl.BlockSpec(memory_space=pltpu.VMEM),
        scratch_shapes=[
            pltpu.VMEM(tokens.shape, tokens.dtype),
            *[pltpu.SMEM(each.shape, each.dtype) for each in inputs[1:]],
            pltpu.SemaphoreType.DMA((len(inputs),)),
        ],
        compiler_params=pltpu.CompilerParams(vmem_limit_bytes=VMEM_LIMIT),
        name="pack",
    )(*held)


def stack_kernel(*refs):
    *pieces, out_ref = refs
    out_ref[...] = jnp.concatenate([piece[...] for piece in pieces], axis=0)


def stack(*pieces):
    rows = sum(piece.shape[0] for piece in pieces)
    vmem = pl.BlockSpec(memory_space=pltpu.VMEM)
    return pl.pallas_call(
        stack_kernel,
        out_shape=jax.ShapeDtypeStruct((rows, pieces[0].shape[1]), pieces[0].dtype),
        in_specs=[vmem] * len(pieces),
        out_specs=vmem,
        compiler_params=pltpu.CompilerParams(vmem_limit_bytes=VMEM_LIMIT),
        name="stack",
    )(*pieces)


def hidden_kernel(experts, *refs):
    *pieces, gate_ref, up_ref, out_ref, x_ref, weight_ref = refs
    members, width, hid = gate_ref.shape
    x_ref[...] = jnp.concatenate([piece[:, :width] for piece in pieces], axis=0)
    tail = jnp.concatenate([piece[:, width:] for piece in pieces], axis=0)
    tail = tail.astype(jnp.float32)
    column = lax.broadcasted_iota(jnp.int32, tail.shape, 1)
    for member in range(members):
        slot = lax.axis_index("node") * members + member
        mine = (lax.rem(column, experts) == slot) & (column < 3 * experts)
        weight_ref[member] = jnp.sum(jnp.where(mine, tail, 0.0), axis=1, keepdims=True)
    tiles = hid // N_TILE

    @pl.loop(0, members * tiles)
    def _(step):
        member = step // tiles
        at = pl.ds(pl.multiple_of(lax.rem(step, tiles) * N_TILE, N_TILE), N_TILE)
        gate, up = [
            jnp.dot(x_ref[...], ref[member, :, at], preferred_element_type=jnp.float32)
            for ref in (gate_ref, up_ref)
        ]
        hidden = gate / (1.0 + jnp.exp(-gate)) * up * weight_ref[member]
        to = pl.ds(pl.multiple_of(step * N_TILE, N_TILE), N_TILE)
        out_ref[:, to] = hidden.astype(jnp.bfloat16)


def hidden_units(pieces, w_gate, w_up, experts):
    members, width, hid = w_gate.shape
    rows = sum(piece.shape[0] for piece in pieces)
    vmem = pl.BlockSpec(memory_space=pltpu.VMEM)
    return pl.pallas_call(
        functools.partial(hidden_kernel, experts),
        out_shape=jax.ShapeDtypeStruct((rows, members * hid), jnp.bfloat16),
        in_specs=[vmem] * (len(pieces) + 2),
        out_specs=vmem,
        scratch_shapes=[
            pltpu.VMEM((rows, width), jnp.bfloat16),
            pltpu.VMEM((members, rows, 1), jnp.float32),
        ],
        compiler_params=pltpu.CompilerParams(vmem_limit_bytes=VMEM_LIMIT),
        cost_estimate=pl.CostEstimate(
            flops=4 * rows * members * width * hid,
            bytes_accessed=0,
            transcendentals=rows * members * hid,
        ),
        name="hidden",
    )(*pieces, w_gate, w_up)


def down_kernel(hidden_ref, down_ref, here_ref, other_ref):
    half, width = here_ref.shape

    @pl.loop(0, width // DOWN_TILE)
    def _(step):
        at = pl.ds(pl.multiple_of(step * DOWN_TILE, DOWN_TILE), DOWN_TILE)
        total = jnp.dot(
            hidden_ref[...], down_ref[:, at], preferred_element_type=jnp.float32
        ).astype(jnp.bfloat16)
        here_ref[:, at] = total[:half]
        other_ref[:, at] = total[half:]


def down(hidden, w_down):
    units, width = w_down.shape
    rows = hidden.shape[0]
    vmem = pl.BlockSpec(memory_space=pltpu.VMEM)
    return pl.pallas_call(
        down_kernel,
        out_shape=[jax.ShapeDtypeStruct((rows // 2, width), jnp.bfloat16)] * 2,
        in_specs=[vmem, vmem],
        out_specs=[vmem, vmem],
        compiler_params=pltpu.CompilerParams(vmem_limit_bytes=VMEM_LIMIT),
        cost_estimate=pl.CostEstimate(
            flops=2 * rows * units * width, bytes_accessed=0, transcendentals=0
        ),
        name="down",
    )(hidden, w_down)


CHIPS, PLACES = 2, 4


def to_core(value):
    return lax.ppermute(value, "node", [(i, i ^ 1) for i in range(2 * CHIPS)])


def to_chip(value):
    return lax.ppermute(value, "node", [(i, i ^ 2) for i in range(2 * CHIPS)])


def to_place(value, bits):
    return lax.ppermute(value, "local", [(i, i ^ bits) for i in range(PLACES)])


def to_both(value, bits):
    count = 2 * CHIPS * PLACES
    perm = [(i, i ^ (2 * PLACES + bits)) for i in range(count)]
    return lax.ppermute(value, ("node", "local"), perm)


def after(value, *others):
    return lax.optimization_barrier((value, *others))[0]


def hidden_groups(own, hidden_of):
    second, first, far_own = to_place(own, 2), to_place(own, 1), to_chip(own)
    far_first = to_both(own, 1)
    group = [own, far_own, first, far_first]
    early = hidden_of(group + [to_core(stack(after(own, second), *group[1:]))])
    far_second, far_third, third = to_chip(second), to_both(second, 1), to_place(second, 1)
    group = [after(piece, early) for piece in (second, third, far_second, far_third)]
    return early, hidden_of(group + [to_core(piece) for piece in group])


def total(*terms):
    return sum(term.astype(jnp.float32) for term in terms)


def reduce_blocks(hidden_early, hidden_late, matrix, rows):
    def shares(hidden):
        here, other = down(hidden, matrix)
        return here, to_core(other), other

    def blocks(here, other):
        return total(here, other).astype(jnp.bfloat16).reshape(PLACES, rows, -1)

    here, other, leaving = shares(hidden_late)
    here_early, other_early, _ = shares(after(hidden_early, leaving))
    second, third, far_second, far_third = blocks(here, other)
    second = total(second, to_chip(far_second), to_both(far_third, 1), to_place(third, 1))
    second = second.astype(jnp.bfloat16)
    own, far_own, first, far_first = blocks(here_early, other_early)
    own = total(own, after(to_place(first, 1), second))
    far_own, far_first = to_chip(after(far_own, own)), to_both(after(far_first, own), 1)
    return total(own, to_place(second, 2), far_own, far_first).astype(jnp.bfloat16)


def by_permutes(tokens, expert_ids, route_weights, expert_slot, w_gate, w_up, w_down):
    own = pack(tokens, expert_ids, route_weights, expert_slot, w_gate, w_up, w_down)
    experts = expert_slot.shape[0]
    early, late = hidden_groups(own, lambda rows: hidden_units(rows, w_gate, w_up, experts))
    matrix = w_down.reshape(-1, w_down.shape[-1])
    return reduce_blocks(early, late, matrix, tokens.shape[0])


def by_collectives(tokens, expert_ids, route_weights, expert_slot, w_gate, w_up, w_down):
    members, width, _ = w_gate.shape
    experts = expert_slot.shape[0]
    packed = pack(tokens, expert_ids, route_weights, expert_slot)
    gathered = lax.all_gather(packed, ("node", "local"), axis=0, tiled=True)
    rows = gathered[:, :width]
    tail = gathered[:, width : width + 3 * experts].astype(jnp.float32)
    weights = tail.reshape(-1, 3, experts).sum(axis=1)
    mine = lax.dynamic_slice_in_dim(weights, lax.axis_index("node") * members, members, axis=1)
    gate = jnp.einsum("td,edh->eth", rows, w_gate, preferred_element_type=jnp.float32)
    up = jnp.einsum("td,edh->eth", rows, w_up, preferred_element_type=jnp.float32)
    hidden = (jax.nn.silu(gate) * up * mine.T[..., None]).astype(jnp.bfloat16)
    result = jnp.einsum("eth,ehd->td", hidden, w_down, preferred_element_type=jnp.float32)
    return lax.psum_scatter(
        result.astype(jnp.bfloat16), ("node", "local"), scatter_dimension=0, tiled=True
    )


def per_device(*args):
    small = (lax.axis_size("node"), lax.axis_size("local")) == (2 * CHIPS, PLACES)
    return (by_permutes if small else by_collectives)(*args)


def solution(mesh):
    rows = P(("parts", "node", "local"), None)
    in_specs = (
        rows,
        rows,
        rows,
        P(),
        P("node", None, "local"),
        P("node", None, "local"),
        P("node", "local", None),
    )
    return jax.shard_map(
        per_device, mesh=mesh, in_specs=in_specs, out_specs=rows, check_vma=False
    )
```

```python
import functools

import jax
import jax.numpy as jnp
from jax import lax
from jax.experimental import pallas as pl
from jax.experimental.pallas import tpu as pltpu
from jax.sharding import PartitionSpec as P

LANES = 128
N_TILE = 256
DOWN_TILE = 1792
OUT_CHUNKS = 1
VMEM_LIMIT = 4 * 2**20


def pack_kernel(*refs):
    inputs, out_ref, local, sems = refs[:4], refs[-6], refs[-5:-1], refs[-1]
    copies = [
        pltpu.make_async_copy(here, there, sems.at[i])
        for i, (here, there) in enumerate(zip(inputs, local))
    ]
    for copy in copies:
        copy.start()
    for copy in copies:
        copy.wait()
    tokens_ref, ids_ref, route_ref, slot_ref = local
    rows, width = tokens_ref.shape
    experts = slot_ref.shape[0]
    row = lax.broadcasted_iota(jnp.int32, (rows, LANES), 0)
    column = lax.broadcasted_iota(jnp.int32, (rows, LANES), 1)
    slot = lax.rem(column, experts)
    weights = jnp.zeros((rows, LANES), jnp.float32)
    for k in range(ids_ref.shape[0]):
        for token in range(rows):
            named = (row == token) & (slot == slot_ref[ids_ref[k, token]])
            weights = jnp.where(named, route_ref[k, token], weights)
    first = weights.astype(jnp.bfloat16).astype(jnp.float32)
    second = (weights - first).astype(jnp.bfloat16).astype(jnp.float32)
    third = weights - first - second
    tail = jnp.where(column < experts, first, jnp.where(column < 2 * experts, second, third))
    out_ref[:, :width] = tokens_ref[...]
    out_ref[:, width:] = jnp.where(column < 3 * experts, tail, 0.0).astype(jnp.bfloat16)


def pack(tokens, expert_ids, route_weights, expert_slot, *weights):
    rows, width = tokens.shape
    inputs = (tokens, expert_ids.T, route_weights.T, expert_slot)
    held = [pltpu.with_memory_space_constraint(each, pltpu.HBM) for each in inputs + weights]
    return pl.pallas_call(
        pack_kernel,
        out_shape=jax.ShapeDtypeStruct((rows, width + LANES), jnp.bfloat16),
        in_specs=[pl.BlockSpec(memory_space=pl.ANY)] * len(held),
        out_specs=pl.BlockSpec(memory_space=pltpu.VMEM),
        scratch_shapes=[
            pltpu.VMEM(tokens.shape, tokens.dtype),
            *[pltpu.SMEM(each.shape, each.dtype) for each in inputs[1:]],
            pltpu.SemaphoreType.DMA((len(inputs),)),
        ],
        compiler_params=pltpu.CompilerParams(vmem_limit_bytes=VMEM_LIMIT),
        name="pack",
    )(*held)


def hidden_kernel(experts, *refs):
    *pieces, gate_ref, up_ref, out_ref, x_ref, weight_ref = refs
    members, width, hid = gate_ref.shape
    x_ref[...] = jnp.concatenate([piece[:, :width] for piece in pieces], axis=0)
    tail = jnp.concatenate([piece[:, width:] for piece in pieces], axis=0)
    tail = tail.astype(jnp.float32)
    column = lax.broadcasted_iota(jnp.int32, tail.shape, 1)
    for member in range(members):
        slot = lax.axis_index("node") * members + member
        mine = (lax.rem(column, experts) == slot) & (column < 3 * experts)
        weight_ref[member] = jnp.sum(jnp.where(mine, tail, 0.0), axis=1, keepdims=True)
    tiles = hid // N_TILE

    @pl.loop(0, members * tiles)
    def _(step):
        member = step // tiles
        at = pl.ds(pl.multiple_of(lax.rem(step, tiles) * N_TILE, N_TILE), N_TILE)
        gate, up = [
            jnp.dot(x_ref[...], ref[member, :, at], preferred_element_type=jnp.float32)
            for ref in (gate_ref, up_ref)
        ]
        hidden = gate / (1.0 + jnp.exp(-gate)) * up * weight_ref[member]
        to = pl.ds(pl.multiple_of(step * N_TILE, N_TILE), N_TILE)
        out_ref[:, to] = hidden.astype(jnp.bfloat16)


def hidden_units(pieces, w_gate, w_up, experts):
    members, width, hid = w_gate.shape
    rows = sum(piece.shape[0] for piece in pieces)
    vmem = pl.BlockSpec(memory_space=pltpu.VMEM)
    return pl.pallas_call(
        functools.partial(hidden_kernel, experts),
        out_shape=jax.ShapeDtypeStruct((rows, members * hid), jnp.bfloat16),
        in_specs=[vmem] * (len(pieces) + 2),
        out_specs=vmem,
        scratch_shapes=[
            pltpu.VMEM((rows, width), jnp.bfloat16),
            pltpu.VMEM((members, rows, 1), jnp.float32),
        ],
        compiler_params=pltpu.CompilerParams(vmem_limit_bytes=VMEM_LIMIT),
        cost_estimate=pl.CostEstimate(
            flops=4 * rows * members * width * hid,
            bytes_accessed=4 * members * width * hid,
            transcendentals=rows * members * hid,
        ),
        name="hidden",
    )(*pieces, w_gate, w_up)


def down_kernel(chunk, hidden_ref, down_ref, *outs):
    part, width = outs[0].shape

    @pl.loop(0, width // DOWN_TILE)
    def _(step):
        at = pl.ds(pl.multiple_of(step * DOWN_TILE, DOWN_TILE), DOWN_TILE)
        there = pl.ds(pl.multiple_of(chunk * width + step * DOWN_TILE, DOWN_TILE), DOWN_TILE)
        total = jnp.dot(
            hidden_ref[...], down_ref[:, there], preferred_element_type=jnp.float32
        ).astype(jnp.bfloat16)
        for i, ref in enumerate(outs):
            ref[:, at] = total[i * part : (i + 1) * part]


def down(hidden, w_down, chunk, chunks):
    units, width = w_down.shape
    rows = hidden.shape[0]
    vmem = pl.BlockSpec(memory_space=pltpu.VMEM)
    return pl.pallas_call(
        functools.partial(down_kernel, chunk),
        out_shape=[jax.ShapeDtypeStruct((rows // 4, width // chunks), jnp.bfloat16)] * 4,
        in_specs=[vmem, vmem],
        out_specs=[vmem] * 4,
        compiler_params=pltpu.CompilerParams(vmem_limit_bytes=VMEM_LIMIT),
        cost_estimate=pl.CostEstimate(
            flops=2 * rows * units * width // chunks,
            bytes_accessed=2 * units * width // chunks,
            transcendentals=0,
        ),
        name="down",
    )(hidden, w_down)


CHIPS, PLACES = 2, 4


def to_core(value):
    return lax.ppermute(value, "node", [(i, i ^ 1) for i in range(2 * CHIPS)])


def to_chip(value):
    return lax.ppermute(value, "node", [(i, i ^ 2) for i in range(2 * CHIPS)])


def to_place(value, bits):
    return lax.ppermute(value, "local", [(i, i ^ bits) for i in range(PLACES)])


def to_both(value, bits):
    count = 2 * CHIPS * PLACES
    perm = [(i, i ^ (2 * PLACES + bits)) for i in range(count)]
    return lax.ppermute(value, ("node", "local"), perm)


def after(value, *others):
    return lax.optimization_barrier((value, *others))[0]


def gather_blocks(own):
    second, first, far_own = to_place(own, 2), to_place(own, 1), to_chip(own)
    far_first = to_chip(first)
    other = [to_core(own), to_core(far_own), to_core(first)]
    ready = after(second, other[2], far_own)
    far_second, third = to_chip(ready), to_place(ready, 1)
    far_third = to_both(after(ready, far_first), 1)
    other += [to_core(after(piece, far_second)) for piece in (far_first, second, third)]
    other += [to_core(piece) for piece in (far_second, far_third)]
    chip = [own, far_own, first, far_first, second, third, far_second, far_third]
    return chip + other


def total(*terms):
    return sum(term.astype(jnp.float32) for term in terms)


def reduce_blocks(early, late, other_early, other_late, rows):
    def blocks(here, other):
        return total(here, other).astype(jnp.bfloat16).reshape(PLACES, rows, -1)

    other_late = to_core(other_late)
    other_early = to_core(after(other_early, other_late))
    second, third, far_second, far_third = blocks(late, other_late)
    second = total(second, to_chip(far_second), to_both(far_third, 1), to_place(third, 1))
    second = second.astype(jnp.bfloat16)
    own, far_own, first, far_first = blocks(early, other_early)
    first = total(first, to_chip(far_first)).astype(jnp.bfloat16)
    far_own = to_chip(after(far_own, second))
    return total(own, to_place(second, 2), far_own, to_place(first, 1)).astype(jnp.bfloat16)


def by_permutes(tokens, expert_ids, route_weights, expert_slot, w_gate, w_up, w_down):
    rows = tokens.shape[0]
    own = pack(tokens, expert_ids, route_weights, expert_slot, w_gate, w_up, w_down)
    hidden = hidden_units(gather_blocks(own), w_gate, w_up, expert_slot.shape[0])
    matrix = w_down.reshape(-1, w_down.shape[-1])
    outs = []
    for chunk in range(OUT_CHUNKS):
        outs.append(reduce_blocks(*down(hidden, matrix, chunk, OUT_CHUNKS), rows))
    return jnp.concatenate(outs, axis=1)


def by_collectives(tokens, expert_ids, route_weights, expert_slot, w_gate, w_up, w_down):
    members, width, _ = w_gate.shape
    experts = expert_slot.shape[0]
    packed = pack(tokens, expert_ids, route_weights, expert_slot)
    gathered = lax.all_gather(packed, ("node", "local"), axis=0, tiled=True)
    rows = gathered[:, :width]
    tail = gathered[:, width : width + 3 * experts].astype(jnp.float32)
    weights = tail.reshape(-1, 3, experts).sum(axis=1)
    mine = lax.dynamic_slice_in_dim(weights, lax.axis_index("node") * members, members, axis=1)
    gate = jnp.einsum("td,edh->eth", rows, w_gate, preferred_element_type=jnp.float32)
    up = jnp.einsum("td,edh->eth", rows, w_up, preferred_element_type=jnp.float32)
    hidden = (jax.nn.silu(gate) * up * mine.T[..., None]).astype(jnp.bfloat16)
    result = jnp.einsum("eth,ehd->td", hidden, w_down, preferred_element_type=jnp.float32)
    return lax.psum_scatter(
        result.astype(jnp.bfloat16), ("node", "local"), scatter_dimension=0, tiled=True
    )


def per_device(*args):
    small = (lax.axis_size("node"), lax.axis_size("local")) == (2 * CHIPS, PLACES)
    return (by_permutes if small else by_collectives)(*args)


def solution(mesh):
    rows = P(("parts", "node", "local"), None)
    in_specs = (
        rows,
        rows,
        rows,
        P(),
        P("node", None, "local"),
        P("node", None, "local"),
        P("node", "local", None),
    )
    return jax.shard_map(
        per_device, mesh=mesh, in_specs=in_specs, out_specs=rows, check_vma=False
    )
```

```python
import functools

import jax
import jax.numpy as jnp
from jax import lax
from jax.experimental import pallas as pl
from jax.experimental.pallas import tpu as pltpu
from jax.sharding import PartitionSpec as P

LANES = 128
N_TILE = 256
DOWN_TILE = 1792
OUT_CHUNKS = 1
VMEM_LIMIT = 4 * 2**20


def pack_kernel(*refs):
    inputs, out_ref, local, sems = refs[:4], refs[-6], refs[-5:-1], refs[-1]
    copies = [
        pltpu.make_async_copy(here, there, sems.at[i])
        for i, (here, there) in enumerate(zip(inputs, local))
    ]
    for copy in copies:
        copy.start()
    for copy in copies:
        copy.wait()
    tokens_ref, ids_ref, route_ref, slot_ref = local
    rows, width = tokens_ref.shape
    experts = slot_ref.shape[0]
    row = lax.broadcasted_iota(jnp.int32, (rows, LANES), 0)
    column = lax.broadcasted_iota(jnp.int32, (rows, LANES), 1)
    slot = lax.rem(column, experts)
    weights = jnp.zeros((rows, LANES), jnp.float32)
    for k in range(ids_ref.shape[0]):
        for token in range(rows):
            named = (row == token) & (slot == slot_ref[ids_ref[k, token]])
            weights = jnp.where(named, route_ref[k, token], weights)
    first = weights.astype(jnp.bfloat16).astype(jnp.float32)
    second = (weights - first).astype(jnp.bfloat16).astype(jnp.float32)
    third = weights - first - second
    tail = jnp.where(column < experts, first, jnp.where(column < 2 * experts, second, third))
    out_ref[:, :width] = tokens_ref[...]
    out_ref[:, width:] = jnp.where(column < 3 * experts, tail, 0.0).astype(jnp.bfloat16)


def pack(tokens, expert_ids, route_weights, expert_slot, *weights):
    rows, width = tokens.shape
    inputs = (tokens, expert_ids.T, route_weights.T, expert_slot)
    held = [pltpu.with_memory_space_constraint(each, pltpu.HBM) for each in inputs + weights]
    return pl.pallas_call(
        pack_kernel,
        out_shape=jax.ShapeDtypeStruct((rows, width + LANES), jnp.bfloat16),
        in_specs=[pl.BlockSpec(memory_space=pl.ANY)] * len(held),
        out_specs=pl.BlockSpec(memory_space=pltpu.VMEM),
        scratch_shapes=[
            pltpu.VMEM(tokens.shape, tokens.dtype),
            *[pltpu.SMEM(each.shape, each.dtype) for each in inputs[1:]],
            pltpu.SemaphoreType.DMA((len(inputs),)),
        ],
        compiler_params=pltpu.CompilerParams(vmem_limit_bytes=VMEM_LIMIT),
        name="pack",
    )(*held)


def stack_kernel(*refs):
    *pieces, out_ref = refs
    out_ref[...] = jnp.concatenate([piece[...] for piece in pieces], axis=0)


def stack(*pieces):
    rows = sum(piece.shape[0] for piece in pieces)
    vmem = pl.BlockSpec(memory_space=pltpu.VMEM)
    return pl.pallas_call(
        stack_kernel,
        out_shape=jax.ShapeDtypeStruct((rows, pieces[0].shape[1]), pieces[0].dtype),
        in_specs=[vmem] * len(pieces),
        out_specs=vmem,
        compiler_params=pltpu.CompilerParams(vmem_limit_bytes=VMEM_LIMIT),
        name="stack",
    )(*pieces)


def hidden_kernel(experts, *refs):
    *pieces, gate_ref, up_ref, out_ref, x_ref, weight_ref = refs
    members, width, hid = gate_ref.shape
    x_ref[...] = jnp.concatenate([piece[:, :width] for piece in pieces], axis=0)
    tail = jnp.concatenate([piece[:, width:] for piece in pieces], axis=0)
    tail = tail.astype(jnp.float32)
    column = lax.broadcasted_iota(jnp.int32, tail.shape, 1)
    for member in range(members):
        slot = lax.axis_index("node") * members + member
        mine = (lax.rem(column, experts) == slot) & (column < 3 * experts)
        weight_ref[member] = jnp.sum(jnp.where(mine, tail, 0.0), axis=1, keepdims=True)
    tiles = hid // N_TILE

    @pl.loop(0, members * tiles)
    def _(step):
        member = step // tiles
        at = pl.ds(pl.multiple_of(lax.rem(step, tiles) * N_TILE, N_TILE), N_TILE)
        gate, up = [
            jnp.dot(x_ref[...], ref[member, :, at], preferred_element_type=jnp.float32)
            for ref in (gate_ref, up_ref)
        ]
        hidden = gate / (1.0 + jnp.exp(-gate)) * up * weight_ref[member]
        to = pl.ds(pl.multiple_of(step * N_TILE, N_TILE), N_TILE)
        out_ref[:, to] = hidden.astype(jnp.bfloat16)


def hidden_units(pieces, w_gate, w_up, experts):
    members, width, hid = w_gate.shape
    rows = sum(piece.shape[0] for piece in pieces)
    vmem = pl.BlockSpec(memory_space=pltpu.VMEM)
    return pl.pallas_call(
        functools.partial(hidden_kernel, experts),
        out_shape=jax.ShapeDtypeStruct((rows, members * hid), jnp.bfloat16),
        in_specs=[vmem] * (len(pieces) + 2),
        out_specs=vmem,
        scratch_shapes=[
            pltpu.VMEM((rows, width), jnp.bfloat16),
            pltpu.VMEM((members, rows, 1), jnp.float32),
        ],
        compiler_params=pltpu.CompilerParams(vmem_limit_bytes=VMEM_LIMIT),
        cost_estimate=pl.CostEstimate(
            flops=4 * rows * members * width * hid,
            bytes_accessed=4 * members * width * hid,
            transcendentals=rows * members * hid,
        ),
        name="hidden",
    )(*pieces, w_gate, w_up)


def down_kernel(chunk, hidden_ref, down_ref, *outs):
    part, width = outs[0].shape

    @pl.loop(0, width // DOWN_TILE)
    def _(step):
        at = pl.ds(pl.multiple_of(step * DOWN_TILE, DOWN_TILE), DOWN_TILE)
        there = pl.ds(pl.multiple_of(chunk * width + step * DOWN_TILE, DOWN_TILE), DOWN_TILE)
        total = jnp.dot(
            hidden_ref[...], down_ref[:, there], preferred_element_type=jnp.float32
        ).astype(jnp.bfloat16)
        for i, ref in enumerate(outs):
            ref[:, at] = total[i * part : (i + 1) * part]


def down(hidden, w_down, chunk, chunks):
    units, width = w_down.shape
    rows = hidden.shape[0]
    vmem = pl.BlockSpec(memory_space=pltpu.VMEM)
    return pl.pallas_call(
        functools.partial(down_kernel, chunk),
        out_shape=[jax.ShapeDtypeStruct((rows // 4, width // chunks), jnp.bfloat16)] * 4,
        in_specs=[vmem, vmem],
        out_specs=[vmem] * 4,
        compiler_params=pltpu.CompilerParams(vmem_limit_bytes=VMEM_LIMIT),
        cost_estimate=pl.CostEstimate(
            flops=2 * rows * units * width // chunks,
            bytes_accessed=2 * units * width // chunks,
            transcendentals=0,
        ),
        name="down",
    )(hidden, w_down)


CHIPS, PLACES = 2, 4


def to_core(value):
    return lax.ppermute(value, "node", [(i, i ^ 1) for i in range(2 * CHIPS)])


def to_chip(value):
    return lax.ppermute(value, "node", [(i, i ^ 2) for i in range(2 * CHIPS)])


def to_place(value, bits):
    return lax.ppermute(value, "local", [(i, i ^ bits) for i in range(PLACES)])


def to_both(value, bits):
    count = 2 * CHIPS * PLACES
    perm = [(i, i ^ (2 * PLACES + bits)) for i in range(count)]
    return lax.ppermute(value, ("node", "local"), perm)


def after(value, *others):
    return lax.optimization_barrier((value, *others))[0]


def gather_blocks(own):
    second, first, far_own = to_place(own, 2), to_place(own, 1), to_chip(own)
    far_first = to_chip(first)
    ready = after(second, far_own)
    far_second, far_third = to_chip(ready), to_both(ready, 1)
    third = to_place(after(ready, far_first), 1)
    early, late = stack(own, far_own, first, far_first), stack(second, third, far_second, far_third)
    return [early, late, to_core(early), to_core(late)]


def total(*terms):
    return sum(term.astype(jnp.float32) for term in terms)


def reduce_blocks(early, late, other_early, other_late, rows):
    def blocks(here, other):
        return total(here, other).astype(jnp.bfloat16).reshape(PLACES, rows, -1)

    other_late = to_core(other_late)
    other_early = to_core(after(other_early, other_late))
    second, third, far_second, far_third = blocks(late, other_late)
    second = total(second, to_chip(far_second), to_both(far_third, 1), to_place(third, 1))
    second = second.astype(jnp.bfloat16)
    own, far_own, first, far_first = blocks(early, other_early)
    first = total(first, to_chip(far_first)).astype(jnp.bfloat16)
    far_own = to_chip(after(far_own, second))
    return total(own, to_place(second, 2), far_own, to_place(first, 1)).astype(jnp.bfloat16)


def by_permutes(tokens, expert_ids, route_weights, expert_slot, w_gate, w_up, w_down):
    rows = tokens.shape[0]
    own = pack(tokens, expert_ids, route_weights, expert_slot, w_gate, w_up, w_down)
    hidden = hidden_units(gather_blocks(own), w_gate, w_up, expert_slot.shape[0])
    matrix = w_down.reshape(-1, w_down.shape[-1])
    outs = []
    for chunk in range(OUT_CHUNKS):
        outs.append(reduce_blocks(*down(hidden, matrix, chunk, OUT_CHUNKS), rows))
    return jnp.concatenate(outs, axis=1)


def by_collectives(tokens, expert_ids, route_weights, expert_slot, w_gate, w_up, w_down):
    members, width, _ = w_gate.shape
    experts = expert_slot.shape[0]
    packed = pack(tokens, expert_ids, route_weights, expert_slot)
    gathered = lax.all_gather(packed, ("node", "local"), axis=0, tiled=True)
    rows = gathered[:, :width]
    tail = gathered[:, width : width + 3 * experts].astype(jnp.float32)
    weights = tail.reshape(-1, 3, experts).sum(axis=1)
    mine = lax.dynamic_slice_in_dim(weights, lax.axis_index("node") * members, members, axis=1)
    gate = jnp.einsum("td,edh->eth", rows, w_gate, preferred_element_type=jnp.float32)
    up = jnp.einsum("td,edh->eth", rows, w_up, preferred_element_type=jnp.float32)
    hidden = (jax.nn.silu(gate) * up * mine.T[..., None]).astype(jnp.bfloat16)
    result = jnp.einsum("eth,ehd->td", hidden, w_down, preferred_element_type=jnp.float32)
    return lax.psum_scatter(
        result.astype(jnp.bfloat16), ("node", "local"), scatter_dimension=0, tiled=True
    )


def per_device(*args):
    small = (lax.axis_size("node"), lax.axis_size("local")) == (2 * CHIPS, PLACES)
    return (by_permutes if small else by_collectives)(*args)


def solution(mesh):
    rows = P(("parts", "node", "local"), None)
    in_specs = (
        rows,
        rows,
        rows,
        P(),
        P("node", None, "local"),
        P("node", None, "local"),
        P("node", "local", None),
    )
    return jax.shard_map(
        per_device, mesh=mesh, in_specs=in_specs, out_specs=rows, check_vma=False
    )
```

```python
import functools

import jax
import jax.numpy as jnp
from jax import lax
from jax.experimental import pallas as pl
from jax.experimental.pallas import tpu as pltpu
from jax.sharding import PartitionSpec as P

LANES = 128
N_TILE = 256
DOWN_TILE = 1792
OUT_CHUNKS = 1
VMEM_LIMIT = 4 * 2**20


def pack_kernel(*refs):
    inputs, out_ref, local, sems = refs[:4], refs[-6], refs[-5:-1], refs[-1]
    copies = [
        pltpu.make_async_copy(here, there, sems.at[i])
        for i, (here, there) in enumerate(zip(inputs, local))
    ]
    for copy in copies:
        copy.start()
    for copy in copies:
        copy.wait()
    tokens_ref, ids_ref, route_ref, slot_ref = local
    rows, width = tokens_ref.shape
    experts = slot_ref.shape[0]
    row = lax.broadcasted_iota(jnp.int32, (rows, LANES), 0)
    column = lax.broadcasted_iota(jnp.int32, (rows, LANES), 1)
    slot = lax.rem(column, experts)
    weights = jnp.zeros((rows, LANES), jnp.float32)
    for k in range(ids_ref.shape[0]):
        for token in range(rows):
            named = (row == token) & (slot == slot_ref[ids_ref[k, token]])
            weights = jnp.where(named, route_ref[k, token], weights)
    first = weights.astype(jnp.bfloat16).astype(jnp.float32)
    second = (weights - first).astype(jnp.bfloat16).astype(jnp.float32)
    third = weights - first - second
    tail = jnp.where(column < experts, first, jnp.where(column < 2 * experts, second, third))
    out_ref[:, :width] = tokens_ref[...]
    out_ref[:, width:] = jnp.where(column < 3 * experts, tail, 0.0).astype(jnp.bfloat16)


def pack(tokens, expert_ids, route_weights, expert_slot, *weights):
    rows, width = tokens.shape
    inputs = (tokens, expert_ids.T, route_weights.T, expert_slot)
    held = [pltpu.with_memory_space_constraint(each, pltpu.HBM) for each in inputs + weights]
    return pl.pallas_call(
        pack_kernel,
        out_shape=jax.ShapeDtypeStruct((rows, width + LANES), jnp.bfloat16),
        in_specs=[pl.BlockSpec(memory_space=pl.ANY)] * len(held),
        out_specs=pl.BlockSpec(memory_space=pltpu.VMEM),
        scratch_shapes=[
            pltpu.VMEM(tokens.shape, tokens.dtype),
            *[pltpu.SMEM(each.shape, each.dtype) for each in inputs[1:]],
            pltpu.SemaphoreType.DMA((len(inputs),)),
        ],
        compiler_params=pltpu.CompilerParams(vmem_limit_bytes=VMEM_LIMIT),
        name="pack",
    )(*held)


def stack_kernel(*refs):
    *pieces, out_ref = refs
    out_ref[...] = jnp.concatenate([piece[...] for piece in pieces], axis=0)


def stack(*pieces):
    rows = sum(piece.shape[0] for piece in pieces)
    vmem = pl.BlockSpec(memory_space=pltpu.VMEM)
    return pl.pallas_call(
        stack_kernel,
        out_shape=jax.ShapeDtypeStruct((rows, pieces[0].shape[1]), pieces[0].dtype),
        in_specs=[vmem] * len(pieces),
        out_specs=vmem,
        compiler_params=pltpu.CompilerParams(vmem_limit_bytes=VMEM_LIMIT),
        name="stack",
    )(*pieces)


def hidden_kernel(experts, *refs):
    *pieces, gate_ref, up_ref, out_ref, x_ref, weight_ref = refs
    members, width, hid = gate_ref.shape
    x_ref[...] = jnp.concatenate([piece[:, :width] for piece in pieces], axis=0)
    tail = jnp.concatenate([piece[:, width:] for piece in pieces], axis=0)
    tail = tail.astype(jnp.float32)
    column = lax.broadcasted_iota(jnp.int32, tail.shape, 1)
    for member in range(members):
        slot = lax.axis_index("node") * members + member
        mine = (lax.rem(column, experts) == slot) & (column < 3 * experts)
        weight_ref[member] = jnp.sum(jnp.where(mine, tail, 0.0), axis=1, keepdims=True)
    tiles = hid // N_TILE

    @pl.loop(0, members * tiles)
    def _(step):
        member = step // tiles
        at = pl.ds(pl.multiple_of(lax.rem(step, tiles) * N_TILE, N_TILE), N_TILE)
        gate, up = [
            jnp.dot(x_ref[...], ref[member, :, at], preferred_element_type=jnp.float32)
            for ref in (gate_ref, up_ref)
        ]
        hidden = gate / (1.0 + jnp.exp(-gate)) * up * weight_ref[member]
        to = pl.ds(pl.multiple_of(step * N_TILE, N_TILE), N_TILE)
        out_ref[:, to] = hidden.astype(jnp.bfloat16)


def hidden_units(pieces, w_gate, w_up, experts):
    members, width, hid = w_gate.shape
    rows = sum(piece.shape[0] for piece in pieces)
    vmem = pl.BlockSpec(memory_space=pltpu.VMEM)
    return pl.pallas_call(
        functools.partial(hidden_kernel, experts),
        out_shape=jax.ShapeDtypeStruct((rows, members * hid), jnp.bfloat16),
        in_specs=[vmem] * (len(pieces) + 2),
        out_specs=vmem,
        scratch_shapes=[
            pltpu.VMEM((rows, width), jnp.bfloat16),
            pltpu.VMEM((members, rows, 1), jnp.float32),
        ],
        compiler_params=pltpu.CompilerParams(vmem_limit_bytes=VMEM_LIMIT),
        cost_estimate=pl.CostEstimate(
            flops=4 * rows * members * width * hid,
            bytes_accessed=4 * members * width * hid,
            transcendentals=rows * members * hid,
        ),
        name="hidden",
    )(*pieces, w_gate, w_up)


def down_kernel(chunk, hidden_ref, down_ref, *outs):
    part, width = outs[0].shape

    @pl.loop(0, width // DOWN_TILE)
    def _(step):
        at = pl.ds(pl.multiple_of(step * DOWN_TILE, DOWN_TILE), DOWN_TILE)
        there = pl.ds(pl.multiple_of(chunk * width + step * DOWN_TILE, DOWN_TILE), DOWN_TILE)
        total = jnp.dot(
            hidden_ref[...], down_ref[:, there], preferred_element_type=jnp.float32
        ).astype(jnp.bfloat16)
        for i, ref in enumerate(outs):
            ref[:, at] = total[i * part : (i + 1) * part]


def down(hidden, w_down, chunk, chunks):
    units, width = w_down.shape
    rows = hidden.shape[0]
    vmem = pl.BlockSpec(memory_space=pltpu.VMEM)
    return pl.pallas_call(
        functools.partial(down_kernel, chunk),
        out_shape=[jax.ShapeDtypeStruct((rows // 4, width // chunks), jnp.bfloat16)] * 4,
        in_specs=[vmem, vmem],
        out_specs=[vmem] * 4,
        compiler_params=pltpu.CompilerParams(vmem_limit_bytes=VMEM_LIMIT),
        cost_estimate=pl.CostEstimate(
            flops=2 * rows * units * width // chunks,
            bytes_accessed=2 * units * width // chunks,
            transcendentals=0,
        ),
        name="down",
    )(hidden, w_down)


CHIPS, PLACES = 2, 4


def to_core(value):
    return lax.ppermute(value, "node", [(i, i ^ 1) for i in range(2 * CHIPS)])


def to_chip(value):
    return lax.ppermute(value, "node", [(i, i ^ 2) for i in range(2 * CHIPS)])


def to_place(value, bits):
    return lax.ppermute(value, "local", [(i, i ^ bits) for i in range(PLACES)])


def to_both(value, bits):
    count = 2 * CHIPS * PLACES
    perm = [(i, i ^ (2 * PLACES + bits)) for i in range(count)]
    return lax.ppermute(value, ("node", "local"), perm)


def after(value, *others):
    return lax.optimization_barrier((value, *others))[0]


def gather_blocks(own):
    second, first, far_own = to_place(own, 2), to_place(own, 1), to_chip(own)
    far_first = to_chip(first)
    ready = after(second, far_own)
    far_second, third = to_chip(ready), to_place(ready, 1)
    far_third = to_both(after(ready, far_first), 1)
    early = stack(own, far_own, first, far_first)
    late = stack(second, third, far_second, far_third)
    return [early, late, to_core(early), to_core(late)]


def total(*terms):
    return sum(term.astype(jnp.float32) for term in terms)


def reduce_blocks(early, late, other_early, other_late, rows):
    def blocks(here, other):
        return total(here, other).astype(jnp.bfloat16).reshape(PLACES, rows, -1)

    other_late = to_core(other_late)
    other_early = to_core(after(other_early, other_late))
    second, third, far_second, far_third = blocks(late, other_late)
    second = total(second, to_chip(far_second), to_both(far_third, 1), to_place(third, 1))
    second = second.astype(jnp.bfloat16)
    own, far_own, first, far_first = blocks(early, other_early)
    first = total(first, to_chip(far_first)).astype(jnp.bfloat16)
    far_own = to_chip(after(far_own, second))
    return total(own, to_place(second, 2), far_own, to_place(first, 1)).astype(jnp.bfloat16)


def by_permutes(tokens, expert_ids, route_weights, expert_slot, w_gate, w_up, w_down):
    rows = tokens.shape[0]
    own = pack(tokens, expert_ids, route_weights, expert_slot, w_gate, w_up, w_down)
    hidden = hidden_units(gather_blocks(own), w_gate, w_up, expert_slot.shape[0])
    matrix = w_down.reshape(-1, w_down.shape[-1])
    outs = []
    for chunk in range(OUT_CHUNKS):
        outs.append(reduce_blocks(*down(hidden, matrix, chunk, OUT_CHUNKS), rows))
    return jnp.concatenate(outs, axis=1)


def by_collectives(tokens, expert_ids, route_weights, expert_slot, w_gate, w_up, w_down):
    members, width, _ = w_gate.shape
    experts = expert_slot.shape[0]
    packed = pack(tokens, expert_ids, route_weights, expert_slot)
    gathered = lax.all_gather(packed, ("node", "local"), axis=0, tiled=True)
    rows = gathered[:, :width]
    tail = gathered[:, width : width + 3 * experts].astype(jnp.float32)
    weights = tail.reshape(-1, 3, experts).sum(axis=1)
    mine = lax.dynamic_slice_in_dim(weights, lax.axis_index("node") * members, members, axis=1)
    gate = jnp.einsum("td,edh->eth", rows, w_gate, preferred_element_type=jnp.float32)
    up = jnp.einsum("td,edh->eth", rows, w_up, preferred_element_type=jnp.float32)
    hidden = (jax.nn.silu(gate) * up * mine.T[..., None]).astype(jnp.bfloat16)
    result = jnp.einsum("eth,ehd->td", hidden, w_down, preferred_element_type=jnp.float32)
    return lax.psum_scatter(
        result.astype(jnp.bfloat16), ("node", "local"), scatter_dimension=0, tiled=True
    )


def per_device(*args):
    small = (lax.axis_size("node"), lax.axis_size("local")) == (2 * CHIPS, PLACES)
    return (by_permutes if small else by_collectives)(*args)


def solution(mesh):
    rows = P(("parts", "node", "local"), None)
    in_specs = (
        rows,
        rows,
        rows,
        P(),
        P("node", None, "local"),
        P("node", None, "local"),
        P("node", "local", None),
    )
    return jax.shard_map(
        per_device, mesh=mesh, in_specs=in_specs, out_specs=rows, check_vma=False
    )
```

```python
import functools

import jax
import jax.numpy as jnp
from jax import lax
from jax.experimental import pallas as pl
from jax.experimental.pallas import tpu as pltpu
from jax.sharding import PartitionSpec as P

LANES = 128
N_TILE = 256
DOWN_TILE = 1792
OUT_CHUNKS = 1
VMEM_LIMIT = 4 * 2**20


def pack_kernel(*refs):
    inputs, out_ref, local, sems = refs[:4], refs[-6], refs[-5:-1], refs[-1]
    copies = [
        pltpu.make_async_copy(here, there, sems.at[i])
        for i, (here, there) in enumerate(zip(inputs, local))
    ]
    for copy in copies:
        copy.start()
    for copy in copies:
        copy.wait()
    tokens_ref, ids_ref, route_ref, slot_ref = local
    rows, width = tokens_ref.shape
    experts = slot_ref.shape[0]
    row = lax.broadcasted_iota(jnp.int32, (rows, LANES), 0)
    column = lax.broadcasted_iota(jnp.int32, (rows, LANES), 1)
    slot = lax.rem(column, experts)
    weights = jnp.zeros((rows, LANES), jnp.float32)
    for k in range(ids_ref.shape[0]):
        for token in range(rows):
            named = (row == token) & (slot == slot_ref[ids_ref[k, token]])
            weights = jnp.where(named, route_ref[k, token], weights)
    first = weights.astype(jnp.bfloat16).astype(jnp.float32)
    second = (weights - first).astype(jnp.bfloat16).astype(jnp.float32)
    third = weights - first - second
    tail = jnp.where(column < experts, first, jnp.where(column < 2 * experts, second, third))
    out_ref[:, :width] = tokens_ref[...]
    out_ref[:, width:] = jnp.where(column < 3 * experts, tail, 0.0).astype(jnp.bfloat16)


def pack(tokens, expert_ids, route_weights, expert_slot, *weights):
    rows, width = tokens.shape
    inputs = (tokens, expert_ids.T, route_weights.T, expert_slot)
    held = [pltpu.with_memory_space_constraint(each, pltpu.HBM) for each in inputs + weights]
    return pl.pallas_call(
        pack_kernel,
        out_shape=jax.ShapeDtypeStruct((rows, width + LANES), jnp.bfloat16),
        in_specs=[pl.BlockSpec(memory_space=pl.ANY)] * len(held),
        out_specs=pl.BlockSpec(memory_space=pltpu.VMEM),
        scratch_shapes=[
            pltpu.VMEM(tokens.shape, tokens.dtype),
            *[pltpu.SMEM(each.shape, each.dtype) for each in inputs[1:]],
            pltpu.SemaphoreType.DMA((len(inputs),)),
        ],
        compiler_params=pltpu.CompilerParams(vmem_limit_bytes=VMEM_LIMIT),
        name="pack",
    )(*held)


def stack_kernel(*refs):
    *pieces, out_ref = refs
    out_ref[...] = jnp.concatenate([piece[...] for piece in pieces], axis=0)


def stack(*pieces):
    rows = sum(piece.shape[0] for piece in pieces)
    vmem = pl.BlockSpec(memory_space=pltpu.VMEM)
    return pl.pallas_call(
        stack_kernel,
        out_shape=jax.ShapeDtypeStruct((rows, pieces[0].shape[1]), pieces[0].dtype),
        in_specs=[vmem] * len(pieces),
        out_specs=vmem,
        compiler_params=pltpu.CompilerParams(vmem_limit_bytes=VMEM_LIMIT),
        name="stack",
    )(*pieces)


def hidden_kernel(experts, *refs):
    *pieces, gate_ref, up_ref, out_ref, x_ref, weight_ref = refs
    members, width, hid = gate_ref.shape
    x_ref[...] = jnp.concatenate([piece[:, :width] for piece in pieces], axis=0)
    tail = jnp.concatenate([piece[:, width:] for piece in pieces], axis=0)
    tail = tail.astype(jnp.float32)
    column = lax.broadcasted_iota(jnp.int32, tail.shape, 1)
    for member in range(members):
        slot = lax.axis_index("node") * members + member
        mine = (lax.rem(column, experts) == slot) & (column < 3 * experts)
        weight_ref[member] = jnp.sum(jnp.where(mine, tail, 0.0), axis=1, keepdims=True)
    tiles = hid // N_TILE

    @pl.loop(0, members * tiles)
    def _(step):
        member = step // tiles
        at = pl.ds(pl.multiple_of(lax.rem(step, tiles) * N_TILE, N_TILE), N_TILE)
        gate, up = [
            jnp.dot(x_ref[...], ref[member, :, at], preferred_element_type=jnp.float32)
            for ref in (gate_ref, up_ref)
        ]
        hidden = gate / (1.0 + jnp.exp(-gate)) * up * weight_ref[member]
        to = pl.ds(pl.multiple_of(step * N_TILE, N_TILE), N_TILE)
        out_ref[:, to] = hidden.astype(jnp.bfloat16)


def hidden_units(pieces, w_gate, w_up, experts):
    members, width, hid = w_gate.shape
    rows = sum(piece.shape[0] for piece in pieces)
    vmem = pl.BlockSpec(memory_space=pltpu.VMEM)
    return pl.pallas_call(
        functools.partial(hidden_kernel, experts),
        out_shape=jax.ShapeDtypeStruct((rows, members * hid), jnp.bfloat16),
        in_specs=[vmem] * (len(pieces) + 2),
        out_specs=vmem,
        scratch_shapes=[
            pltpu.VMEM((rows, width), jnp.bfloat16),
            pltpu.VMEM((members, rows, 1), jnp.float32),
        ],
        compiler_params=pltpu.CompilerParams(vmem_limit_bytes=VMEM_LIMIT),
        cost_estimate=pl.CostEstimate(
            flops=4 * rows * members * width * hid,
            bytes_accessed=4 * members * width * hid,
            transcendentals=rows * members * hid,
        ),
        name="hidden",
    )(*pieces, w_gate, w_up)


def down_kernel(chunk, hidden_ref, down_ref, *outs):
    part, width = outs[0].shape

    @pl.loop(0, width // DOWN_TILE)
    def _(step):
        at = pl.ds(pl.multiple_of(step * DOWN_TILE, DOWN_TILE), DOWN_TILE)
        there = pl.ds(pl.multiple_of(chunk * width + step * DOWN_TILE, DOWN_TILE), DOWN_TILE)
        total = jnp.dot(
            hidden_ref[...], down_ref[:, there], preferred_element_type=jnp.float32
        ).astype(jnp.bfloat16)
        for i, ref in enumerate(outs):
            ref[:, at] = total[i * part : (i + 1) * part]


def down(hidden, w_down, chunk, chunks):
    units, width = w_down.shape
    rows = hidden.shape[0]
    vmem = pl.BlockSpec(memory_space=pltpu.VMEM)
    return pl.pallas_call(
        functools.partial(down_kernel, chunk),
        out_shape=[jax.ShapeDtypeStruct((rows // 4, width // chunks), jnp.bfloat16)] * 4,
        in_specs=[vmem, vmem],
        out_specs=[vmem] * 4,
        compiler_params=pltpu.CompilerParams(vmem_limit_bytes=VMEM_LIMIT),
        cost_estimate=pl.CostEstimate(
            flops=2 * rows * units * width // chunks,
            bytes_accessed=2 * units * width // chunks,
            transcendentals=0,
        ),
        name="down",
    )(hidden, w_down)


CHIPS, PLACES = 2, 4


def to_core(value):
    return lax.ppermute(value, "node", [(i, i ^ 1) for i in range(2 * CHIPS)])


def to_chip(value):
    return lax.ppermute(value, "node", [(i, i ^ 2) for i in range(2 * CHIPS)])


def to_place(value, bits):
    return lax.ppermute(value, "local", [(i, i ^ bits) for i in range(PLACES)])


def to_both(value, bits):
    count = 2 * CHIPS * PLACES
    perm = [(i, i ^ (2 * PLACES + bits)) for i in range(count)]
    return lax.ppermute(value, ("node", "local"), perm)


def after(value, *others):
    return lax.optimization_barrier((value, *others))[0]


def gather_blocks(own):
    second, first, far_own = to_place(own, 2), to_place(own, 1), to_chip(own)
    far_first = to_chip(first)
    ready = after(second, far_own)
    far_second, third = to_chip(ready), to_place(ready, 1)
    far_third = to_both(after(ready, far_first), 1)
    early = stack(own, far_own, first, far_first)
    late = stack(second, third, far_second, far_third)
    return [early, late, to_core(early), to_core(late)]


def total(*terms):
    return sum(term.astype(jnp.float32) for term in terms)


def reduce_blocks(early, late, other_early, other_late, rows):
    def blocks(here, other):
        return total(here, other).astype(jnp.bfloat16).reshape(PLACES, rows, -1)

    other_late = to_core(other_late)
    other_early = to_core(after(other_early, other_late))
    second, third, far_second, far_third = blocks(late, other_late)
    far_second = to_chip(far_second)
    far_third = to_both(far_third, 1)
    third = to_place(third, 1)
    second = total(second, far_second, far_third, third).astype(jnp.bfloat16)
    own, far_own, first, far_first = blocks(early, other_early)
    first = total(first, to_chip(after(far_first, third))).astype(jnp.bfloat16)
    first, far_own = lax.optimization_barrier((first, far_own))
    second_here, first_here, far_own = to_place(second, 2), to_place(first, 1), to_chip(far_own)
    return total(own, second_here, first_here, far_own).astype(jnp.bfloat16)


def by_permutes(tokens, expert_ids, route_weights, expert_slot, w_gate, w_up, w_down):
    rows = tokens.shape[0]
    own = pack(tokens, expert_ids, route_weights, expert_slot, w_gate, w_up, w_down)
    hidden = hidden_units(gather_blocks(own), w_gate, w_up, expert_slot.shape[0])
    matrix = w_down.reshape(-1, w_down.shape[-1])
    outs = []
    for chunk in range(OUT_CHUNKS):
        outs.append(reduce_blocks(*down(hidden, matrix, chunk, OUT_CHUNKS), rows))
    return jnp.concatenate(outs, axis=1)


def by_collectives(tokens, expert_ids, route_weights, expert_slot, w_gate, w_up, w_down):
    members, width, _ = w_gate.shape
    experts = expert_slot.shape[0]
    packed = pack(tokens, expert_ids, route_weights, expert_slot)
    gathered = lax.all_gather(packed, ("node", "local"), axis=0, tiled=True)
    rows = gathered[:, :width]
    tail = gathered[:, width : width + 3 * experts].astype(jnp.float32)
    weights = tail.reshape(-1, 3, experts).sum(axis=1)
    mine = lax.dynamic_slice_in_dim(weights, lax.axis_index("node") * members, members, axis=1)
    gate = jnp.einsum("td,edh->eth", rows, w_gate, preferred_element_type=jnp.float32)
    up = jnp.einsum("td,edh->eth", rows, w_up, preferred_element_type=jnp.float32)
    hidden = (jax.nn.silu(gate) * up * mine.T[..., None]).astype(jnp.bfloat16)
    result = jnp.einsum("eth,ehd->td", hidden, w_down, preferred_element_type=jnp.float32)
    return lax.psum_scatter(
        result.astype(jnp.bfloat16), ("node", "local"), scatter_dimension=0, tiled=True
    )


def per_device(*args):
    small = (lax.axis_size("node"), lax.axis_size("local")) == (2 * CHIPS, PLACES)
    return (by_permutes if small else by_collectives)(*args)


def solution(mesh):
    rows = P(("parts", "node", "local"), None)
    in_specs = (
        rows,
        rows,
        rows,
        P(),
        P("node", None, "local"),
        P("node", None, "local"),
        P("node", "local", None),
    )
    return jax.shard_map(
        per_device, mesh=mesh, in_specs=in_specs, out_specs=rows, check_vma=False
    )
```

```python
import functools

import jax
import jax.numpy as jnp
from jax import lax
from jax.experimental import pallas as pl
from jax.experimental.pallas import tpu as pltpu
from jax.sharding import PartitionSpec as P

LANES = 128
N_TILE = 256
DOWN_TILE = 1792
OUT_CHUNKS = 2
VMEM_LIMIT = 4 * 2**20


def pack_kernel(*refs):
    inputs, out_ref, local, sems = refs[:4], refs[-6], refs[-5:-1], refs[-1]
    copies = [
        pltpu.make_async_copy(here, there, sems.at[i])
        for i, (here, there) in enumerate(zip(inputs, local))
    ]
    for copy in copies:
        copy.start()
    for copy in copies:
        copy.wait()
    tokens_ref, ids_ref, route_ref, slot_ref = local
    rows, width = tokens_ref.shape
    experts = slot_ref.shape[0]
    row = lax.broadcasted_iota(jnp.int32, (rows, LANES), 0)
    column = lax.broadcasted_iota(jnp.int32, (rows, LANES), 1)
    slot = lax.rem(column, experts)
    weights = jnp.zeros((rows, LANES), jnp.float32)
    for k in range(ids_ref.shape[0]):
        for token in range(rows):
            named = (row == token) & (slot == slot_ref[ids_ref[k, token]])
            weights = jnp.where(named, route_ref[k, token], weights)
    first = weights.astype(jnp.bfloat16).astype(jnp.float32)
    second = (weights - first).astype(jnp.bfloat16).astype(jnp.float32)
    third = weights - first - second
    tail = jnp.where(column < experts, first, jnp.where(column < 2 * experts, second, third))
    out_ref[:, :width] = tokens_ref[...]
    out_ref[:, width:] = jnp.where(column < 3 * experts, tail, 0.0).astype(jnp.bfloat16)


def pack(tokens, expert_ids, route_weights, expert_slot, *weights):
    rows, width = tokens.shape
    inputs = (tokens, expert_ids.T, route_weights.T, expert_slot)
    held = [pltpu.with_memory_space_constraint(each, pltpu.HBM) for each in inputs + weights]
    return pl.pallas_call(
        pack_kernel,
        out_shape=jax.ShapeDtypeStruct((rows, width + LANES), jnp.bfloat16),
        in_specs=[pl.BlockSpec(memory_space=pl.ANY)] * len(held),
        out_specs=pl.BlockSpec(memory_space=pltpu.VMEM),
        scratch_shapes=[
            pltpu.VMEM(tokens.shape, tokens.dtype),
            *[pltpu.SMEM(each.shape, each.dtype) for each in inputs[1:]],
            pltpu.SemaphoreType.DMA((len(inputs),)),
        ],
        compiler_params=pltpu.CompilerParams(vmem_limit_bytes=VMEM_LIMIT),
        name="pack",
    )(*held)


def stack_kernel(*refs):
    *pieces, out_ref = refs
    out_ref[...] = jnp.concatenate([piece[...] for piece in pieces], axis=0)


def stack(*pieces):
    rows = sum(piece.shape[0] for piece in pieces)
    vmem = pl.BlockSpec(memory_space=pltpu.VMEM)
    return pl.pallas_call(
        stack_kernel,
        out_shape=jax.ShapeDtypeStruct((rows, pieces[0].shape[1]), pieces[0].dtype),
        in_specs=[vmem] * len(pieces),
        out_specs=vmem,
        compiler_params=pltpu.CompilerParams(vmem_limit_bytes=VMEM_LIMIT),
        name="stack",
    )(*pieces)


def hidden_kernel(experts, *refs):
    *pieces, gate_ref, up_ref, out_ref, x_ref, weight_ref = refs
    members, width, hid = gate_ref.shape
    x_ref[...] = jnp.concatenate([piece[:, :width] for piece in pieces], axis=0)
    tail = jnp.concatenate([piece[:, width:] for piece in pieces], axis=0)
    tail = tail.astype(jnp.float32)
    column = lax.broadcasted_iota(jnp.int32, tail.shape, 1)
    for member in range(members):
        slot = lax.axis_index("node") * members + member
        mine = (lax.rem(column, experts) == slot) & (column < 3 * experts)
        weight_ref[member] = jnp.sum(jnp.where(mine, tail, 0.0), axis=1, keepdims=True)
    tiles = hid // N_TILE

    @pl.loop(0, members * tiles)
    def _(step):
        member = step // tiles
        at = pl.ds(pl.multiple_of(lax.rem(step, tiles) * N_TILE, N_TILE), N_TILE)
        gate, up = [
            jnp.dot(x_ref[...], ref[member, :, at], preferred_element_type=jnp.float32)
            for ref in (gate_ref, up_ref)
        ]
        hidden = gate / (1.0 + jnp.exp(-gate)) * up * weight_ref[member]
        to = pl.ds(pl.multiple_of(step * N_TILE, N_TILE), N_TILE)
        out_ref[:, to] = hidden.astype(jnp.bfloat16)


def hidden_units(pieces, w_gate, w_up, experts):
    members, width, hid = w_gate.shape
    rows = sum(piece.shape[0] for piece in pieces)
    vmem = pl.BlockSpec(memory_space=pltpu.VMEM)
    return pl.pallas_call(
        functools.partial(hidden_kernel, experts),
        out_shape=jax.ShapeDtypeStruct((rows, members * hid), jnp.bfloat16),
        in_specs=[vmem] * (len(pieces) + 2),
        out_specs=vmem,
        scratch_shapes=[
            pltpu.VMEM((rows, width), jnp.bfloat16),
            pltpu.VMEM((members, rows, 1), jnp.float32),
        ],
        compiler_params=pltpu.CompilerParams(vmem_limit_bytes=VMEM_LIMIT),
        cost_estimate=pl.CostEstimate(
            flops=4 * rows * members * width * hid,
            bytes_accessed=4 * members * width * hid,
            transcendentals=rows * members * hid,
        ),
        name="hidden",
    )(*pieces, w_gate, w_up)


def down_kernel(chunk, hidden_ref, down_ref, *outs):
    part, width = outs[0].shape

    @pl.loop(0, width // DOWN_TILE)
    def _(step):
        at = pl.ds(pl.multiple_of(step * DOWN_TILE, DOWN_TILE), DOWN_TILE)
        there = pl.ds(pl.multiple_of(chunk * width + step * DOWN_TILE, DOWN_TILE), DOWN_TILE)
        total = jnp.dot(
            hidden_ref[...], down_ref[:, there], preferred_element_type=jnp.float32
        ).astype(jnp.bfloat16)
        for i, ref in enumerate(outs):
            ref[:, at] = total[i * part : (i + 1) * part]


def down(hidden, w_down, chunk, chunks):
    units, width = w_down.shape
    rows = hidden.shape[0]
    vmem = pl.BlockSpec(memory_space=pltpu.VMEM)
    return pl.pallas_call(
        functools.partial(down_kernel, chunk),
        out_shape=[jax.ShapeDtypeStruct((rows // 4, width // chunks), jnp.bfloat16)] * 4,
        in_specs=[vmem, vmem],
        out_specs=[vmem] * 4,
        compiler_params=pltpu.CompilerParams(vmem_limit_bytes=VMEM_LIMIT),
        cost_estimate=pl.CostEstimate(
            flops=2 * rows * units * width // chunks,
            bytes_accessed=2 * units * width // chunks,
            transcendentals=0,
        ),
        name="down",
    )(hidden, w_down)


CHIPS, PLACES = 2, 4


def to_core(value):
    return lax.ppermute(value, "node", [(i, i ^ 1) for i in range(2 * CHIPS)])


def to_chip(value):
    return lax.ppermute(value, "node", [(i, i ^ 2) for i in range(2 * CHIPS)])


def to_place(value, bits):
    return lax.ppermute(value, "local", [(i, i ^ bits) for i in range(PLACES)])


def to_both(value, bits):
    count = 2 * CHIPS * PLACES
    perm = [(i, i ^ (2 * PLACES + bits)) for i in range(count)]
    return lax.ppermute(value, ("node", "local"), perm)


def after(value, *others):
    return lax.optimization_barrier((value, *others))[0]


def gather_blocks(own):
    second, first, far_own = to_place(own, 2), to_place(own, 1), to_chip(own)
    far_first = to_chip(first)
    ready = after(second, far_own)
    far_second, third = to_chip(ready), to_place(ready, 1)
    far_third = to_both(after(ready, far_first), 1)
    early = stack(own, far_own, first, far_first)
    late = stack(second, third, far_second, far_third)
    return [early, late, to_core(early), to_core(late)]


def sums_kernel(*refs):
    inputs, outs = refs[: -PLACES], refs[-PLACES:]
    chunks = len(inputs) // 2
    rows, width = outs[0].shape
    for chunk in range(chunks):
        at = pl.ds(chunk * (width // chunks), width // chunks)
        here, other = [ref[...].astype(jnp.float32) for ref in inputs[chunk::chunks]]
        total = here + other
        for place, ref in enumerate(outs):
            ref[:, at] = total[place * rows : (place + 1) * rows].astype(ref.dtype)


def sums(here, other):
    rows, width = here[0].shape[0] // PLACES, here[0].shape[1] * len(here)
    vmem = pl.BlockSpec(memory_space=pltpu.VMEM)
    return pl.pallas_call(
        sums_kernel,
        out_shape=[jax.ShapeDtypeStruct((rows, width), here[0].dtype)] * PLACES,
        in_specs=[vmem] * (2 * len(here)),
        out_specs=[vmem] * PLACES,
        compiler_params=pltpu.CompilerParams(vmem_limit_bytes=VMEM_LIMIT),
        name="sums",
    )(*here, *other)


def total(*terms):
    return sum(term.astype(jnp.float32) for term in terms)


def reduce_blocks(chunks):
    early, late, other_early, other_late = zip(*chunks)
    other_late = [to_core(each) for each in other_late]
    other_early = [to_core(after(each, *other_late)) for each in other_early]
    second, third, far_second, far_third = sums(late, other_late)
    far_second = to_chip(far_second)
    far_third = to_both(far_third, 1)
    third = to_place(third, 1)
    second = total(second, far_second, far_third, third).astype(jnp.bfloat16)
    own, far_own, first, far_first = sums(early, other_early)
    first = total(first, to_chip(after(far_first, third))).astype(jnp.bfloat16)
    first, far_own = lax.optimization_barrier((first, far_own))
    second_here, first_here, far_own = to_place(second, 2), to_place(first, 1), to_chip(far_own)
    return total(own, second_here, first_here, far_own).astype(jnp.bfloat16)


def by_permutes(tokens, expert_ids, route_weights, expert_slot, w_gate, w_up, w_down):
    own = pack(tokens, expert_ids, route_weights, expert_slot, w_gate, w_up, w_down)
    hidden = hidden_units(gather_blocks(own), w_gate, w_up, expert_slot.shape[0])
    matrix = w_down.reshape(-1, w_down.shape[-1])
    chunks = []
    for chunk in range(OUT_CHUNKS):
        chunks.append(down(hidden, matrix, chunk, OUT_CHUNKS))
        hidden = after(hidden, chunks[-1][-1])
    return reduce_blocks(chunks)


def by_collectives(tokens, expert_ids, route_weights, expert_slot, w_gate, w_up, w_down):
    members, width, _ = w_gate.shape
    experts = expert_slot.shape[0]
    packed = pack(tokens, expert_ids, route_weights, expert_slot)
    gathered = lax.all_gather(packed, ("node", "local"), axis=0, tiled=True)
    rows = gathered[:, :width]
    tail = gathered[:, width : width + 3 * experts].astype(jnp.float32)
    weights = tail.reshape(-1, 3, experts).sum(axis=1)
    mine = lax.dynamic_slice_in_dim(weights, lax.axis_index("node") * members, members, axis=1)
    gate = jnp.einsum("td,edh->eth", rows, w_gate, preferred_element_type=jnp.float32)
    up = jnp.einsum("td,edh->eth", rows, w_up, preferred_element_type=jnp.float32)
    hidden = (jax.nn.silu(gate) * up * mine.T[..., None]).astype(jnp.bfloat16)
    result = jnp.einsum("eth,ehd->td", hidden, w_down, preferred_element_type=jnp.float32)
    return lax.psum_scatter(
        result.astype(jnp.bfloat16), ("node", "local"), scatter_dimension=0, tiled=True
    )


def per_device(*args):
    small = (lax.axis_size("node"), lax.axis_size("local")) == (2 * CHIPS, PLACES)
    return (by_permutes if small else by_collectives)(*args)


def solution(mesh):
    rows = P(("parts", "node", "local"), None)
    in_specs = (
        rows,
        rows,
        rows,
        P(),
        P("node", None, "local"),
        P("node", None, "local"),
        P("node", "local", None),
    )
    return jax.shard_map(
        per_device, mesh=mesh, in_specs=in_specs, out_specs=rows, check_vma=False
    )
```

```python
import functools

import jax
import jax.numpy as jnp
from jax import lax
from jax.experimental import pallas as pl
from jax.experimental.pallas import tpu as pltpu
from jax.sharding import PartitionSpec as P

LANES = 128
N_TILE = 256
DOWN_TILE = 1792
OUT_CHUNKS = 1
VMEM_LIMIT = 4 * 2**20


def pack_kernel(*refs):
    inputs, out_ref, local, sems = refs[:4], refs[-6], refs[-5:-1], refs[-1]
    copies = [
        pltpu.make_async_copy(here, there, sems.at[i])
        for i, (here, there) in enumerate(zip(inputs, local))
    ]
    for copy in copies:
        copy.start()
    for copy in copies:
        copy.wait()
    tokens_ref, ids_ref, route_ref, slot_ref = local
    rows, width = tokens_ref.shape
    experts = slot_ref.shape[0]
    row = lax.broadcasted_iota(jnp.int32, (rows, LANES), 0)
    column = lax.broadcasted_iota(jnp.int32, (rows, LANES), 1)
    slot = lax.rem(column, experts)
    weights = jnp.zeros((rows, LANES), jnp.float32)
    for k in range(ids_ref.shape[0]):
        for token in range(rows):
            named = (row == token) & (slot == slot_ref[ids_ref[k, token]])
            weights = jnp.where(named, route_ref[k, token], weights)
    first = weights.astype(jnp.bfloat16).astype(jnp.float32)
    second = (weights - first).astype(jnp.bfloat16).astype(jnp.float32)
    third = weights - first - second
    tail = jnp.where(column < experts, first, jnp.where(column < 2 * experts, second, third))
    out_ref[:, :width] = tokens_ref[...]
    out_ref[:, width:] = jnp.where(column < 3 * experts, tail, 0.0).astype(jnp.bfloat16)


def pack(tokens, expert_ids, route_weights, expert_slot, *weights):
    rows, width = tokens.shape
    inputs = (tokens, expert_ids.T, route_weights.T, expert_slot)
    held = [pltpu.with_memory_space_constraint(each, pltpu.HBM) for each in inputs + weights]
    return pl.pallas_call(
        pack_kernel,
        out_shape=jax.ShapeDtypeStruct((rows, width + LANES), jnp.bfloat16),
        in_specs=[pl.BlockSpec(memory_space=pl.ANY)] * len(held),
        out_specs=pl.BlockSpec(memory_space=pltpu.VMEM),
        scratch_shapes=[
            pltpu.VMEM(tokens.shape, tokens.dtype),
            *[pltpu.SMEM(each.shape, each.dtype) for each in inputs[1:]],
            pltpu.SemaphoreType.DMA((len(inputs),)),
        ],
        compiler_params=pltpu.CompilerParams(vmem_limit_bytes=VMEM_LIMIT),
        name="pack",
    )(*held)


def stack_kernel(*refs):
    *pieces, out_ref = refs
    out_ref[...] = jnp.concatenate([piece[...] for piece in pieces], axis=0)


def stack(*pieces):
    rows = sum(piece.shape[0] for piece in pieces)
    vmem = pl.BlockSpec(memory_space=pltpu.VMEM)
    return pl.pallas_call(
        stack_kernel,
        out_shape=jax.ShapeDtypeStruct((rows, pieces[0].shape[1]), pieces[0].dtype),
        in_specs=[vmem] * len(pieces),
        out_specs=vmem,
        compiler_params=pltpu.CompilerParams(vmem_limit_bytes=VMEM_LIMIT),
        name="stack",
    )(*pieces)


def hidden_kernel(experts, *refs):
    *pieces, gate_ref, up_ref, out_ref, x_ref, weight_ref = refs
    members, width, hid = gate_ref.shape
    x_ref[...] = jnp.concatenate([piece[:, :width] for piece in pieces], axis=0)
    tail = jnp.concatenate([piece[:, width:] for piece in pieces], axis=0)
    tail = tail.astype(jnp.float32)
    column = lax.broadcasted_iota(jnp.int32, tail.shape, 1)
    for member in range(members):
        slot = lax.axis_index("node") * members + member
        mine = (lax.rem(column, experts) == slot) & (column < 3 * experts)
        weight_ref[member] = jnp.sum(jnp.where(mine, tail, 0.0), axis=1, keepdims=True)
    tiles = hid // N_TILE

    @pl.loop(0, members * tiles, unroll=True)
    def _(step):
        member = step // tiles
        at = pl.ds(pl.multiple_of(lax.rem(step, tiles) * N_TILE, N_TILE), N_TILE)
        gate, up = [
            jnp.dot(x_ref[...], ref[member, :, at], preferred_element_type=jnp.float32)
            for ref in (gate_ref, up_ref)
        ]
        hidden = gate / (1.0 + jnp.exp(-gate)) * up * weight_ref[member]
        to = pl.ds(pl.multiple_of(step * N_TILE, N_TILE), N_TILE)
        out_ref[:, to] = hidden.astype(jnp.bfloat16)


def hidden_units(pieces, w_gate, w_up, experts):
    members, width, hid = w_gate.shape
    rows = sum(piece.shape[0] for piece in pieces)
    vmem = pl.BlockSpec(memory_space=pltpu.VMEM)
    return pl.pallas_call(
        functools.partial(hidden_kernel, experts),
        out_shape=jax.ShapeDtypeStruct((rows, members * hid), jnp.bfloat16),
        in_specs=[vmem] * (len(pieces) + 2),
        out_specs=vmem,
        scratch_shapes=[
            pltpu.VMEM((rows, width), jnp.bfloat16),
            pltpu.VMEM((members, rows, 1), jnp.float32),
        ],
        compiler_params=pltpu.CompilerParams(vmem_limit_bytes=VMEM_LIMIT),
        cost_estimate=pl.CostEstimate(
            flops=4 * rows * members * width * hid,
            bytes_accessed=4 * members * width * hid,
            transcendentals=rows * members * hid,
        ),
        name="hidden",
    )(*pieces, w_gate, w_up)


def down_kernel(chunk, hidden_ref, down_ref, *outs):
    part, width = outs[0].shape

    @pl.loop(0, width // DOWN_TILE, unroll=True)
    def _(step):
        at = pl.ds(pl.multiple_of(step * DOWN_TILE, DOWN_TILE), DOWN_TILE)
        there = pl.ds(pl.multiple_of(chunk * width + step * DOWN_TILE, DOWN_TILE), DOWN_TILE)
        total = jnp.dot(
            hidden_ref[...], down_ref[:, there], preferred_element_type=jnp.float32
        ).astype(jnp.bfloat16)
        for i, ref in enumerate(outs):
            ref[:, at] = total[i * part : (i + 1) * part]


def down(hidden, w_down, chunk, chunks):
    units, width = w_down.shape
    rows = hidden.shape[0]
    vmem = pl.BlockSpec(memory_space=pltpu.VMEM)
    return pl.pallas_call(
        functools.partial(down_kernel, chunk),
        out_shape=[jax.ShapeDtypeStruct((rows // 4, width // chunks), jnp.bfloat16)] * 4,
        in_specs=[vmem, vmem],
        out_specs=[vmem] * 4,
        compiler_params=pltpu.CompilerParams(vmem_limit_bytes=VMEM_LIMIT),
        cost_estimate=pl.CostEstimate(
            flops=2 * rows * units * width // chunks,
            bytes_accessed=2 * units * width // chunks,
            transcendentals=0,
        ),
        name="down",
    )(hidden, w_down)


CHIPS, PLACES = 2, 4


def to_core(value):
    return lax.ppermute(value, "node", [(i, i ^ 1) for i in range(2 * CHIPS)])


def to_chip(value):
    return lax.ppermute(value, "node", [(i, i ^ 2) for i in range(2 * CHIPS)])


def to_place(value, bits):
    return lax.ppermute(value, "local", [(i, i ^ bits) for i in range(PLACES)])


def to_both(value, bits):
    count = 2 * CHIPS * PLACES
    perm = [(i, i ^ (2 * PLACES + bits)) for i in range(count)]
    return lax.ppermute(value, ("node", "local"), perm)


def after(value, *others):
    return lax.optimization_barrier((value, *others))[0]


def gather_blocks(own):
    second, first, far_own = to_place(own, 2), to_place(own, 1), to_chip(own)
    far_first = to_chip(first)
    ready = after(second, far_own)
    far_second, third = to_chip(ready), to_place(ready, 1)
    far_third = to_both(after(ready, far_first), 1)
    early = stack(own, far_own, first, far_first)
    late = stack(second, third, far_second, far_third)
    return [early, late, to_core(early), to_core(late)]


def sums_kernel(*refs):
    inputs, outs = refs[: -PLACES], refs[-PLACES:]
    chunks = len(inputs) // 2
    rows, width = outs[0].shape
    for chunk in range(chunks):
        at = pl.ds(chunk * (width // chunks), width // chunks)
        here, other = [ref[...].astype(jnp.float32) for ref in inputs[chunk::chunks]]
        total = here + other
        for place, ref in enumerate(outs):
            ref[:, at] = total[place * rows : (place + 1) * rows].astype(ref.dtype)


def sums(here, other):
    rows, width = here[0].shape[0] // PLACES, here[0].shape[1] * len(here)
    vmem = pl.BlockSpec(memory_space=pltpu.VMEM)
    return pl.pallas_call(
        sums_kernel,
        out_shape=[jax.ShapeDtypeStruct((rows, width), here[0].dtype)] * PLACES,
        in_specs=[vmem] * (2 * len(here)),
        out_specs=[vmem] * PLACES,
        compiler_params=pltpu.CompilerParams(vmem_limit_bytes=VMEM_LIMIT),
        name="sums",
    )(*here, *other)


def total(*terms):
    return sum(term.astype(jnp.float32) for term in terms)


def reduce_blocks(chunks):
    early, late, other_early, other_late = zip(*chunks)
    other_late = [to_core(each) for each in other_late]
    other_early = [to_core(after(each, *other_late)) for each in other_early]
    second, third, far_second, far_third = sums(late, other_late)
    far_second = to_chip(far_second)
    far_third = to_both(far_third, 1)
    third = to_place(third, 1)
    second = total(second, far_second, far_third, third).astype(jnp.bfloat16)
    own, far_own, first, far_first = sums(early, other_early)
    first = total(first, to_chip(after(far_first, third))).astype(jnp.bfloat16)
    first, far_own = lax.optimization_barrier((first, far_own))
    second_here, first_here, far_own = to_place(second, 2), to_place(first, 1), to_chip(far_own)
    return total(own, second_here, first_here, far_own).astype(jnp.bfloat16)


def by_permutes(tokens, expert_ids, route_weights, expert_slot, w_gate, w_up, w_down):
    own = pack(tokens, expert_ids, route_weights, expert_slot, w_gate, w_up, w_down)
    hidden = hidden_units(gather_blocks(own), w_gate, w_up, expert_slot.shape[0])
    matrix = w_down.reshape(-1, w_down.shape[-1])
    chunks = []
    for chunk in range(OUT_CHUNKS):
        chunks.append(down(hidden, matrix, chunk, OUT_CHUNKS))
        hidden = after(hidden, chunks[-1][-1])
    return reduce_blocks(chunks)


def by_collectives(tokens, expert_ids, route_weights, expert_slot, w_gate, w_up, w_down):
    members, width, _ = w_gate.shape
    experts = expert_slot.shape[0]
    packed = pack(tokens, expert_ids, route_weights, expert_slot)
    gathered = lax.all_gather(packed, ("node", "local"), axis=0, tiled=True)
    rows = gathered[:, :width]
    tail = gathered[:, width : width + 3 * experts].astype(jnp.float32)
    weights = tail.reshape(-1, 3, experts).sum(axis=1)
    mine = lax.dynamic_slice_in_dim(weights, lax.axis_index("node") * members, members, axis=1)
    gate = jnp.einsum("td,edh->eth", rows, w_gate, preferred_element_type=jnp.float32)
    up = jnp.einsum("td,edh->eth", rows, w_up, preferred_element_type=jnp.float32)
    hidden = (jax.nn.silu(gate) * up * mine.T[..., None]).astype(jnp.bfloat16)
    result = jnp.einsum("eth,ehd->td", hidden, w_down, preferred_element_type=jnp.float32)
    return lax.psum_scatter(
        result.astype(jnp.bfloat16), ("node", "local"), scatter_dimension=0, tiled=True
    )


def per_device(*args):
    small = (lax.axis_size("node"), lax.axis_size("local")) == (2 * CHIPS, PLACES)
    return (by_permutes if small else by_collectives)(*args)


def solution(mesh):
    rows = P(("parts", "node", "local"), None)
    in_specs = (
        rows,
        rows,
        rows,
        P(),
        P("node", None, "local"),
        P("node", None, "local"),
        P("node", "local", None),
    )
    return jax.shard_map(
        per_device, mesh=mesh, in_specs=in_specs, out_specs=rows, check_vma=False
    )
```

```python
import functools

import jax
import jax.numpy as jnp
from jax import lax
from jax.experimental import pallas as pl
from jax.experimental.pallas import tpu as pltpu
from jax.sharding import PartitionSpec as P

LANES = 128
N_TILE = 256
DOWN_TILE = 1792
OUT_CHUNKS = 1
VMEM_LIMIT = 4 * 2**20


def pack_kernel(*refs):
    inputs, out_ref, local, sems = refs[:4], refs[-6], refs[-5:-1], refs[-1]
    copies = [
        pltpu.make_async_copy(here, there, sems.at[i])
        for i, (here, there) in enumerate(zip(inputs, local))
    ]
    for copy in copies:
        copy.start()
    for copy in copies:
        copy.wait()
    tokens_ref, ids_ref, route_ref, slot_ref = local
    rows, width = tokens_ref.shape
    experts = slot_ref.shape[0]
    row = lax.broadcasted_iota(jnp.int32, (rows, LANES), 0)
    column = lax.broadcasted_iota(jnp.int32, (rows, LANES), 1)
    slot = lax.rem(column, experts)
    weights = jnp.zeros((rows, LANES), jnp.float32)
    for k in range(ids_ref.shape[0]):
        for token in range(rows):
            named = (row == token) & (slot == slot_ref[ids_ref[k, token]])
            weights = jnp.where(named, route_ref[k, token], weights)
    first = weights.astype(jnp.bfloat16).astype(jnp.float32)
    second = (weights - first).astype(jnp.bfloat16).astype(jnp.float32)
    third = weights - first - second
    tail = jnp.where(column < experts, first, jnp.where(column < 2 * experts, second, third))
    out_ref[:, :width] = tokens_ref[...]
    out_ref[:, width:] = jnp.where(column < 3 * experts, tail, 0.0).astype(jnp.bfloat16)


def pack(tokens, expert_ids, route_weights, expert_slot, *weights):
    rows, width = tokens.shape
    inputs = (tokens, expert_ids.T, route_weights.T, expert_slot)
    held = [pltpu.with_memory_space_constraint(each, pltpu.HBM) for each in inputs + weights]
    return pl.pallas_call(
        pack_kernel,
        out_shape=jax.ShapeDtypeStruct((rows, width + LANES), jnp.bfloat16),
        in_specs=[pl.BlockSpec(memory_space=pl.ANY)] * len(held),
        out_specs=pl.BlockSpec(memory_space=pltpu.VMEM),
        scratch_shapes=[
            pltpu.VMEM(tokens.shape, tokens.dtype),
            *[pltpu.SMEM(each.shape, each.dtype) for each in inputs[1:]],
            pltpu.SemaphoreType.DMA((len(inputs),)),
        ],
        compiler_params=pltpu.CompilerParams(vmem_limit_bytes=VMEM_LIMIT),
        name="pack",
    )(*held)


def stack_kernel(*refs):
    *pieces, out_ref = refs
    out_ref[...] = jnp.concatenate([piece[...] for piece in pieces], axis=0)


def stack(*pieces):
    rows = sum(piece.shape[0] for piece in pieces)
    vmem = pl.BlockSpec(memory_space=pltpu.VMEM)
    return pl.pallas_call(
        stack_kernel,
        out_shape=jax.ShapeDtypeStruct((rows, pieces[0].shape[1]), pieces[0].dtype),
        in_specs=[vmem] * len(pieces),
        out_specs=vmem,
        compiler_params=pltpu.CompilerParams(vmem_limit_bytes=VMEM_LIMIT),
        name="stack",
    )(*pieces)


def hidden_kernel(experts, *refs):
    *pieces, gate_ref, up_ref, out_ref, x_ref, weight_ref = refs
    members, width, hid = gate_ref.shape
    x_ref[...] = jnp.concatenate([piece[:, :width] for piece in pieces], axis=0)
    tail = jnp.concatenate([piece[:, width:] for piece in pieces], axis=0)
    tail = tail.astype(jnp.float32)
    column = lax.broadcasted_iota(jnp.int32, tail.shape, 1)
    for member in range(members):
        slot = lax.axis_index("node") * members + member
        mine = (lax.rem(column, experts) == slot) & (column < 3 * experts)
        weight_ref[member] = jnp.sum(jnp.where(mine, tail, 0.0), axis=1, keepdims=True)
    tiles = hid // N_TILE

    @pl.loop(0, members * tiles, unroll=True)
    def _(step):
        member = step // tiles
        at = pl.ds(pl.multiple_of(lax.rem(step, tiles) * N_TILE, N_TILE), N_TILE)
        gate, up = [
            jnp.dot(x_ref[...], ref[member, :, at], preferred_element_type=jnp.float32)
            for ref in (gate_ref, up_ref)
        ]
        hidden = gate / (1.0 + jnp.exp(-gate)) * up * weight_ref[member]
        to = pl.ds(pl.multiple_of(step * N_TILE, N_TILE), N_TILE)
        out_ref[:, to] = hidden.astype(jnp.bfloat16)


def hidden_units(pieces, w_gate, w_up, experts):
    members, width, hid = w_gate.shape
    rows = sum(piece.shape[0] for piece in pieces)
    vmem = pl.BlockSpec(memory_space=pltpu.VMEM)
    return pl.pallas_call(
        functools.partial(hidden_kernel, experts),
        out_shape=jax.ShapeDtypeStruct((rows, members * hid), jnp.bfloat16),
        in_specs=[vmem] * (len(pieces) + 2),
        out_specs=vmem,
        scratch_shapes=[
            pltpu.VMEM((rows, width), jnp.bfloat16),
            pltpu.VMEM((members, rows, 1), jnp.float32),
        ],
        compiler_params=pltpu.CompilerParams(vmem_limit_bytes=VMEM_LIMIT),
        cost_estimate=pl.CostEstimate(
            flops=4 * rows * members * width * hid,
            bytes_accessed=4 * members * width * hid,
            transcendentals=rows * members * hid,
        ),
        name="hidden",
    )(*pieces, w_gate, w_up)


def down_kernel(chunk, hidden_ref, down_ref, *outs):
    part, width = outs[0].shape

    @pl.loop(0, width // DOWN_TILE, unroll=True)
    def _(step):
        at = pl.ds(pl.multiple_of(step * DOWN_TILE, DOWN_TILE), DOWN_TILE)
        there = pl.ds(pl.multiple_of(chunk * width + step * DOWN_TILE, DOWN_TILE), DOWN_TILE)
        total = jnp.dot(
            hidden_ref[...], down_ref[:, there], preferred_element_type=jnp.float32
        ).astype(jnp.bfloat16)
        for i, ref in enumerate(outs):
            ref[:, at] = total[i * part : (i + 1) * part]


def down(hidden, w_down, chunk, chunks):
    units, width = w_down.shape
    rows = hidden.shape[0]
    vmem = pl.BlockSpec(memory_space=pltpu.VMEM)
    return pl.pallas_call(
        functools.partial(down_kernel, chunk),
        out_shape=[jax.ShapeDtypeStruct((rows // 4, width // chunks), jnp.bfloat16)] * 4,
        in_specs=[vmem, vmem],
        out_specs=[vmem] * 4,
        compiler_params=pltpu.CompilerParams(vmem_limit_bytes=VMEM_LIMIT),
        cost_estimate=pl.CostEstimate(
            flops=2 * rows * units * width // chunks,
            bytes_accessed=2 * units * width // chunks,
            transcendentals=0,
        ),
        name="down",
    )(hidden, w_down)


CHIPS, PLACES = 2, 4


def to_core(value):
    return lax.ppermute(value, "node", [(i, i ^ 1) for i in range(2 * CHIPS)])


def to_chip(value):
    return lax.ppermute(value, "node", [(i, i ^ 2) for i in range(2 * CHIPS)])


def to_place(value, bits):
    return lax.ppermute(value, "local", [(i, i ^ bits) for i in range(PLACES)])


def to_both(value, bits):
    count = 2 * CHIPS * PLACES
    perm = [(i, i ^ (2 * PLACES + bits)) for i in range(count)]
    return lax.ppermute(value, ("node", "local"), perm)


def after(value, *others):
    return lax.optimization_barrier((value, *others))[0]


def gather_blocks(own):
    second, first, far_own = to_place(own, 2), to_place(own, 1), to_chip(own)
    far_first = to_chip(first)
    ready = after(second, far_own)
    far_second, third = to_chip(ready), to_place(ready, 1)
    far_third = to_both(after(ready, far_first), 1)
    early = stack(own, far_own, first, second)
    late = stack(far_first, third, far_second, far_third)
    return [early, late, to_core(early), to_core(late)]


def sums_kernel(*refs):
    inputs, outs = refs[: -PLACES], refs[-PLACES:]
    chunks = len(inputs) // 2
    rows, width = outs[0].shape
    for chunk in range(chunks):
        at = pl.ds(chunk * (width // chunks), width // chunks)
        here, other = [ref[...].astype(jnp.float32) for ref in inputs[chunk::chunks]]
        total = here + other
        for place, ref in enumerate(outs):
            ref[:, at] = total[place * rows : (place + 1) * rows].astype(ref.dtype)


def sums(here, other):
    rows, width = here[0].shape[0] // PLACES, here[0].shape[1] * len(here)
    vmem = pl.BlockSpec(memory_space=pltpu.VMEM)
    return pl.pallas_call(
        sums_kernel,
        out_shape=[jax.ShapeDtypeStruct((rows, width), here[0].dtype)] * PLACES,
        in_specs=[vmem] * (2 * len(here)),
        out_specs=[vmem] * PLACES,
        compiler_params=pltpu.CompilerParams(vmem_limit_bytes=VMEM_LIMIT),
        name="sums",
    )(*here, *other)


def total(*terms):
    return sum(term.astype(jnp.float32) for term in terms)


def reduce_blocks(chunks):
    early, late, other_early, other_late = zip(*chunks)
    other_late = [to_core(each) for each in other_late]
    other_early = [to_core(after(each, *other_late)) for each in other_early]
    far_first, third, far_second, far_third = sums(late, other_late)
    third, far_second = to_place(third, 1), to_chip(far_second)
    far_third, far_first = to_both(far_third, 1), to_chip(far_first)
    own, far_own, first, second = sums(early, other_early)
    first = total(first, far_first).astype(jnp.bfloat16)
    second = total(second, third, far_second, far_third).astype(jnp.bfloat16)
    first, far_own = lax.optimization_barrier((first, far_own))
    first_here, second_here, far_own = to_place(first, 1), to_place(second, 2), to_chip(far_own)
    return total(own, second_here, first_here, far_own).astype(jnp.bfloat16)


def by_permutes(tokens, expert_ids, route_weights, expert_slot, w_gate, w_up, w_down):
    own = pack(tokens, expert_ids, route_weights, expert_slot, w_gate, w_up, w_down)
    hidden = hidden_units(gather_blocks(own), w_gate, w_up, expert_slot.shape[0])
    matrix = w_down.reshape(-1, w_down.shape[-1])
    chunks = []
    for chunk in range(OUT_CHUNKS):
        chunks.append(down(hidden, matrix, chunk, OUT_CHUNKS))
        hidden = after(hidden, chunks[-1][-1])
    return reduce_blocks(chunks)


def by_collectives(tokens, expert_ids, route_weights, expert_slot, w_gate, w_up, w_down):
    members, width, _ = w_gate.shape
    experts = expert_slot.shape[0]
    packed = pack(tokens, expert_ids, route_weights, expert_slot)
    gathered = lax.all_gather(packed, ("node", "local"), axis=0, tiled=True)
    rows = gathered[:, :width]
    tail = gathered[:, width : width + 3 * experts].astype(jnp.float32)
    weights = tail.reshape(-1, 3, experts).sum(axis=1)
    mine = lax.dynamic_slice_in_dim(weights, lax.axis_index("node") * members, members, axis=1)
    gate = jnp.einsum("td,edh->eth", rows, w_gate, preferred_element_type=jnp.float32)
    up = jnp.einsum("td,edh->eth", rows, w_up, preferred_element_type=jnp.float32)
    hidden = (jax.nn.silu(gate) * up * mine.T[..., None]).astype(jnp.bfloat16)
    result = jnp.einsum("eth,ehd->td", hidden, w_down, preferred_element_type=jnp.float32)
    return lax.psum_scatter(
        result.astype(jnp.bfloat16), ("node", "local"), scatter_dimension=0, tiled=True
    )


def per_device(*args):
    small = (lax.axis_size("node"), lax.axis_size("local")) == (2 * CHIPS, PLACES)
    return (by_permutes if small else by_collectives)(*args)


def solution(mesh):
    rows = P(("parts", "node", "local"), None)
    in_specs = (
        rows,
        rows,
        rows,
        P(),
        P("node", None, "local"),
        P("node", None, "local"),
        P("node", "local", None),
    )
    return jax.shard_map(
        per_device, mesh=mesh, in_specs=in_specs, out_specs=rows, check_vma=False
    )
```

```python
import functools

import jax
import jax.numpy as jnp
from jax import lax
from jax.experimental import pallas as pl
from jax.experimental.pallas import tpu as pltpu
from jax.sharding import PartitionSpec as P

LANES = 128
N_TILE = 256
DOWN_TILE = 1792
OUT_CHUNKS = 1
VMEM_LIMIT = 4 * 2**20


def pack_kernel(*refs):
    inputs, out_ref, local, sems = refs[:4], refs[-6], refs[-5:-1], refs[-1]
    copies = [
        pltpu.make_async_copy(here, there, sems.at[i])
        for i, (here, there) in enumerate(zip(inputs, local))
    ]
    for copy in copies:
        copy.start()
    for copy in copies:
        copy.wait()
    tokens_ref, ids_ref, route_ref, slot_ref = local
    rows, width = tokens_ref.shape
    experts = slot_ref.shape[0]
    row = lax.broadcasted_iota(jnp.int32, (rows, LANES), 0)
    column = lax.broadcasted_iota(jnp.int32, (rows, LANES), 1)
    slot = lax.rem(column, experts)
    weights = jnp.zeros((rows, LANES), jnp.float32)
    for k in range(ids_ref.shape[0]):
        for token in range(rows):
            named = (row == token) & (slot == slot_ref[ids_ref[k, token]])
            weights = jnp.where(named, route_ref[k, token], weights)
    first = weights.astype(jnp.bfloat16).astype(jnp.float32)
    second = (weights - first).astype(jnp.bfloat16).astype(jnp.float32)
    third = weights - first - second
    tail = jnp.where(column < experts, first, jnp.where(column < 2 * experts, second, third))
    out_ref[:, :width] = tokens_ref[...]
    out_ref[:, width:] = jnp.where(column < 3 * experts, tail, 0.0).astype(jnp.bfloat16)


def pack(tokens, expert_ids, route_weights, expert_slot, *weights):
    rows, width = tokens.shape
    inputs = (tokens, expert_ids.T, route_weights.T, expert_slot)
    held = [pltpu.with_memory_space_constraint(each, pltpu.HBM) for each in inputs + weights]
    return pl.pallas_call(
        pack_kernel,
        out_shape=jax.ShapeDtypeStruct((rows, width + LANES), jnp.bfloat16),
        in_specs=[pl.BlockSpec(memory_space=pl.ANY)] * len(held),
        out_specs=pl.BlockSpec(memory_space=pltpu.VMEM),
        scratch_shapes=[
            pltpu.VMEM(tokens.shape, tokens.dtype),
            *[pltpu.SMEM(each.shape, each.dtype) for each in inputs[1:]],
            pltpu.SemaphoreType.DMA((len(inputs),)),
        ],
        compiler_params=pltpu.CompilerParams(vmem_limit_bytes=VMEM_LIMIT),
        name="pack",
    )(*held)


def stack_kernel(*refs):
    *pieces, out_ref = refs
    out_ref[...] = jnp.concatenate([piece[...] for piece in pieces], axis=0)


def stack(*pieces):
    rows = sum(piece.shape[0] for piece in pieces)
    vmem = pl.BlockSpec(memory_space=pltpu.VMEM)
    return pl.pallas_call(
        stack_kernel,
        out_shape=jax.ShapeDtypeStruct((rows, pieces[0].shape[1]), pieces[0].dtype),
        in_specs=[vmem] * len(pieces),
        out_specs=vmem,
        compiler_params=pltpu.CompilerParams(vmem_limit_bytes=VMEM_LIMIT),
        name="stack",
    )(*pieces)


def hidden_kernel(experts, *refs):
    *pieces, gate_ref, up_ref, out_ref, x_ref, weight_ref = refs
    members, width, hid = gate_ref.shape
    x_ref[...] = jnp.concatenate([piece[:, :width] for piece in pieces], axis=0)
    tail = jnp.concatenate([piece[:, width:] for piece in pieces], axis=0)
    tail = tail.astype(jnp.float32)
    column = lax.broadcasted_iota(jnp.int32, tail.shape, 1)
    for member in range(members):
        slot = lax.axis_index("node") * members + member
        mine = (lax.rem(column, experts) == slot) & (column < 3 * experts)
        weight_ref[member] = jnp.sum(jnp.where(mine, tail, 0.0), axis=1, keepdims=True)
    tiles = hid // N_TILE

    @pl.loop(0, members * tiles, unroll=True)
    def _(step):
        member = step // tiles
        at = pl.ds(pl.multiple_of(lax.rem(step, tiles) * N_TILE, N_TILE), N_TILE)
        gate, up = [
            jnp.dot(x_ref[...], ref[member, :, at], preferred_element_type=jnp.float32)
            for ref in (gate_ref, up_ref)
        ]
        hidden = gate / (1.0 + jnp.exp(-gate)) * up * weight_ref[member]
        to = pl.ds(pl.multiple_of(step * N_TILE, N_TILE), N_TILE)
        out_ref[:, to] = hidden.astype(jnp.bfloat16)


def hidden_units(pieces, w_gate, w_up, experts):
    members, width, hid = w_gate.shape
    rows = sum(piece.shape[0] for piece in pieces)
    vmem = pl.BlockSpec(memory_space=pltpu.VMEM)
    return pl.pallas_call(
        functools.partial(hidden_kernel, experts),
        out_shape=jax.ShapeDtypeStruct((rows, members * hid), jnp.bfloat16),
        in_specs=[vmem] * (len(pieces) + 2),
        out_specs=vmem,
        scratch_shapes=[
            pltpu.VMEM((rows, width), jnp.bfloat16),
            pltpu.VMEM((members, rows, 1), jnp.float32),
        ],
        compiler_params=pltpu.CompilerParams(vmem_limit_bytes=VMEM_LIMIT),
        cost_estimate=pl.CostEstimate(
            flops=4 * rows * members * width * hid,
            bytes_accessed=4 * members * width * hid,
            transcendentals=rows * members * hid,
        ),
        name="hidden",
    )(*pieces, w_gate, w_up)


def down_kernel(chunk, hidden_ref, down_ref, *outs):
    part, width = outs[0].shape

    @pl.loop(0, width // DOWN_TILE, unroll=True)
    def _(step):
        at = pl.ds(pl.multiple_of(step * DOWN_TILE, DOWN_TILE), DOWN_TILE)
        there = pl.ds(pl.multiple_of(chunk * width + step * DOWN_TILE, DOWN_TILE), DOWN_TILE)
        total = jnp.dot(
            hidden_ref[...], down_ref[:, there], preferred_element_type=jnp.float32
        ).astype(jnp.bfloat16)
        for i, ref in enumerate(outs):
            ref[:, at] = total[i * part : (i + 1) * part]


def down(hidden, w_down, chunk, chunks):
    units, width = w_down.shape
    rows = hidden.shape[0]
    vmem = pl.BlockSpec(memory_space=pltpu.VMEM)
    return pl.pallas_call(
        functools.partial(down_kernel, chunk),
        out_shape=[jax.ShapeDtypeStruct((rows // 4, width // chunks), jnp.bfloat16)] * 4,
        in_specs=[vmem, vmem],
        out_specs=[vmem] * 4,
        compiler_params=pltpu.CompilerParams(vmem_limit_bytes=VMEM_LIMIT),
        cost_estimate=pl.CostEstimate(
            flops=2 * rows * units * width // chunks,
            bytes_accessed=2 * units * width // chunks,
            transcendentals=0,
        ),
        name="down",
    )(hidden, w_down)


CHIPS, PLACES = 2, 4


def to_core(value):
    return lax.ppermute(value, "node", [(i, i ^ 1) for i in range(2 * CHIPS)])


def to_chip(value):
    return lax.ppermute(value, "node", [(i, i ^ 2) for i in range(2 * CHIPS)])


def to_place(value, bits):
    return lax.ppermute(value, "local", [(i, i ^ bits) for i in range(PLACES)])


def to_both(value, bits):
    count = 2 * CHIPS * PLACES
    perm = [(i, i ^ (2 * PLACES + bits)) for i in range(count)]
    return lax.ppermute(value, ("node", "local"), perm)


def after(value, *others):
    return lax.optimization_barrier((value, *others))[0]


def gather_blocks(own):
    second, first, far_own = to_place(own, 2), to_place(own, 1), to_chip(own)
    far_first = to_chip(first)
    ready = after(second, far_own)
    far_second, third = to_chip(ready), to_place(ready, 1)
    far_third = to_both(after(ready, far_first), 1)
    early = stack(own, far_own, first, second)
    late = stack(far_first, third, far_second, far_third)
    return [early, late, to_core(early), to_core(late)]


def sums_kernel(*refs):
    inputs, outs = refs[: -PLACES], refs[-PLACES:]
    chunks = len(inputs) // 2
    rows, width = outs[0].shape
    for chunk in range(chunks):
        at = pl.ds(chunk * (width // chunks), width // chunks)
        here, other = [ref[...].astype(jnp.float32) for ref in inputs[chunk::chunks]]
        total = here + other
        for place, ref in enumerate(outs):
            ref[:, at] = total[place * rows : (place + 1) * rows].astype(ref.dtype)


def sums(here, other):
    rows, width = here[0].shape[0] // PLACES, here[0].shape[1] * len(here)
    vmem = pl.BlockSpec(memory_space=pltpu.VMEM)
    return pl.pallas_call(
        sums_kernel,
        out_shape=[jax.ShapeDtypeStruct((rows, width), here[0].dtype)] * PLACES,
        in_specs=[vmem] * (2 * len(here)),
        out_specs=[vmem] * PLACES,
        compiler_params=pltpu.CompilerParams(vmem_limit_bytes=VMEM_LIMIT),
        name="sums",
    )(*here, *other)


def total(*terms):
    return sum(term.astype(jnp.float32) for term in terms)


def reduce_blocks(chunks):
    early, late, other_early, other_late = zip(*chunks)
    other_late = [to_core(each) for each in other_late]
    other_early = [to_core(after(each, *other_late)) for each in other_early]
    far_first, third, far_second, far_third = sums(late, other_late)
    third, far_second = to_place(third, 1), to_chip(far_second)
    far_third, far_first = to_both(far_third, 1), to_chip(far_first)
    own, far_own, first, second = sums(early, other_early)
    first = total(first, far_first).astype(jnp.bfloat16)
    first_here = to_place(first, 1)
    far_own = to_chip(after(far_own, first_here))
    second = total(second, third, far_second, far_third).astype(jnp.bfloat16)
    return total(own, to_place(second, 2), first_here, far_own).astype(jnp.bfloat16)


def by_permutes(tokens, expert_ids, route_weights, expert_slot, w_gate, w_up, w_down):
    own = pack(tokens, expert_ids, route_weights, expert_slot, w_gate, w_up, w_down)
    hidden = hidden_units(gather_blocks(own), w_gate, w_up, expert_slot.shape[0])
    matrix = w_down.reshape(-1, w_down.shape[-1])
    chunks = []
    for chunk in range(OUT_CHUNKS):
        chunks.append(down(hidden, matrix, chunk, OUT_CHUNKS))
        hidden = after(hidden, chunks[-1][-1])
    return reduce_blocks(chunks)


def by_collectives(tokens, expert_ids, route_weights, expert_slot, w_gate, w_up, w_down):
    members, width, _ = w_gate.shape
    experts = expert_slot.shape[0]
    packed = pack(tokens, expert_ids, route_weights, expert_slot)
    gathered = lax.all_gather(packed, ("node", "local"), axis=0, tiled=True)
    rows = gathered[:, :width]
    tail = gathered[:, width : width + 3 * experts].astype(jnp.float32)
    weights = tail.reshape(-1, 3, experts).sum(axis=1)
    mine = lax.dynamic_slice_in_dim(weights, lax.axis_index("node") * members, members, axis=1)
    gate = jnp.einsum("td,edh->eth", rows, w_gate, preferred_element_type=jnp.float32)
    up = jnp.einsum("td,edh->eth", rows, w_up, preferred_element_type=jnp.float32)
    hidden = (jax.nn.silu(gate) * up * mine.T[..., None]).astype(jnp.bfloat16)
    result = jnp.einsum("eth,ehd->td", hidden, w_down, preferred_element_type=jnp.float32)
    return lax.psum_scatter(
        result.astype(jnp.bfloat16), ("node", "local"), scatter_dimension=0, tiled=True
    )


def per_device(*args):
    small = (lax.axis_size("node"), lax.axis_size("local")) == (2 * CHIPS, PLACES)
    return (by_permutes if small else by_collectives)(*args)


def solution(mesh):
    rows = P(("parts", "node", "local"), None)
    in_specs = (
        rows,
        rows,
        rows,
        P(),
        P("node", None, "local"),
        P("node", None, "local"),
        P("node", "local", None),
    )
    return jax.shard_map(
        per_device, mesh=mesh, in_specs=in_specs, out_specs=rows, check_vma=False
    )
```

```python
import functools

import jax
import jax.numpy as jnp
from jax import lax
from jax.experimental import pallas as pl
from jax.experimental.pallas import tpu as pltpu
from jax.sharding import PartitionSpec as P

LANES = 128
N_TILE = 256
DOWN_TILE = 1792
OUT_CHUNKS = 1
VMEM_LIMIT = 4 * 2**20


def pack_kernel(*refs):
    inputs, out_ref, local, sems = refs[:4], refs[-6], refs[-5:-1], refs[-1]
    copies = [
        pltpu.make_async_copy(here, there, sems.at[i])
        for i, (here, there) in enumerate(zip(inputs, local))
    ]
    for copy in copies:
        copy.start()
    for copy in copies:
        copy.wait()
    tokens_ref, ids_ref, route_ref, slot_ref = local
    rows, width = tokens_ref.shape
    experts = slot_ref.shape[0]
    row = lax.broadcasted_iota(jnp.int32, (rows, LANES), 0)
    column = lax.broadcasted_iota(jnp.int32, (rows, LANES), 1)
    slot = lax.rem(column, experts)
    weights = jnp.zeros((rows, LANES), jnp.float32)
    for k in range(ids_ref.shape[0]):
        for token in range(rows):
            named = (row == token) & (slot == slot_ref[ids_ref[k, token]])
            weights = jnp.where(named, route_ref[k, token], weights)
    first = weights.astype(jnp.bfloat16).astype(jnp.float32)
    second = (weights - first).astype(jnp.bfloat16).astype(jnp.float32)
    third = weights - first - second
    tail = jnp.where(column < experts, first, jnp.where(column < 2 * experts, second, third))
    out_ref[:, :width] = tokens_ref[...]
    out_ref[:, width:] = jnp.where(column < 3 * experts, tail, 0.0).astype(jnp.bfloat16)


def pack(tokens, expert_ids, route_weights, expert_slot, *weights):
    rows, width = tokens.shape
    inputs = (tokens, expert_ids.T, route_weights.T, expert_slot)
    held = [pltpu.with_memory_space_constraint(each, pltpu.HBM) for each in inputs + weights]
    return pl.pallas_call(
        pack_kernel,
        out_shape=jax.ShapeDtypeStruct((rows, width + LANES), jnp.bfloat16),
        in_specs=[pl.BlockSpec(memory_space=pl.ANY)] * len(held),
        out_specs=pl.BlockSpec(memory_space=pltpu.VMEM),
        scratch_shapes=[
            pltpu.VMEM(tokens.shape, tokens.dtype),
            *[pltpu.SMEM(each.shape, each.dtype) for each in inputs[1:]],
            pltpu.SemaphoreType.DMA((len(inputs),)),
        ],
        compiler_params=pltpu.CompilerParams(vmem_limit_bytes=VMEM_LIMIT),
        name="pack",
    )(*held)


def stack_kernel(*refs):
    *pieces, out_ref = refs
    out_ref[...] = jnp.concatenate([piece[...] for piece in pieces], axis=0)


def stack(*pieces):
    rows = sum(piece.shape[0] for piece in pieces)
    vmem = pl.BlockSpec(memory_space=pltpu.VMEM)
    return pl.pallas_call(
        stack_kernel,
        out_shape=jax.ShapeDtypeStruct((rows, pieces[0].shape[1]), pieces[0].dtype),
        in_specs=[vmem] * len(pieces),
        out_specs=vmem,
        compiler_params=pltpu.CompilerParams(vmem_limit_bytes=VMEM_LIMIT),
        name="stack",
    )(*pieces)


def hidden_kernel(experts, *refs):
    *pieces, gate_ref, up_ref, out_ref, x_ref, weight_ref = refs
    members, width, hid = gate_ref.shape
    x_ref[...] = jnp.concatenate([piece[:, :width] for piece in pieces], axis=0)
    tail = jnp.concatenate([piece[:, width:] for piece in pieces], axis=0)
    tail = tail.astype(jnp.float32)
    column = lax.broadcasted_iota(jnp.int32, tail.shape, 1)
    for member in range(members):
        slot = lax.axis_index("node") * members + member
        mine = (lax.rem(column, experts) == slot) & (column < 3 * experts)
        weight_ref[member] = jnp.sum(jnp.where(mine, tail, 0.0), axis=1, keepdims=True)
    tiles = hid // N_TILE

    @pl.loop(0, members * tiles, unroll=True)
    def _(step):
        member = step // tiles
        at = pl.ds(pl.multiple_of(lax.rem(step, tiles) * N_TILE, N_TILE), N_TILE)
        gate, up = [
            jnp.dot(x_ref[...], ref[member, :, at], preferred_element_type=jnp.float32)
            for ref in (gate_ref, up_ref)
        ]
        hidden = gate / (1.0 + jnp.exp(-gate)) * up * weight_ref[member]
        to = pl.ds(pl.multiple_of(step * N_TILE, N_TILE), N_TILE)
        out_ref[:, to] = hidden.astype(jnp.bfloat16)


def hidden_units(pieces, w_gate, w_up, experts):
    members, width, hid = w_gate.shape
    rows = sum(piece.shape[0] for piece in pieces)
    vmem = pl.BlockSpec(memory_space=pltpu.VMEM)
    return pl.pallas_call(
        functools.partial(hidden_kernel, experts),
        out_shape=jax.ShapeDtypeStruct((rows, members * hid), jnp.bfloat16),
        in_specs=[vmem] * (len(pieces) + 2),
        out_specs=vmem,
        scratch_shapes=[
            pltpu.VMEM((rows, width), jnp.bfloat16),
            pltpu.VMEM((members, rows, 1), jnp.float32),
        ],
        compiler_params=pltpu.CompilerParams(vmem_limit_bytes=VMEM_LIMIT),
        cost_estimate=pl.CostEstimate(
            flops=4 * rows * members * width * hid,
            bytes_accessed=4 * members * width * hid,
            transcendentals=rows * members * hid,
        ),
        name="hidden",
    )(*pieces, w_gate, w_up)


def down_kernel(chunk, hidden_ref, down_ref, *outs):
    part, width = outs[0].shape

    @pl.loop(0, width // DOWN_TILE, unroll=True)
    def _(step):
        at = pl.ds(pl.multiple_of(step * DOWN_TILE, DOWN_TILE), DOWN_TILE)
        there = pl.ds(pl.multiple_of(chunk * width + step * DOWN_TILE, DOWN_TILE), DOWN_TILE)
        total = jnp.dot(
            hidden_ref[...], down_ref[:, there], preferred_element_type=jnp.float32
        ).astype(jnp.bfloat16)
        for i, ref in enumerate(outs):
            ref[:, at] = total[i * part : (i + 1) * part]


def down(hidden, w_down, chunk, chunks):
    units, width = w_down.shape
    rows = hidden.shape[0]
    vmem = pl.BlockSpec(memory_space=pltpu.VMEM)
    return pl.pallas_call(
        functools.partial(down_kernel, chunk),
        out_shape=[jax.ShapeDtypeStruct((rows // 4, width // chunks), jnp.bfloat16)] * 4,
        in_specs=[vmem, vmem],
        out_specs=[vmem] * 4,
        compiler_params=pltpu.CompilerParams(vmem_limit_bytes=VMEM_LIMIT),
        cost_estimate=pl.CostEstimate(
            flops=2 * rows * units * width // chunks,
            bytes_accessed=2 * units * width // chunks,
            transcendentals=0,
        ),
        name="down",
    )(hidden, w_down)


CHIPS, PLACES = 2, 4


def to_core(value):
    return lax.ppermute(value, "node", [(i, i ^ 1) for i in range(2 * CHIPS)])


def to_chip(value):
    return lax.ppermute(value, "node", [(i, i ^ 2) for i in range(2 * CHIPS)])


def to_place(value, bits):
    return lax.ppermute(value, "local", [(i, i ^ bits) for i in range(PLACES)])


def to_both(value, bits):
    count = 2 * CHIPS * PLACES
    perm = [(i, i ^ (2 * PLACES + bits)) for i in range(count)]
    return lax.ppermute(value, ("node", "local"), perm)


def after(value, *others):
    return lax.optimization_barrier((value, *others))[0]


def gather_blocks(own):
    second, first, far_own = to_place(own, 2), to_place(own, 1), to_chip(own)
    far_first = to_both(own, 1)
    far_second, third = to_chip(second), to_place(second, 1)
    far_third = to_both(after(second, first), 1)
    early = stack(own, far_own, first, second)
    late = stack(far_first, third, far_second, far_third)
    return [early, late, to_core(early), to_core(late)]


def sums_kernel(*refs):
    inputs, outs = refs[: -PLACES], refs[-PLACES:]
    chunks = len(inputs) // 2
    rows, width = outs[0].shape
    for chunk in range(chunks):
        at = pl.ds(chunk * (width // chunks), width // chunks)
        here, other = [ref[...].astype(jnp.float32) for ref in inputs[chunk::chunks]]
        total = here + other
        for place, ref in enumerate(outs):
            ref[:, at] = total[place * rows : (place + 1) * rows].astype(ref.dtype)


def sums(here, other):
    rows, width = here[0].shape[0] // PLACES, here[0].shape[1] * len(here)
    vmem = pl.BlockSpec(memory_space=pltpu.VMEM)
    return pl.pallas_call(
        sums_kernel,
        out_shape=[jax.ShapeDtypeStruct((rows, width), here[0].dtype)] * PLACES,
        in_specs=[vmem] * (2 * len(here)),
        out_specs=[vmem] * PLACES,
        compiler_params=pltpu.CompilerParams(vmem_limit_bytes=VMEM_LIMIT),
        name="sums",
    )(*here, *other)


def total(*terms):
    return sum(term.astype(jnp.float32) for term in terms)


def reduce_blocks(chunks):
    early, late, other_early, other_late = zip(*chunks)
    other_late = [to_core(each) for each in other_late]
    other_early = [to_core(after(each, *other_late)) for each in other_early]
    far_first, third, far_second, far_third = sums(late, other_late)
    third, far_second = to_place(third, 1), to_chip(far_second)
    far_third, far_first = to_both(far_third, 1), to_chip(far_first)
    own, far_own, first, second = sums(early, other_early)
    first = total(first, far_first).astype(jnp.bfloat16)
    first_here = to_place(first, 1)
    far_own = to_chip(after(far_own, first_here))
    second = total(second, third, far_second, far_third).astype(jnp.bfloat16)
    return total(own, to_place(second, 2), first_here, far_own).astype(jnp.bfloat16)


def by_permutes(tokens, expert_ids, route_weights, expert_slot, w_gate, w_up, w_down):
    own = pack(tokens, expert_ids, route_weights, expert_slot, w_gate, w_up, w_down)
    hidden = hidden_units(gather_blocks(own), w_gate, w_up, expert_slot.shape[0])
    matrix = w_down.reshape(-1, w_down.shape[-1])
    chunks = []
    for chunk in range(OUT_CHUNKS):
        chunks.append(down(hidden, matrix, chunk, OUT_CHUNKS))
        hidden = after(hidden, chunks[-1][-1])
    return reduce_blocks(chunks)


def by_collectives(tokens, expert_ids, route_weights, expert_slot, w_gate, w_up, w_down):
    members, width, _ = w_gate.shape
    experts = expert_slot.shape[0]
    packed = pack(tokens, expert_ids, route_weights, expert_slot)
    gathered = lax.all_gather(packed, ("node", "local"), axis=0, tiled=True)
    rows = gathered[:, :width]
    tail = gathered[:, width : width + 3 * experts].astype(jnp.float32)
    weights = tail.reshape(-1, 3, experts).sum(axis=1)
    mine = lax.dynamic_slice_in_dim(weights, lax.axis_index("node") * members, members, axis=1)
    gate = jnp.einsum("td,edh->eth", rows, w_gate, preferred_element_type=jnp.float32)
    up = jnp.einsum("td,edh->eth", rows, w_up, preferred_element_type=jnp.float32)
    hidden = (jax.nn.silu(gate) * up * mine.T[..., None]).astype(jnp.bfloat16)
    result = jnp.einsum("eth,ehd->td", hidden, w_down, preferred_element_type=jnp.float32)
    return lax.psum_scatter(
        result.astype(jnp.bfloat16), ("node", "local"), scatter_dimension=0, tiled=True
    )


def per_device(*args):
    small = (lax.axis_size("node"), lax.axis_size("local")) == (2 * CHIPS, PLACES)
    return (by_permutes if small else by_collectives)(*args)


def solution(mesh):
    rows = P(("parts", "node", "local"), None)
    in_specs = (
        rows,
        rows,
        rows,
        P(),
        P("node", None, "local"),
        P("node", None, "local"),
        P("node", "local", None),
    )
    return jax.shard_map(
        per_device, mesh=mesh, in_specs=in_specs, out_specs=rows, check_vma=False
    )
```

```python
import functools

import jax
import jax.numpy as jnp
from jax import lax
from jax.experimental import pallas as pl
from jax.experimental.pallas import tpu as pltpu
from jax.sharding import PartitionSpec as P

LANES = 128
N_TILE = 256
DOWN_TILE = 1792
OUT_CHUNKS = 1
VMEM_LIMIT = 4 * 2**20


def pack_kernel(*refs):
    inputs, out_ref, local, sems = refs[:4], refs[-6], refs[-5:-1], refs[-1]
    copies = [
        pltpu.make_async_copy(here, there, sems.at[i])
        for i, (here, there) in enumerate(zip(inputs, local))
    ]
    for copy in copies:
        copy.start()
    for copy in copies[1:]:
        copy.wait()
    tokens_ref, ids_ref, route_ref, slot_ref = local
    rows, width = tokens_ref.shape
    experts = slot_ref.shape[0]
    row = lax.broadcasted_iota(jnp.int32, (rows, LANES), 0)
    column = lax.broadcasted_iota(jnp.int32, (rows, LANES), 1)
    slot = lax.rem(column, experts)
    weights = jnp.zeros((rows, LANES), jnp.float32)
    for k in range(ids_ref.shape[0]):
        for token in range(rows):
            named = (row == token) & (slot == slot_ref[ids_ref[k, token]])
            weights = jnp.where(named, route_ref[k, token], weights)
    first = weights.astype(jnp.bfloat16).astype(jnp.float32)
    second = (weights - first).astype(jnp.bfloat16).astype(jnp.float32)
    third = weights - first - second
    tail = jnp.where(column < experts, first, jnp.where(column < 2 * experts, second, third))
    copies[0].wait()
    out_ref[:, :width] = tokens_ref[...]
    out_ref[:, width:] = jnp.where(column < 3 * experts, tail, 0.0).astype(jnp.bfloat16)


def pack(tokens, expert_ids, route_weights, expert_slot, *weights):
    rows, width = tokens.shape
    inputs = (tokens, expert_ids.T, route_weights.T, expert_slot)
    held = [pltpu.with_memory_space_constraint(each, pltpu.HBM) for each in inputs + weights]
    return pl.pallas_call(
        pack_kernel,
        out_shape=jax.ShapeDtypeStruct((rows, width + LANES), jnp.bfloat16),
        in_specs=[pl.BlockSpec(memory_space=pl.ANY)] * len(held),
        out_specs=pl.BlockSpec(memory_space=pltpu.VMEM),
        scratch_shapes=[
            pltpu.VMEM(tokens.shape, tokens.dtype),
            *[pltpu.SMEM(each.shape, each.dtype) for each in inputs[1:]],
            pltpu.SemaphoreType.DMA((len(inputs),)),
        ],
        compiler_params=pltpu.CompilerParams(vmem_limit_bytes=VMEM_LIMIT),
        name="pack",
    )(*held)


def stack_kernel(*refs):
    *pieces, out_ref = refs
    out_ref[...] = jnp.concatenate([piece[...] for piece in pieces], axis=0)


def stack(*pieces):
    rows = sum(piece.shape[0] for piece in pieces)
    vmem = pl.BlockSpec(memory_space=pltpu.VMEM)
    return pl.pallas_call(
        stack_kernel,
        out_shape=jax.ShapeDtypeStruct((rows, pieces[0].shape[1]), pieces[0].dtype),
        in_specs=[vmem] * len(pieces),
        out_specs=vmem,
        compiler_params=pltpu.CompilerParams(vmem_limit_bytes=VMEM_LIMIT),
        name="stack",
    )(*pieces)


def hidden_kernel(experts, *refs):
    *pieces, gate_ref, up_ref, out_ref, x_ref, weight_ref = refs
    members, width, hid = gate_ref.shape
    x_ref[...] = jnp.concatenate([piece[:, :width] for piece in pieces], axis=0)
    tail = jnp.concatenate([piece[:, width:] for piece in pieces], axis=0)
    tail = tail.astype(jnp.float32)
    column = lax.broadcasted_iota(jnp.int32, tail.shape, 1)
    for member in range(members):
        slot = lax.axis_index("node") * members + member
        mine = (lax.rem(column, experts) == slot) & (column < 3 * experts)
        weight_ref[member] = jnp.sum(jnp.where(mine, tail, 0.0), axis=1, keepdims=True)
    tiles = hid // N_TILE

    @pl.loop(0, members * tiles, unroll=True)
    def _(step):
        member = step // tiles
        at = pl.ds(pl.multiple_of(lax.rem(step, tiles) * N_TILE, N_TILE), N_TILE)
        gate, up = [
            jnp.dot(x_ref[...], ref[member, :, at], preferred_element_type=jnp.float32)
            for ref in (gate_ref, up_ref)
        ]
        hidden = gate / (1.0 + jnp.exp(-gate)) * up * weight_ref[member]
        to = pl.ds(pl.multiple_of(step * N_TILE, N_TILE), N_TILE)
        out_ref[:, to] = hidden.astype(jnp.bfloat16)


def hidden_units(pieces, w_gate, w_up, experts):
    members, width, hid = w_gate.shape
    rows = sum(piece.shape[0] for piece in pieces)
    vmem = pl.BlockSpec(memory_space=pltpu.VMEM)
    return pl.pallas_call(
        functools.partial(hidden_kernel, experts),
        out_shape=jax.ShapeDtypeStruct((rows, members * hid), jnp.bfloat16),
        in_specs=[vmem] * (len(pieces) + 2),
        out_specs=vmem,
        scratch_shapes=[
            pltpu.VMEM((rows, width), jnp.bfloat16),
            pltpu.VMEM((members, rows, 1), jnp.float32),
        ],
        compiler_params=pltpu.CompilerParams(vmem_limit_bytes=VMEM_LIMIT),
        cost_estimate=pl.CostEstimate(
            flops=4 * rows * members * width * hid,
            bytes_accessed=4 * members * width * hid,
            transcendentals=rows * members * hid,
        ),
        name="hidden",
    )(*pieces, w_gate, w_up)


def down_kernel(chunk, hidden_ref, down_ref, *outs):
    part, width = outs[0].shape

    @pl.loop(0, width // DOWN_TILE, unroll=True)
    def _(step):
        at = pl.ds(pl.multiple_of(step * DOWN_TILE, DOWN_TILE), DOWN_TILE)
        there = pl.ds(pl.multiple_of(chunk * width + step * DOWN_TILE, DOWN_TILE), DOWN_TILE)
        total = jnp.dot(
            hidden_ref[...], down_ref[:, there], preferred_element_type=jnp.float32
        ).astype(jnp.bfloat16)
        for i, ref in enumerate(outs):
            ref[:, at] = total[i * part : (i + 1) * part]


def down(hidden, w_down, chunk, chunks):
    units, width = w_down.shape
    rows = hidden.shape[0]
    vmem = pl.BlockSpec(memory_space=pltpu.VMEM)
    return pl.pallas_call(
        functools.partial(down_kernel, chunk),
        out_shape=[jax.ShapeDtypeStruct((rows // 4, width // chunks), jnp.bfloat16)] * 4,
        in_specs=[vmem, vmem],
        out_specs=[vmem] * 4,
        compiler_params=pltpu.CompilerParams(vmem_limit_bytes=VMEM_LIMIT),
        cost_estimate=pl.CostEstimate(
            flops=2 * rows * units * width // chunks,
            bytes_accessed=2 * units * width // chunks,
            transcendentals=0,
        ),
        name="down",
    )(hidden, w_down)


CHIPS, PLACES = 2, 4


def to_core(value):
    return lax.ppermute(value, "node", [(i, i ^ 1) for i in range(2 * CHIPS)])


def to_chip(value):
    return lax.ppermute(value, "node", [(i, i ^ 2) for i in range(2 * CHIPS)])


def to_place(value, bits):
    return lax.ppermute(value, "local", [(i, i ^ bits) for i in range(PLACES)])


def to_both(value, bits):
    count = 2 * CHIPS * PLACES
    perm = [(i, i ^ (2 * PLACES + bits)) for i in range(count)]
    return lax.ppermute(value, ("node", "local"), perm)


def after(value, *others):
    return lax.optimization_barrier((value, *others))[0]


def gather_blocks(own):
    second, first, far_own = to_place(own, 2), to_place(own, 1), to_chip(own)
    far_first = to_chip(first)
    ready = after(second, far_own)
    far_second, third = to_chip(ready), to_place(ready, 1)
    far_third = to_both(after(ready, far_first), 1)
    early = stack(own, far_own, first, far_first)
    late = stack(second, third, far_second, far_third)
    return [early, late, to_core(early), to_core(late)]


def sums_kernel(*refs):
    inputs, outs = refs[: -PLACES], refs[-PLACES:]
    chunks = len(inputs) // 2
    rows, width = outs[0].shape
    for chunk in range(chunks):
        at = pl.ds(chunk * (width // chunks), width // chunks)
        here, other = [ref[...].astype(jnp.float32) for ref in inputs[chunk::chunks]]
        total = here + other
        for place, ref in enumerate(outs):
            ref[:, at] = total[place * rows : (place + 1) * rows].astype(ref.dtype)


def sums(here, other):
    rows, width = here[0].shape[0] // PLACES, here[0].shape[1] * len(here)
    vmem = pl.BlockSpec(memory_space=pltpu.VMEM)
    return pl.pallas_call(
        sums_kernel,
        out_shape=[jax.ShapeDtypeStruct((rows, width), here[0].dtype)] * PLACES,
        in_specs=[vmem] * (2 * len(here)),
        out_specs=[vmem] * PLACES,
        compiler_params=pltpu.CompilerParams(vmem_limit_bytes=VMEM_LIMIT),
        name="sums",
    )(*here, *other)


def total(*terms):
    return sum(term.astype(jnp.float32) for term in terms)


def reduce_blocks(chunks):
    early, late, other_early, other_late = zip(*chunks)
    other_late = [to_core(each) for each in other_late]
    other_early = [to_core(after(each, *other_late)) for each in other_early]
    second, third, far_second, far_third = sums(late, other_late)
    far_second = to_chip(far_second)
    far_third = to_both(far_third, 1)
    third = to_place(third, 1)
    second = total(second, far_second, far_third, third).astype(jnp.bfloat16)
    own, far_own, first, far_first = sums(early, other_early)
    first = total(first, to_chip(after(far_first, far_second))).astype(jnp.bfloat16)
    first, far_own = lax.optimization_barrier((first, far_own))
    second_here, first_here, far_own = to_place(second, 2), to_place(first, 1), to_chip(far_own)
    return total(own, second_here, first_here, far_own).astype(jnp.bfloat16)


def by_permutes(tokens, expert_ids, route_weights, expert_slot, w_gate, w_up, w_down):
    own = pack(tokens, expert_ids, route_weights, expert_slot, w_gate, w_up, w_down)
    hidden = hidden_units(gather_blocks(own), w_gate, w_up, expert_slot.shape[0])
    matrix = w_down.reshape(-1, w_down.shape[-1])
    chunks = []
    for chunk in range(OUT_CHUNKS):
        chunks.append(down(hidden, matrix, chunk, OUT_CHUNKS))
        hidden = after(hidden, chunks[-1][-1])
    return reduce_blocks(chunks)


def by_collectives(tokens, expert_ids, route_weights, expert_slot, w_gate, w_up, w_down):
    members, width, _ = w_gate.shape
    experts = expert_slot.shape[0]
    packed = pack(tokens, expert_ids, route_weights, expert_slot)
    gathered = lax.all_gather(packed, ("node", "local"), axis=0, tiled=True)
    rows = gathered[:, :width]
    tail = gathered[:, width : width + 3 * experts].astype(jnp.float32)
    weights = tail.reshape(-1, 3, experts).sum(axis=1)
    mine = lax.dynamic_slice_in_dim(weights, lax.axis_index("node") * members, members, axis=1)
    gate = jnp.einsum("td,edh->eth", rows, w_gate, preferred_element_type=jnp.float32)
    up = jnp.einsum("td,edh->eth", rows, w_up, preferred_element_type=jnp.float32)
    hidden = (jax.nn.silu(gate) * up * mine.T[..., None]).astype(jnp.bfloat16)
    result = jnp.einsum("eth,ehd->td", hidden, w_down, preferred_element_type=jnp.float32)
    return lax.psum_scatter(
        result.astype(jnp.bfloat16), ("node", "local"), scatter_dimension=0, tiled=True
    )


def per_device(*args):
    small = (lax.axis_size("node"), lax.axis_size("local")) == (2 * CHIPS, PLACES)
    return (by_permutes if small else by_collectives)(*args)


def solution(mesh):
    rows = P(("parts", "node", "local"), None)
    in_specs = (
        rows,
        rows,
        rows,
        P(),
        P("node", None, "local"),
        P("node", None, "local"),
        P("node", "local", None),
    )
    return jax.shard_map(
        per_device, mesh=mesh, in_specs=in_specs, out_specs=rows, check_vma=False
    )
```

```python
import functools

import jax
import jax.numpy as jnp
from jax import lax
from jax.experimental import pallas as pl
from jax.experimental.pallas import tpu as pltpu
from jax.sharding import PartitionSpec as P

LANES = 128
N_TILE = 256
DOWN_TILE = 1792
VMEM_LIMIT = 4 * 2**20


def pack_kernel(*refs):
    inputs, out_ref, local, sems = refs[:4], refs[-6], refs[-5:-1], refs[-1]
    copies = [
        pltpu.make_async_copy(here, there, sems.at[i])
        for i, (here, there) in enumerate(zip(inputs, local))
    ]
    for copy in copies:
        copy.start()
    for copy in copies[1:]:
        copy.wait()
    tokens_ref, ids_ref, route_ref, slot_ref = local
    rows, width = tokens_ref.shape
    experts = slot_ref.shape[0]
    row = lax.broadcasted_iota(jnp.int32, (rows, LANES), 0)
    column = lax.broadcasted_iota(jnp.int32, (rows, LANES), 1)
    slot = lax.rem(column, experts)
    weights = jnp.zeros((rows, LANES), jnp.float32)
    for k in range(ids_ref.shape[0]):
        for token in range(rows):
            named = (row == token) & (slot == slot_ref[ids_ref[k, token]])
            weights = jnp.where(named, route_ref[k, token], weights)
    first = weights.astype(jnp.bfloat16).astype(jnp.float32)
    second = (weights - first).astype(jnp.bfloat16).astype(jnp.float32)
    third = weights - first - second
    tail = jnp.where(column < experts, first, jnp.where(column < 2 * experts, second, third))
    copies[0].wait()
    out_ref[:, :width] = tokens_ref[...]
    out_ref[:, width:] = jnp.where(column < 3 * experts, tail, 0.0).astype(jnp.bfloat16)


def pack(tokens, expert_ids, route_weights, expert_slot, *weights):
    rows, width = tokens.shape
    inputs = (tokens, expert_ids.T, route_weights.T, expert_slot)
    held = [pltpu.with_memory_space_constraint(each, pltpu.HBM) for each in inputs + weights]
    return pl.pallas_call(
        pack_kernel,
        out_shape=jax.ShapeDtypeStruct((rows, width + LANES), jnp.bfloat16),
        in_specs=[pl.BlockSpec(memory_space=pl.ANY)] * len(held),
        out_specs=pl.BlockSpec(memory_space=pltpu.VMEM),
        scratch_shapes=[
            pltpu.VMEM(tokens.shape, tokens.dtype),
            *[pltpu.SMEM(each.shape, each.dtype) for each in inputs[1:]],
            pltpu.SemaphoreType.DMA((len(inputs),)),
        ],
        compiler_params=pltpu.CompilerParams(vmem_limit_bytes=VMEM_LIMIT),
        name="pack",
    )(*held)


def stack_kernel(*refs):
    *pieces, out_ref = refs
    out_ref[...] = jnp.concatenate([piece[...] for piece in pieces], axis=0)


def stack(*pieces):
    rows = sum(piece.shape[0] for piece in pieces)
    vmem = pl.BlockSpec(memory_space=pltpu.VMEM)
    return pl.pallas_call(
        stack_kernel,
        out_shape=jax.ShapeDtypeStruct((rows, pieces[0].shape[1]), pieces[0].dtype),
        in_specs=[vmem] * len(pieces),
        out_specs=vmem,
        compiler_params=pltpu.CompilerParams(vmem_limit_bytes=VMEM_LIMIT),
        name="stack",
    )(*pieces)


def hidden_kernel(experts, *refs):
    *pieces, gate_ref, up_ref, out_ref, x_ref, weight_ref = refs
    members, width, hid = gate_ref.shape
    x_ref[...] = jnp.concatenate([piece[:, :width] for piece in pieces], axis=0)
    tail = jnp.concatenate([piece[:, width:] for piece in pieces], axis=0)
    tail = tail.astype(jnp.float32)
    column = lax.broadcasted_iota(jnp.int32, tail.shape, 1)
    for member in range(members):
        slot = lax.axis_index("node") * members + member
        mine = (lax.rem(column, experts) == slot) & (column < 3 * experts)
        weight_ref[member] = jnp.sum(jnp.where(mine, tail, 0.0), axis=1, keepdims=True)
    tiles = hid // N_TILE

    @pl.loop(0, members * tiles, unroll=True)
    def _(step):
        member = step // tiles
        at = pl.ds(pl.multiple_of(lax.rem(step, tiles) * N_TILE, N_TILE), N_TILE)
        gate, up = [
            jnp.dot(x_ref[...], ref[member, :, at], preferred_element_type=jnp.float32)
            for ref in (gate_ref, up_ref)
        ]
        hidden = gate / (1.0 + jnp.exp(-gate)) * up * weight_ref[member]
        to = pl.ds(pl.multiple_of(step * N_TILE, N_TILE), N_TILE)
        out_ref[:, to] = hidden.astype(jnp.bfloat16)


def hidden_units(pieces, w_gate, w_up, experts):
    members, width, hid = w_gate.shape
    rows = sum(piece.shape[0] for piece in pieces)
    vmem = pl.BlockSpec(memory_space=pltpu.VMEM)
    return pl.pallas_call(
        functools.partial(hidden_kernel, experts),
        out_shape=jax.ShapeDtypeStruct((rows, members * hid), jnp.bfloat16),
        in_specs=[vmem] * (len(pieces) + 2),
        out_specs=vmem,
        scratch_shapes=[
            pltpu.VMEM((rows, width), jnp.bfloat16),
            pltpu.VMEM((members, rows, 1), jnp.float32),
        ],
        compiler_params=pltpu.CompilerParams(vmem_limit_bytes=VMEM_LIMIT),
        cost_estimate=pl.CostEstimate(
            flops=4 * rows * members * width * hid,
            bytes_accessed=4 * members * width * hid,
            transcendentals=rows * members * hid,
        ),
        name="hidden",
    )(*pieces, w_gate, w_up)


def down_kernel(hidden_ref, down_ref, *outs):
    width = down_ref.shape[1]

    @pl.loop(0, width // DOWN_TILE, unroll=True)
    def _(step):
        at = pl.ds(pl.multiple_of(step * DOWN_TILE, DOWN_TILE), DOWN_TILE)
        total = jnp.dot(hidden_ref[...], down_ref[:, at], preferred_element_type=jnp.float32)
        start = 0
        for ref in outs:
            ref[:, at] = total[start : start + ref.shape[0]].astype(ref.dtype)
            start += ref.shape[0]


def down(hidden, w_down, groups):
    units, width = w_down.shape
    rows = hidden.shape[0]
    vmem = pl.BlockSpec(memory_space=pltpu.VMEM)
    return pl.pallas_call(
        down_kernel,
        out_shape=[jax.ShapeDtypeStruct((size, width), jnp.bfloat16) for size in groups],
        in_specs=[vmem, vmem],
        out_specs=[vmem] * len(groups),
        compiler_params=pltpu.CompilerParams(vmem_limit_bytes=VMEM_LIMIT),
        cost_estimate=pl.CostEstimate(
            flops=2 * rows * units * width,
            bytes_accessed=2 * units * width,
            transcendentals=0,
        ),
        name="down",
    )(hidden, w_down)


CHIPS, PLACES = 2, 4
EARLY, LATE = 5, 3


def to_core(value):
    return lax.ppermute(value, "node", [(i, i ^ 1) for i in range(2 * CHIPS)])


def to_chip(value):
    return lax.ppermute(value, "node", [(i, i ^ 2) for i in range(2 * CHIPS)])


def to_place(value, bits):
    return lax.ppermute(value, "local", [(i, i ^ bits) for i in range(PLACES)])


def to_both(value, bits):
    count = 2 * CHIPS * PLACES
    perm = [(i, i ^ (2 * PLACES + bits)) for i in range(count)]
    return lax.ppermute(value, ("node", "local"), perm)


def after(value, *others):
    return lax.optimization_barrier((value, *others))[0]


def gather_blocks(own):
    second, first, far_own = to_place(own, 2), to_place(own, 1), to_chip(own)
    far_first = to_chip(first)
    ready = after(second, far_own)
    far_second, third = to_chip(ready), to_place(ready, 1)
    far_third = to_both(after(ready, far_first), 1)
    early = stack(own, far_own, first, far_first)
    late = stack(second, third, far_second, far_third)
    return [early, late, to_core(early), to_core(late)]


def sums_kernel(here_ref, other_ref, *outs):
    total = here_ref[...].astype(jnp.float32) + other_ref[...].astype(jnp.float32)
    rows = outs[0].shape[0]
    for i, ref in enumerate(outs):
        ref[...] = total[i * rows : (i + 1) * rows].astype(ref.dtype)


def sums(here, other, blocks):
    vmem = pl.BlockSpec(memory_space=pltpu.VMEM)
    block = jax.ShapeDtypeStruct((here.shape[0] // blocks, here.shape[1]), here.dtype)
    return pl.pallas_call(
        sums_kernel,
        out_shape=[block] * blocks,
        in_specs=[vmem, vmem],
        out_specs=[vmem] * blocks,
        compiler_params=pltpu.CompilerParams(vmem_limit_bytes=VMEM_LIMIT),
        name="sums",
    )(here, other)


def total(*terms):
    return sum(term.astype(jnp.float32) for term in terms)


def reduce_blocks(early, late, other_early, other_late):
    other_late = to_core(other_late)
    other_early = to_core(after(other_early, other_late))
    third, far_second, far_third = sums(late, other_late, LATE)
    far_second = to_chip(far_second)
    far_third = to_both(far_third, 1)
    third = to_place(third, 1)
    own, far_own, first, far_first, second = sums(early, other_early, EARLY)
    second = total(second, far_second, far_third, third).astype(jnp.bfloat16)
    first = total(first, to_chip(after(far_first, third))).astype(jnp.bfloat16)
    first, far_own = lax.optimization_barrier((first, far_own))
    second_here, first_here, far_own = to_place(second, 2), to_place(first, 1), to_chip(far_own)
    return total(own, second_here, first_here, far_own).astype(jnp.bfloat16)


def by_permutes(tokens, expert_ids, route_weights, expert_slot, w_gate, w_up, w_down):
    own = pack(tokens, expert_ids, route_weights, expert_slot, w_gate, w_up, w_down)
    hidden = hidden_units(gather_blocks(own), w_gate, w_up, expert_slot.shape[0])
    matrix = w_down.reshape(-1, w_down.shape[-1])
    rows = tokens.shape[0]
    groups = (EARLY * rows, LATE * rows) * 2
    return reduce_blocks(*down(hidden, matrix, groups))


def by_collectives(tokens, expert_ids, route_weights, expert_slot, w_gate, w_up, w_down):
    members, width, _ = w_gate.shape
    experts = expert_slot.shape[0]
    packed = pack(tokens, expert_ids, route_weights, expert_slot)
    gathered = lax.all_gather(packed, ("node", "local"), axis=0, tiled=True)
    rows = gathered[:, :width]
    tail = gathered[:, width : width + 3 * experts].astype(jnp.float32)
    weights = tail.reshape(-1, 3, experts).sum(axis=1)
    mine = lax.dynamic_slice_in_dim(weights, lax.axis_index("node") * members, members, axis=1)
    gate = jnp.einsum("td,edh->eth", rows, w_gate, preferred_element_type=jnp.float32)
    up = jnp.einsum("td,edh->eth", rows, w_up, preferred_element_type=jnp.float32)
    hidden = (jax.nn.silu(gate) * up * mine.T[..., None]).astype(jnp.bfloat16)
    result = jnp.einsum("eth,ehd->td", hidden, w_down, preferred_element_type=jnp.float32)
    return lax.psum_scatter(
        result.astype(jnp.bfloat16), ("node", "local"), scatter_dimension=0, tiled=True
    )


def per_device(*args):
    small = (lax.axis_size("node"), lax.axis_size("local")) == (2 * CHIPS, PLACES)
    return (by_permutes if small else by_collectives)(*args)


def solution(mesh):
    rows = P(("parts", "node", "local"), None)
    in_specs = (
        rows,
        rows,
        rows,
        P(),
        P("node", None, "local"),
        P("node", None, "local"),
        P("node", "local", None),
    )
    return jax.shard_map(
        per_device, mesh=mesh, in_specs=in_specs, out_specs=rows, check_vma=False
    )
```

```python
import functools

import jax
import jax.numpy as jnp
from jax import lax
from jax.experimental import pallas as pl
from jax.experimental.pallas import tpu as pltpu
from jax.sharding import PartitionSpec as P

LANES = 128
N_TILE = 256
DOWN_TILE = 1792
OUT_CHUNKS = 1
VMEM_LIMIT = 4 * 2**20


def pack_kernel(*refs):
    inputs, out_ref, local, sems = refs[:4], refs[-6], refs[-5:-1], refs[-1]
    copies = [
        pltpu.make_async_copy(here, there, sems.at[i])
        for i, (here, there) in enumerate(zip(inputs, local))
    ]
    for copy in copies:
        copy.start()
    for copy in copies[1:]:
        copy.wait()
    tokens_ref, ids_ref, route_ref, slot_ref = local
    rows, width = tokens_ref.shape
    experts = slot_ref.shape[0]
    row = lax.broadcasted_iota(jnp.int32, (rows, LANES), 0)
    column = lax.broadcasted_iota(jnp.int32, (rows, LANES), 1)
    slot = lax.rem(column, experts)
    weights = jnp.zeros((rows, LANES), jnp.float32)
    for k in range(ids_ref.shape[0]):
        for token in range(rows):
            named = (row == token) & (slot == slot_ref[ids_ref[k, token]])
            weights = jnp.where(named, route_ref[k, token], weights)
    first = weights.astype(jnp.bfloat16).astype(jnp.float32)
    second = (weights - first).astype(jnp.bfloat16).astype(jnp.float32)
    third = weights - first - second
    tail = jnp.where(column < experts, first, jnp.where(column < 2 * experts, second, third))
    copies[0].wait()
    out_ref[:, :width] = tokens_ref[...]
    out_ref[:, width:] = jnp.where(column < 3 * experts, tail, 0.0).astype(jnp.bfloat16)


def pack(tokens, expert_ids, route_weights, expert_slot, *weights):
    rows, width = tokens.shape
    inputs = (tokens, expert_ids.T, route_weights.T, expert_slot)
    held = [pltpu.with_memory_space_constraint(each, pltpu.HBM) for each in inputs + weights]
    return pl.pallas_call(
        pack_kernel,
        out_shape=jax.ShapeDtypeStruct((rows, width + LANES), jnp.bfloat16),
        in_specs=[pl.BlockSpec(memory_space=pl.ANY)] * len(held),
        out_specs=pl.BlockSpec(memory_space=pltpu.VMEM),
        scratch_shapes=[
            pltpu.VMEM(tokens.shape, tokens.dtype),
            *[pltpu.SMEM(each.shape, each.dtype) for each in inputs[1:]],
            pltpu.SemaphoreType.DMA((len(inputs),)),
        ],
        compiler_params=pltpu.CompilerParams(vmem_limit_bytes=VMEM_LIMIT),
        name="pack",
    )(*held)


def stack_kernel(*refs):
    *pieces, out_ref = refs
    out_ref[...] = jnp.concatenate([piece[...] for piece in pieces], axis=0)


def stack(*pieces):
    rows = sum(piece.shape[0] for piece in pieces)
    vmem = pl.BlockSpec(memory_space=pltpu.VMEM)
    return pl.pallas_call(
        stack_kernel,
        out_shape=jax.ShapeDtypeStruct((rows, pieces[0].shape[1]), pieces[0].dtype),
        in_specs=[vmem] * len(pieces),
        out_specs=vmem,
        compiler_params=pltpu.CompilerParams(vmem_limit_bytes=VMEM_LIMIT),
        name="stack",
    )(*pieces)


def hidden_kernel(experts, *refs):
    *pieces, gate_ref, up_ref, out_ref, x_ref, weight_ref = refs
    members, width, hid = gate_ref.shape
    x_ref[...] = jnp.concatenate([piece[:, :width] for piece in pieces], axis=0)
    tail = jnp.concatenate([piece[:, width:] for piece in pieces], axis=0)
    tail = tail.astype(jnp.float32)
    column = lax.broadcasted_iota(jnp.int32, tail.shape, 1)
    for member in range(members):
        slot = lax.axis_index("node") * members + member
        mine = (lax.rem(column, experts) == slot) & (column < 3 * experts)
        weight_ref[member] = jnp.sum(jnp.where(mine, tail, 0.0), axis=1, keepdims=True)
    tiles = hid // N_TILE

    @pl.loop(0, members * tiles, unroll=True)
    def _(step):
        member = step // tiles
        at = pl.ds(pl.multiple_of(lax.rem(step, tiles) * N_TILE, N_TILE), N_TILE)
        gate, up = [
            jnp.dot(x_ref[...], ref[member, :, at], preferred_element_type=jnp.float32)
            for ref in (gate_ref, up_ref)
        ]
        hidden = gate / (1.0 + jnp.exp(-gate)) * up * weight_ref[member]
        to = pl.ds(pl.multiple_of(step * N_TILE, N_TILE), N_TILE)
        out_ref[:, to] = hidden.astype(jnp.bfloat16)


def hidden_units(pieces, w_gate, w_up, experts):
    members, width, hid = w_gate.shape
    rows = sum(piece.shape[0] for piece in pieces)
    vmem = pl.BlockSpec(memory_space=pltpu.VMEM)
    return pl.pallas_call(
        functools.partial(hidden_kernel, experts),
        out_shape=jax.ShapeDtypeStruct((rows, members * hid), jnp.bfloat16),
        in_specs=[vmem] * (len(pieces) + 2),
        out_specs=vmem,
        scratch_shapes=[
            pltpu.VMEM((rows, width), jnp.bfloat16),
            pltpu.VMEM((members, rows, 1), jnp.float32),
        ],
        compiler_params=pltpu.CompilerParams(vmem_limit_bytes=VMEM_LIMIT),
        cost_estimate=pl.CostEstimate(
            flops=4 * rows * members * width * hid,
            bytes_accessed=4 * members * width * hid,
            transcendentals=rows * members * hid,
        ),
        name="hidden",
    )(*pieces, w_gate, w_up)


def down_kernel(chunk, hidden_ref, down_ref, *outs):
    part, width = outs[0].shape

    @pl.loop(0, width // DOWN_TILE, unroll=True)
    def _(step):
        at = pl.ds(pl.multiple_of(step * DOWN_TILE, DOWN_TILE), DOWN_TILE)
        there = pl.ds(pl.multiple_of(chunk * width + step * DOWN_TILE, DOWN_TILE), DOWN_TILE)
        total = jnp.dot(
            hidden_ref[...], down_ref[:, there], preferred_element_type=jnp.float32
        ).astype(jnp.bfloat16)
        for i, ref in enumerate(outs):
            ref[:, at] = total[i * part : (i + 1) * part]


def down(hidden, w_down, chunk, chunks):
    units, width = w_down.shape
    rows = hidden.shape[0]
    vmem = pl.BlockSpec(memory_space=pltpu.VMEM)
    return pl.pallas_call(
        functools.partial(down_kernel, chunk),
        out_shape=[jax.ShapeDtypeStruct((rows // 4, width // chunks), jnp.bfloat16)] * 4,
        in_specs=[vmem, vmem],
        out_specs=[vmem] * 4,
        compiler_params=pltpu.CompilerParams(vmem_limit_bytes=VMEM_LIMIT),
        cost_estimate=pl.CostEstimate(
            flops=2 * rows * units * width // chunks,
            bytes_accessed=2 * units * width // chunks,
            transcendentals=0,
        ),
        name="down",
    )(hidden, w_down)


CHIPS, PLACES = 2, 4


def to_core(value):
    return lax.ppermute(value, "node", [(i, i ^ 1) for i in range(2 * CHIPS)])


def to_chip(value):
    return lax.ppermute(value, "node", [(i, i ^ 2) for i in range(2 * CHIPS)])


def to_place(value, bits):
    return lax.ppermute(value, "local", [(i, i ^ bits) for i in range(PLACES)])


def to_both(value, bits):
    count = 2 * CHIPS * PLACES
    perm = [(i, i ^ (2 * PLACES + bits)) for i in range(count)]
    return lax.ppermute(value, ("node", "local"), perm)


def after(value, *others):
    return lax.optimization_barrier((value, *others))[0]


def gather_blocks(own):
    second, first, far_own = to_place(own, 2), to_place(own, 1), to_chip(own)
    far_first = to_chip(first)
    ready = after(second, far_own)
    far_second, third = to_chip(ready), to_place(ready, 1)
    far_third = to_both(after(ready, far_first), 1)
    early = stack(own, far_own, first, second)
    late = stack(far_first, third, far_second, far_third)
    return [early, late, to_core(early), to_core(late)]


def sums_kernel(*refs):
    inputs, outs = refs[: -PLACES], refs[-PLACES:]
    chunks = len(inputs) // 2
    rows, width = outs[0].shape
    for chunk in range(chunks):
        at = pl.ds(chunk * (width // chunks), width // chunks)
        here, other = [ref[...].astype(jnp.float32) for ref in inputs[chunk::chunks]]
        total = here + other
        for place, ref in enumerate(outs):
            ref[:, at] = total[place * rows : (place + 1) * rows].astype(ref.dtype)


def sums(here, other):
    rows, width = here[0].shape[0] // PLACES, here[0].shape[1] * len(here)
    vmem = pl.BlockSpec(memory_space=pltpu.VMEM)
    return pl.pallas_call(
        sums_kernel,
        out_shape=[jax.ShapeDtypeStruct((rows, width), here[0].dtype)] * PLACES,
        in_specs=[vmem] * (2 * len(here)),
        out_specs=[vmem] * PLACES,
        compiler_params=pltpu.CompilerParams(vmem_limit_bytes=VMEM_LIMIT),
        name="sums",
    )(*here, *other)


def total(*terms):
    return sum(term.astype(jnp.float32) for term in terms)


def reduce_blocks(chunks):
    early, late, other_early, other_late = zip(*chunks)
    other_late = [to_core(each) for each in other_late]
    other_early = [to_core(after(each, *other_late)) for each in other_early]
    far_first, third, far_second, far_third = sums(late, other_late)
    third, far_second = to_place(third, 1), to_chip(far_second)
    far_third, far_first = to_both(far_third, 1), to_chip(far_first)
    own, far_own, first, second = sums(early, other_early)
    first = total(first, far_first).astype(jnp.bfloat16)
    first_here = to_place(first, 1)
    far_own = to_chip(after(far_own, first_here))
    second = total(second, third, far_second, far_third).astype(jnp.bfloat16)
    return total(own, to_place(second, 2), first_here, far_own).astype(jnp.bfloat16)


def by_permutes(tokens, expert_ids, route_weights, expert_slot, w_gate, w_up, w_down):
    own = pack(tokens, expert_ids, route_weights, expert_slot, w_gate, w_up, w_down)
    hidden = hidden_units(gather_blocks(own), w_gate, w_up, expert_slot.shape[0])
    matrix = w_down.reshape(-1, w_down.shape[-1])
    chunks = []
    for chunk in range(OUT_CHUNKS):
        chunks.append(down(hidden, matrix, chunk, OUT_CHUNKS))
        hidden = after(hidden, chunks[-1][-1])
    return reduce_blocks(chunks)


def by_collectives(tokens, expert_ids, route_weights, expert_slot, w_gate, w_up, w_down):
    members, width, _ = w_gate.shape
    experts = expert_slot.shape[0]
    packed = pack(tokens, expert_ids, route_weights, expert_slot)
    gathered = lax.all_gather(packed, ("node", "local"), axis=0, tiled=True)
    rows = gathered[:, :width]
    tail = gathered[:, width : width + 3 * experts].astype(jnp.float32)
    weights = tail.reshape(-1, 3, experts).sum(axis=1)
    mine = lax.dynamic_slice_in_dim(weights, lax.axis_index("node") * members, members, axis=1)
    gate = jnp.einsum("td,edh->eth", rows, w_gate, preferred_element_type=jnp.float32)
    up = jnp.einsum("td,edh->eth", rows, w_up, preferred_element_type=jnp.float32)
    hidden = (jax.nn.silu(gate) * up * mine.T[..., None]).astype(jnp.bfloat16)
    result = jnp.einsum("eth,ehd->td", hidden, w_down, preferred_element_type=jnp.float32)
    return lax.psum_scatter(
        result.astype(jnp.bfloat16), ("node", "local"), scatter_dimension=0, tiled=True
    )


def per_device(*args):
    small = (lax.axis_size("node"), lax.axis_size("local")) == (2 * CHIPS, PLACES)
    return (by_permutes if small else by_collectives)(*args)


def solution(mesh):
    rows = P(("parts", "node", "local"), None)
    in_specs = (
        rows,
        rows,
        rows,
        P(),
        P("node", None, "local"),
        P("node", None, "local"),
        P("node", "local", None),
    )
    return jax.shard_map(
        per_device, mesh=mesh, in_specs=in_specs, out_specs=rows, check_vma=False
    )
```

```python
import functools

import jax
import jax.numpy as jnp
from jax import lax
from jax.experimental import pallas as pl
from jax.experimental.pallas import tpu as pltpu
from jax.sharding import PartitionSpec as P

LANES = 128
N_TILE = 256
DOWN_TILE = 1792
OUT_CHUNKS = 1
VMEM_LIMIT = 4 * 2**20


def pack_kernel(*refs):
    inputs, out_ref, local, sems = refs[:4], refs[-6], refs[-5:-1], refs[-1]
    copies = [
        pltpu.make_async_copy(here, there, sems.at[i])
        for i, (here, there) in enumerate(zip(inputs, local))
    ]
    for copy in copies:
        copy.start()
    for copy in copies[1:]:
        copy.wait()
    tokens_ref, ids_ref, route_ref, slot_ref = local
    rows, width = tokens_ref.shape
    experts = slot_ref.shape[0]
    row = lax.broadcasted_iota(jnp.int32, (rows, LANES), 0)
    column = lax.broadcasted_iota(jnp.int32, (rows, LANES), 1)
    slot = lax.rem(column, experts)
    weights = jnp.zeros((rows, LANES), jnp.float32)
    for k in range(ids_ref.shape[0]):
        for token in range(rows):
            named = (row == token) & (slot == slot_ref[ids_ref[k, token]])
            weights = jnp.where(named, route_ref[k, token], weights)
    first = weights.astype(jnp.bfloat16).astype(jnp.float32)
    second = (weights - first).astype(jnp.bfloat16).astype(jnp.float32)
    third = weights - first - second
    tail = jnp.where(column < experts, first, jnp.where(column < 2 * experts, second, third))
    copies[0].wait()
    out_ref[:, :width] = tokens_ref[...]
    out_ref[:, width:] = jnp.where(column < 3 * experts, tail, 0.0).astype(jnp.bfloat16)


def pack(tokens, expert_ids, route_weights, expert_slot, *weights):
    rows, width = tokens.shape
    inputs = (tokens, expert_ids.T, route_weights.T, expert_slot)
    held = [pltpu.with_memory_space_constraint(each, pltpu.HBM) for each in inputs + weights]
    return pl.pallas_call(
        pack_kernel,
        out_shape=jax.ShapeDtypeStruct((rows, width + LANES), jnp.bfloat16),
        in_specs=[pl.BlockSpec(memory_space=pl.ANY)] * len(held),
        out_specs=pl.BlockSpec(memory_space=pltpu.VMEM),
        scratch_shapes=[
            pltpu.VMEM(tokens.shape, tokens.dtype),
            *[pltpu.SMEM(each.shape, each.dtype) for each in inputs[1:]],
            pltpu.SemaphoreType.DMA((len(inputs),)),
        ],
        compiler_params=pltpu.CompilerParams(vmem_limit_bytes=VMEM_LIMIT),
        name="pack",
    )(*held)


def stack_kernel(*refs):
    *pieces, out_ref = refs
    out_ref[...] = jnp.concatenate([piece[...] for piece in pieces], axis=0)


def stack(*pieces):
    rows = sum(piece.shape[0] for piece in pieces)
    vmem = pl.BlockSpec(memory_space=pltpu.VMEM)
    return pl.pallas_call(
        stack_kernel,
        out_shape=jax.ShapeDtypeStruct((rows, pieces[0].shape[1]), pieces[0].dtype),
        in_specs=[vmem] * len(pieces),
        out_specs=vmem,
        compiler_params=pltpu.CompilerParams(vmem_limit_bytes=VMEM_LIMIT),
        name="stack",
    )(*pieces)


def hidden_kernel(experts, *refs):
    *pieces, gate_ref, up_ref, out_ref, x_ref, weight_ref = refs
    members, width, hid = gate_ref.shape
    x_ref[...] = jnp.concatenate([piece[:, :width] for piece in pieces], axis=0)
    tail = jnp.concatenate([piece[:, width:] for piece in pieces], axis=0)
    tail = tail.astype(jnp.float32)
    column = lax.broadcasted_iota(jnp.int32, tail.shape, 1)
    for member in range(members):
        slot = lax.axis_index("node") * members + member
        mine = (lax.rem(column, experts) == slot) & (column < 3 * experts)
        weight_ref[member] = jnp.sum(jnp.where(mine, tail, 0.0), axis=1, keepdims=True)
    tiles = hid // N_TILE

    @pl.loop(0, members * tiles, unroll=True)
    def _(step):
        member = step // tiles
        at = pl.ds(pl.multiple_of(lax.rem(step, tiles) * N_TILE, N_TILE), N_TILE)
        gate, up = [
            jnp.dot(x_ref[...], ref[member, :, at], preferred_element_type=jnp.float32)
            for ref in (gate_ref, up_ref)
        ]
        hidden = gate / (1.0 + jnp.exp(-gate)) * up * weight_ref[member]
        to = pl.ds(pl.multiple_of(step * N_TILE, N_TILE), N_TILE)
        out_ref[:, to] = hidden.astype(jnp.bfloat16)


def hidden_units(pieces, w_gate, w_up, experts):
    members, width, hid = w_gate.shape
    rows = sum(piece.shape[0] for piece in pieces)
    vmem = pl.BlockSpec(memory_space=pltpu.VMEM)
    return pl.pallas_call(
        functools.partial(hidden_kernel, experts),
        out_shape=jax.ShapeDtypeStruct((rows, members * hid), jnp.bfloat16),
        in_specs=[vmem] * (len(pieces) + 2),
        out_specs=vmem,
        scratch_shapes=[
            pltpu.VMEM((rows, width), jnp.bfloat16),
            pltpu.VMEM((members, rows, 1), jnp.float32),
        ],
        compiler_params=pltpu.CompilerParams(vmem_limit_bytes=VMEM_LIMIT),
        cost_estimate=pl.CostEstimate(
            flops=4 * rows * members * width * hid,
            bytes_accessed=4 * members * width * hid,
            transcendentals=rows * members * hid,
        ),
        name="hidden",
    )(*pieces, w_gate, w_up)


def down_kernel(chunk, hidden_ref, down_ref, *outs):
    part, width = outs[0].shape

    @pl.loop(0, width // DOWN_TILE, unroll=True)
    def _(step):
        at = pl.ds(pl.multiple_of(step * DOWN_TILE, DOWN_TILE), DOWN_TILE)
        there = pl.ds(pl.multiple_of(chunk * width + step * DOWN_TILE, DOWN_TILE), DOWN_TILE)
        total = jnp.dot(
            hidden_ref[...], down_ref[:, there], preferred_element_type=jnp.float32
        ).astype(jnp.bfloat16)
        for i, ref in enumerate(outs):
            ref[:, at] = total[i * part : (i + 1) * part]


def down(hidden, w_down, chunk, chunks):
    units, width = w_down.shape
    rows = hidden.shape[0]
    vmem = pl.BlockSpec(memory_space=pltpu.VMEM)
    return pl.pallas_call(
        functools.partial(down_kernel, chunk),
        out_shape=[jax.ShapeDtypeStruct((rows // 4, width // chunks), jnp.bfloat16)] * 4,
        in_specs=[vmem, vmem],
        out_specs=[vmem] * 4,
        compiler_params=pltpu.CompilerParams(vmem_limit_bytes=VMEM_LIMIT),
        cost_estimate=pl.CostEstimate(
            flops=2 * rows * units * width // chunks,
            bytes_accessed=2 * units * width // chunks,
            transcendentals=0,
        ),
        name="down",
    )(hidden, w_down)


CHIPS, PLACES = 2, 4


def to_core(value):
    return lax.ppermute(value, "node", [(i, i ^ 1) for i in range(2 * CHIPS)])


def to_chip(value):
    return lax.ppermute(value, "node", [(i, i ^ 2) for i in range(2 * CHIPS)])


def to_place(value, bits):
    return lax.ppermute(value, "local", [(i, i ^ bits) for i in range(PLACES)])


def to_both(value, bits):
    count = 2 * CHIPS * PLACES
    perm = [(i, i ^ (2 * PLACES + bits)) for i in range(count)]
    return lax.ppermute(value, ("node", "local"), perm)


def after(value, *others):
    return lax.optimization_barrier((value, *others))[0]


def gather_blocks(own):
    second, first, far_own = to_place(own, 2), to_place(own, 1), to_chip(own)
    far_first = to_chip(first)
    ready = after(second, far_own)
    far_second, third = to_chip(ready), to_place(ready, 1)
    far_third = to_both(after(ready, far_first), 1)
    early = stack(own, far_own, first, far_first)
    late = stack(second, third, far_second, far_third)
    return [early, late, to_core(early), to_core(late)]


def sums_kernel(*refs):
    inputs, outs = refs[: -PLACES], refs[-PLACES:]
    chunks = len(inputs) // 2
    rows, width = outs[0].shape
    for chunk in range(chunks):
        at = pl.ds(chunk * (width // chunks), width // chunks)
        here, other = [ref[...].astype(jnp.float32) for ref in inputs[chunk::chunks]]
        total = here + other
        for place, ref in enumerate(outs):
            ref[:, at] = total[place * rows : (place + 1) * rows].astype(ref.dtype)


def sums(here, other):
    rows, width = here[0].shape[0] // PLACES, here[0].shape[1] * len(here)
    vmem = pl.BlockSpec(memory_space=pltpu.VMEM)
    return pl.pallas_call(
        sums_kernel,
        out_shape=[jax.ShapeDtypeStruct((rows, width), here[0].dtype)] * PLACES,
        in_specs=[vmem] * (2 * len(here)),
        out_specs=[vmem] * PLACES,
        compiler_params=pltpu.CompilerParams(vmem_limit_bytes=VMEM_LIMIT),
        name="sums",
    )(*here, *other)


def total(*terms):
    return sum(term.astype(jnp.float32) for term in terms)


def reduce_blocks(chunks):
    early, late, other_early, other_late = zip(*chunks)
    other_late = [to_core(each) for each in other_late]
    other_early = [to_core(after(each, *other_late)) for each in other_early]
    second, third, far_second, far_third = sums(late, other_late)
    far_second = to_chip(far_second)
    far_third = to_both(far_third, 1)
    third = to_place(third, 1)
    second = total(second, far_second, far_third, third).astype(jnp.bfloat16)
    own, far_own, first, far_first = sums(early, other_early)
    first = total(first, to_chip(after(far_first, far_second, third))).astype(jnp.bfloat16)
    first, far_own = lax.optimization_barrier((first, far_own))
    second_here, first_here, far_own = to_place(second, 2), to_place(first, 1), to_chip(far_own)
    return total(own, second_here, first_here, far_own).astype(jnp.bfloat16)


def by_permutes(tokens, expert_ids, route_weights, expert_slot, w_gate, w_up, w_down):
    own = pack(tokens, expert_ids, route_weights, expert_slot, w_gate, w_up, w_down)
    hidden = hidden_units(gather_blocks(own), w_gate, w_up, expert_slot.shape[0])
    matrix = w_down.reshape(-1, w_down.shape[-1])
    chunks = []
    for chunk in range(OUT_CHUNKS):
        chunks.append(down(hidden, matrix, chunk, OUT_CHUNKS))
        hidden = after(hidden, chunks[-1][-1])
    return reduce_blocks(chunks)


def by_collectives(tokens, expert_ids, route_weights, expert_slot, w_gate, w_up, w_down):
    members, width, _ = w_gate.shape
    experts = expert_slot.shape[0]
    packed = pack(tokens, expert_ids, route_weights, expert_slot)
    gathered = lax.all_gather(packed, ("node", "local"), axis=0, tiled=True)
    rows = gathered[:, :width]
    tail = gathered[:, width : width + 3 * experts].astype(jnp.float32)
    weights = tail.reshape(-1, 3, experts).sum(axis=1)
    mine = lax.dynamic_slice_in_dim(weights, lax.axis_index("node") * members, members, axis=1)
    gate = jnp.einsum("td,edh->eth", rows, w_gate, preferred_element_type=jnp.float32)
    up = jnp.einsum("td,edh->eth", rows, w_up, preferred_element_type=jnp.float32)
    hidden = (jax.nn.silu(gate) * up * mine.T[..., None]).astype(jnp.bfloat16)
    result = jnp.einsum("eth,ehd->td", hidden, w_down, preferred_element_type=jnp.float32)
    return lax.psum_scatter(
        result.astype(jnp.bfloat16), ("node", "local"), scatter_dimension=0, tiled=True
    )


def per_device(*args):
    small = (lax.axis_size("node"), lax.axis_size("local")) == (2 * CHIPS, PLACES)
    return (by_permutes if small else by_collectives)(*args)


def solution(mesh):
    rows = P(("parts", "node", "local"), None)
    in_specs = (
        rows,
        rows,
        rows,
        P(),
        P("node", None, "local"),
        P("node", None, "local"),
        P("node", "local", None),
    )
    return jax.shard_map(
        per_device, mesh=mesh, in_specs=in_specs, out_specs=rows, check_vma=False
    )
```

```python
import functools

import jax
import jax.numpy as jnp
from jax import lax
from jax.experimental import pallas as pl
from jax.experimental.pallas import tpu as pltpu
from jax.sharding import PartitionSpec as P

LANES = 128
N_TILE = 256
DOWN_TILE = 1792
VMEM_LIMIT = 4 * 2**20


def pack_kernel(*refs):
    inputs, out_ref, local, sems = refs[:4], refs[-6], refs[-5:-1], refs[-1]
    copies = [
        pltpu.make_async_copy(here, there, sems.at[i])
        for i, (here, there) in enumerate(zip(inputs, local))
    ]
    for copy in copies:
        copy.start()
    for copy in copies[1:]:
        copy.wait()
    tokens_ref, ids_ref, route_ref, slot_ref = local
    rows, width = tokens_ref.shape
    experts = slot_ref.shape[0]
    row = lax.broadcasted_iota(jnp.int32, (rows, LANES), 0)
    column = lax.broadcasted_iota(jnp.int32, (rows, LANES), 1)
    slot = lax.rem(column, experts)
    weights = jnp.zeros((rows, LANES), jnp.float32)
    for k in range(ids_ref.shape[0]):
        for token in range(rows):
            named = (row == token) & (slot == slot_ref[ids_ref[k, token]])
            weights = jnp.where(named, route_ref[k, token], weights)
    first = weights.astype(jnp.bfloat16).astype(jnp.float32)
    second = (weights - first).astype(jnp.bfloat16).astype(jnp.float32)
    third = weights - first - second
    tail = jnp.where(column < experts, first, jnp.where(column < 2 * experts, second, third))
    copies[0].wait()
    out_ref[:, :width] = tokens_ref[...]
    out_ref[:, width:] = jnp.where(column < 3 * experts, tail, 0.0).astype(jnp.bfloat16)


def pack(tokens, expert_ids, route_weights, expert_slot, *weights):
    rows, width = tokens.shape
    inputs = (tokens, expert_ids.T, route_weights.T, expert_slot)
    held = [pltpu.with_memory_space_constraint(each, pltpu.HBM) for each in inputs + weights]
    return pl.pallas_call(
        pack_kernel,
        out_shape=jax.ShapeDtypeStruct((rows, width + LANES), jnp.bfloat16),
        in_specs=[pl.BlockSpec(memory_space=pl.ANY)] * len(held),
        out_specs=pl.BlockSpec(memory_space=pltpu.VMEM),
        scratch_shapes=[
            pltpu.VMEM(tokens.shape, tokens.dtype),
            *[pltpu.SMEM(each.shape, each.dtype) for each in inputs[1:]],
            pltpu.SemaphoreType.DMA((len(inputs),)),
        ],
        compiler_params=pltpu.CompilerParams(vmem_limit_bytes=VMEM_LIMIT),
        name="pack",
    )(*held)


def stack_kernel(*refs):
    *pieces, out_ref = refs
    out_ref[...] = jnp.concatenate([piece[...] for piece in pieces], axis=0)


def stack(*pieces):
    rows = sum(piece.shape[0] for piece in pieces)
    vmem = pl.BlockSpec(memory_space=pltpu.VMEM)
    return pl.pallas_call(
        stack_kernel,
        out_shape=jax.ShapeDtypeStruct((rows, pieces[0].shape[1]), pieces[0].dtype),
        in_specs=[vmem] * len(pieces),
        out_specs=vmem,
        compiler_params=pltpu.CompilerParams(vmem_limit_bytes=VMEM_LIMIT),
        name="stack",
    )(*pieces)


def hidden_kernel(experts, *refs):
    *pieces, gate_ref, up_ref, out_ref, x_ref, weight_ref = refs
    members, width, hid = gate_ref.shape
    x_ref[...] = jnp.concatenate([piece[:, :width] for piece in pieces], axis=0)
    tail = jnp.concatenate([piece[:, width:] for piece in pieces], axis=0)
    tail = tail.astype(jnp.float32)
    column = lax.broadcasted_iota(jnp.int32, tail.shape, 1)
    for member in range(members):
        slot = lax.axis_index("node") * members + member
        mine = (lax.rem(column, experts) == slot) & (column < 3 * experts)
        weight_ref[member] = jnp.sum(jnp.where(mine, tail, 0.0), axis=1, keepdims=True)
    tiles = hid // N_TILE

    @pl.loop(0, members * tiles, unroll=True)
    def _(step):
        member = step // tiles
        at = pl.ds(pl.multiple_of(lax.rem(step, tiles) * N_TILE, N_TILE), N_TILE)
        gate, up = [
            jnp.dot(x_ref[...], ref[member, :, at], preferred_element_type=jnp.float32)
            for ref in (gate_ref, up_ref)
        ]
        hidden = gate / (1.0 + jnp.exp(-gate)) * up * weight_ref[member]
        to = pl.ds(pl.multiple_of(step * N_TILE, N_TILE), N_TILE)
        out_ref[:, to] = hidden.astype(jnp.bfloat16)


def hidden_units(pieces, w_gate, w_up, experts):
    members, width, hid = w_gate.shape
    rows = sum(piece.shape[0] for piece in pieces)
    vmem = pl.BlockSpec(memory_space=pltpu.VMEM)
    return pl.pallas_call(
        functools.partial(hidden_kernel, experts),
        out_shape=jax.ShapeDtypeStruct((rows, members * hid), jnp.bfloat16),
        in_specs=[vmem] * (len(pieces) + 2),
        out_specs=vmem,
        scratch_shapes=[
            pltpu.VMEM((rows, width), jnp.bfloat16),
            pltpu.VMEM((members, rows, 1), jnp.float32),
        ],
        compiler_params=pltpu.CompilerParams(vmem_limit_bytes=VMEM_LIMIT),
        cost_estimate=pl.CostEstimate(
            flops=4 * rows * members * width * hid,
            bytes_accessed=4 * members * width * hid,
            transcendentals=rows * members * hid,
        ),
        name="hidden",
    )(*pieces, w_gate, w_up)


def down_kernel(hidden_ref, down_ref, *outs):
    width = down_ref.shape[1]

    @pl.loop(0, width // DOWN_TILE, unroll=True)
    def _(step):
        at = pl.ds(pl.multiple_of(step * DOWN_TILE, DOWN_TILE), DOWN_TILE)
        total = jnp.dot(hidden_ref[...], down_ref[:, at], preferred_element_type=jnp.float32)
        start = 0
        for ref in outs:
            ref[:, at] = total[start : start + ref.shape[0]].astype(ref.dtype)
            start += ref.shape[0]


def down(hidden, w_down, groups):
    units, width = w_down.shape
    rows = hidden.shape[0]
    vmem = pl.BlockSpec(memory_space=pltpu.VMEM)
    return pl.pallas_call(
        down_kernel,
        out_shape=[jax.ShapeDtypeStruct((size, width), jnp.bfloat16) for size in groups],
        in_specs=[vmem, vmem],
        out_specs=[vmem] * len(groups),
        compiler_params=pltpu.CompilerParams(vmem_limit_bytes=VMEM_LIMIT),
        cost_estimate=pl.CostEstimate(
            flops=2 * rows * units * width,
            bytes_accessed=2 * units * width,
            transcendentals=0,
        ),
        name="down",
    )(hidden, w_down)


CHIPS, PLACES = 2, 4
EARLY, LATE = 5, 3


def to_core(value):
    return lax.ppermute(value, "node", [(i, i ^ 1) for i in range(2 * CHIPS)])


def to_chip(value):
    return lax.ppermute(value, "node", [(i, i ^ 2) for i in range(2 * CHIPS)])


def to_place(value, bits):
    return lax.ppermute(value, "local", [(i, i ^ bits) for i in range(PLACES)])


def to_both(value, bits):
    count = 2 * CHIPS * PLACES
    perm = [(i, i ^ (2 * PLACES + bits)) for i in range(count)]
    return lax.ppermute(value, ("node", "local"), perm)


def after(value, *others):
    return lax.optimization_barrier((value, *others))[0]


def gather_blocks(own):
    second, first, far_own = to_place(own, 2), to_place(own, 1), to_chip(own)
    far_first = to_chip(first)
    ready = after(second, far_own)
    far_second, third = to_chip(ready), to_place(ready, 1)
    far_third = to_both(after(ready, far_first), 1)
    early = stack(own, far_own, first, far_first)
    late = stack(second, third, far_second, far_third)
    return [early, late, to_core(early), to_core(late)]


def sums_kernel(here_ref, other_ref, *outs):
    total = here_ref[...].astype(jnp.float32) + other_ref[...].astype(jnp.float32)
    rows = outs[0].shape[0]
    for i, ref in enumerate(outs):
        ref[...] = total[i * rows : (i + 1) * rows].astype(ref.dtype)


def sums(here, other, blocks):
    vmem = pl.BlockSpec(memory_space=pltpu.VMEM)
    block = jax.ShapeDtypeStruct((here.shape[0] // blocks, here.shape[1]), here.dtype)
    return pl.pallas_call(
        sums_kernel,
        out_shape=[block] * blocks,
        in_specs=[vmem, vmem],
        out_specs=[vmem] * blocks,
        compiler_params=pltpu.CompilerParams(vmem_limit_bytes=VMEM_LIMIT),
        name="sums",
    )(here, other)


def total(*terms):
    return sum(term.astype(jnp.float32) for term in terms)


def reduce_blocks(early, late, other_early, other_late):
    other_late = to_core(other_late)
    other_early = to_core(after(other_early, other_late))
    third, far_second, far_third = sums(late, other_late, LATE)
    far_second = to_chip(far_second)
    far_third = to_both(far_third, 1)
    third = to_place(third, 1)
    own, far_own, first, far_first, second = sums(early, other_early, EARLY)
    second = total(second, far_second, far_third, third).astype(jnp.bfloat16)
    first = total(first, to_chip(after(far_first, far_second, third))).astype(jnp.bfloat16)
    first, far_own = lax.optimization_barrier((first, far_own))
    second_here, first_here, far_own = to_place(second, 2), to_place(first, 1), to_chip(far_own)
    return total(own, second_here, first_here, far_own).astype(jnp.bfloat16)


def by_permutes(tokens, expert_ids, route_weights, expert_slot, w_gate, w_up, w_down):
    own = pack(tokens, expert_ids, route_weights, expert_slot, w_gate, w_up, w_down)
    hidden = hidden_units(gather_blocks(own), w_gate, w_up, expert_slot.shape[0])
    matrix = w_down.reshape(-1, w_down.shape[-1])
    rows = tokens.shape[0]
    groups = (EARLY * rows, LATE * rows) * 2
    return reduce_blocks(*down(hidden, matrix, groups))


def by_collectives(tokens, expert_ids, route_weights, expert_slot, w_gate, w_up, w_down):
    members, width, _ = w_gate.shape
    experts = expert_slot.shape[0]
    packed = pack(tokens, expert_ids, route_weights, expert_slot)
    gathered = lax.all_gather(packed, ("node", "local"), axis=0, tiled=True)
    rows = gathered[:, :width]
    tail = gathered[:, width : width + 3 * experts].astype(jnp.float32)
    weights = tail.reshape(-1, 3, experts).sum(axis=1)
    mine = lax.dynamic_slice_in_dim(weights, lax.axis_index("node") * members, members, axis=1)
    gate = jnp.einsum("td,edh->eth", rows, w_gate, preferred_element_type=jnp.float32)
    up = jnp.einsum("td,edh->eth", rows, w_up, preferred_element_type=jnp.float32)
    hidden = (jax.nn.silu(gate) * up * mine.T[..., None]).astype(jnp.bfloat16)
    result = jnp.einsum("eth,ehd->td", hidden, w_down, preferred_element_type=jnp.float32)
    return lax.psum_scatter(
        result.astype(jnp.bfloat16), ("node", "local"), scatter_dimension=0, tiled=True
    )


def per_device(*args):
    small = (lax.axis_size("node"), lax.axis_size("local")) == (2 * CHIPS, PLACES)
    return (by_permutes if small else by_collectives)(*args)


def solution(mesh):
    rows = P(("parts", "node", "local"), None)
    in_specs = (
        rows,
        rows,
        rows,
        P(),
        P("node", None, "local"),
        P("node", None, "local"),
        P("node", "local", None),
    )
    return jax.shard_map(
        per_device, mesh=mesh, in_specs=in_specs, out_specs=rows, check_vma=False
    )
```

```python
import functools

import jax
import jax.numpy as jnp
from jax import lax
from jax.experimental import pallas as pl
from jax.experimental.pallas import tpu as pltpu
from jax.sharding import PartitionSpec as P

LANES = 128
N_TILE = 512
DOWN_TILE = 1792
VMEM_LIMIT = 4 * 2**20


def pack_kernel(*refs):
    inputs, out_ref, local, sems = refs[:4], refs[-6], refs[-5:-1], refs[-1]
    copies = [
        pltpu.make_async_copy(here, there, sems.at[i])
        for i, (here, there) in enumerate(zip(inputs, local))
    ]
    for copy in copies:
        copy.start()
    for copy in copies[1:]:
        copy.wait()
    tokens_ref, ids_ref, route_ref, slot_ref = local
    rows, width = tokens_ref.shape
    experts = slot_ref.shape[0]
    row = lax.broadcasted_iota(jnp.int32, (rows, LANES), 0)
    column = lax.broadcasted_iota(jnp.int32, (rows, LANES), 1)
    slot = lax.rem(column, experts)
    weights = jnp.zeros((rows, LANES), jnp.float32)
    for k in range(ids_ref.shape[0]):
        for token in range(rows):
            named = (row == token) & (slot == slot_ref[ids_ref[k, token]])
            weights = jnp.where(named, route_ref[k, token], weights)
    first = weights.astype(jnp.bfloat16).astype(jnp.float32)
    second = (weights - first).astype(jnp.bfloat16).astype(jnp.float32)
    third = weights - first - second
    tail = jnp.where(column < experts, first, jnp.where(column < 2 * experts, second, third))
    copies[0].wait()
    out_ref[:, :width] = tokens_ref[...]
    out_ref[:, width:] = jnp.where(column < 3 * experts, tail, 0.0).astype(jnp.bfloat16)


def pack(tokens, expert_ids, route_weights, expert_slot, *weights):
    rows, width = tokens.shape
    inputs = (tokens, expert_ids.T, route_weights.T, expert_slot)
    held = [pltpu.with_memory_space_constraint(each, pltpu.HBM) for each in inputs + weights]
    return pl.pallas_call(
        pack_kernel,
        out_shape=jax.ShapeDtypeStruct((rows, width + LANES), jnp.bfloat16),
        in_specs=[pl.BlockSpec(memory_space=pl.ANY)] * len(held),
        out_specs=pl.BlockSpec(memory_space=pltpu.VMEM),
        scratch_shapes=[
            pltpu.VMEM(tokens.shape, tokens.dtype),
            *[pltpu.SMEM(each.shape, each.dtype) for each in inputs[1:]],
            pltpu.SemaphoreType.DMA((len(inputs),)),
        ],
        compiler_params=pltpu.CompilerParams(vmem_limit_bytes=VMEM_LIMIT),
        name="pack",
    )(*held)


def stack_kernel(*refs):
    *pieces, out_ref = refs
    out_ref[...] = jnp.concatenate([piece[...] for piece in pieces], axis=0)


def stack(*pieces):
    rows = sum(piece.shape[0] for piece in pieces)
    vmem = pl.BlockSpec(memory_space=pltpu.VMEM)
    return pl.pallas_call(
        stack_kernel,
        out_shape=jax.ShapeDtypeStruct((rows, pieces[0].shape[1]), pieces[0].dtype),
        in_specs=[vmem] * len(pieces),
        out_specs=vmem,
        compiler_params=pltpu.CompilerParams(vmem_limit_bytes=VMEM_LIMIT),
        name="stack",
    )(*pieces)


def hidden_kernel(experts, *refs):
    *pieces, gate_ref, up_ref, out_ref, x_ref, weight_ref = refs
    members, width, hid = gate_ref.shape
    x_ref[...] = jnp.concatenate([piece[:, :width] for piece in pieces], axis=0)
    tail = jnp.concatenate([piece[:, width:] for piece in pieces], axis=0)
    tail = tail.astype(jnp.float32)
    column = lax.broadcasted_iota(jnp.int32, tail.shape, 1)
    for member in range(members):
        slot = lax.axis_index("node") * members + member
        mine = (lax.rem(column, experts) == slot) & (column < 3 * experts)
        weight_ref[member] = jnp.sum(jnp.where(mine, tail, 0.0), axis=1, keepdims=True)
    tiles = hid // N_TILE

    @pl.loop(0, members * tiles, unroll=True)
    def _(step):
        member = step // tiles
        at = pl.ds(pl.multiple_of(lax.rem(step, tiles) * N_TILE, N_TILE), N_TILE)
        gate, up = [
            jnp.dot(x_ref[...], ref[member, :, at], preferred_element_type=jnp.float32)
            for ref in (gate_ref, up_ref)
        ]
        hidden = gate / (1.0 + jnp.exp(-gate)) * up * weight_ref[member]
        to = pl.ds(pl.multiple_of(step * N_TILE, N_TILE), N_TILE)
        out_ref[:, to] = hidden.astype(jnp.bfloat16)


def hidden_units(pieces, w_gate, w_up, experts):
    members, width, hid = w_gate.shape
    rows = sum(piece.shape[0] for piece in pieces)
    vmem = pl.BlockSpec(memory_space=pltpu.VMEM)
    return pl.pallas_call(
        functools.partial(hidden_kernel, experts),
        out_shape=jax.ShapeDtypeStruct((rows, members * hid), jnp.bfloat16),
        in_specs=[vmem] * (len(pieces) + 2),
        out_specs=vmem,
        scratch_shapes=[
            pltpu.VMEM((rows, width), jnp.bfloat16),
            pltpu.VMEM((members, rows, 1), jnp.float32),
        ],
        compiler_params=pltpu.CompilerParams(vmem_limit_bytes=VMEM_LIMIT),
        cost_estimate=pl.CostEstimate(
            flops=4 * rows * members * width * hid,
            bytes_accessed=4 * members * width * hid,
            transcendentals=rows * members * hid,
        ),
        name="hidden",
    )(*pieces, w_gate, w_up)


def down_kernel(hidden_ref, down_ref, *outs):
    width = down_ref.shape[1]

    @pl.loop(0, width // DOWN_TILE, unroll=True)
    def _(step):
        at = pl.ds(pl.multiple_of(step * DOWN_TILE, DOWN_TILE), DOWN_TILE)
        total = jnp.dot(hidden_ref[...], down_ref[:, at], preferred_element_type=jnp.float32)
        start = 0
        for ref in outs:
            ref[:, at] = total[start : start + ref.shape[0]].astype(ref.dtype)
            start += ref.shape[0]


def down(hidden, w_down, groups):
    units, width = w_down.shape
    rows = hidden.shape[0]
    vmem = pl.BlockSpec(memory_space=pltpu.VMEM)
    return pl.pallas_call(
        down_kernel,
        out_shape=[jax.ShapeDtypeStruct((size, width), jnp.bfloat16) for size in groups],
        in_specs=[vmem, vmem],
        out_specs=[vmem] * len(groups),
        compiler_params=pltpu.CompilerParams(vmem_limit_bytes=VMEM_LIMIT),
        cost_estimate=pl.CostEstimate(
            flops=2 * rows * units * width,
            bytes_accessed=2 * units * width,
            transcendentals=0,
        ),
        name="down",
    )(hidden, w_down)


CHIPS, PLACES = 2, 4
EARLY, LATE = 5, 3


def to_core(value):
    return lax.ppermute(value, "node", [(i, i ^ 1) for i in range(2 * CHIPS)])


def to_chip(value):
    return lax.ppermute(value, "node", [(i, i ^ 2) for i in range(2 * CHIPS)])


def to_place(value, bits):
    return lax.ppermute(value, "local", [(i, i ^ bits) for i in range(PLACES)])


def to_both(value, bits):
    count = 2 * CHIPS * PLACES
    perm = [(i, i ^ (2 * PLACES + bits)) for i in range(count)]
    return lax.ppermute(value, ("node", "local"), perm)


def after(value, *others):
    return lax.optimization_barrier((value, *others))[0]


def gather_blocks(own):
    second, first, far_own = to_place(own, 2), to_place(own, 1), to_chip(own)
    far_first = to_chip(first)
    ready = after(second, far_own)
    far_second, third = to_chip(ready), to_place(ready, 1)
    far_third = to_both(after(ready, far_first), 1)
    early = stack(own, far_own, first, far_first)
    late = stack(second, third, far_second, far_third)
    return [early, late, to_core(early), to_core(late)]


def sums_kernel(here_ref, other_ref, *outs):
    total = here_ref[...].astype(jnp.float32) + other_ref[...].astype(jnp.float32)
    rows = outs[0].shape[0]
    for i, ref in enumerate(outs):
        ref[...] = total[i * rows : (i + 1) * rows].astype(ref.dtype)


def sums(here, other, blocks):
    vmem = pl.BlockSpec(memory_space=pltpu.VMEM)
    block = jax.ShapeDtypeStruct((here.shape[0] // blocks, here.shape[1]), here.dtype)
    return pl.pallas_call(
        sums_kernel,
        out_shape=[block] * blocks,
        in_specs=[vmem, vmem],
        out_specs=[vmem] * blocks,
        compiler_params=pltpu.CompilerParams(vmem_limit_bytes=VMEM_LIMIT),
        name="sums",
    )(here, other)


def total(*terms):
    return sum(term.astype(jnp.float32) for term in terms)


def reduce_blocks(early, late, other_early, other_late):
    other_late = to_core(other_late)
    other_early = to_core(after(other_early, other_late))
    third, far_second, far_third = sums(late, other_late, LATE)
    far_second = to_chip(far_second)
    far_third = to_both(far_third, 1)
    third = to_place(third, 1)
    own, far_own, first, far_first, second = sums(early, other_early, EARLY)
    second = total(second, far_second, far_third, third).astype(jnp.bfloat16)
    first = total(first, to_chip(after(far_first, far_second, third))).astype(jnp.bfloat16)
    first, far_own = lax.optimization_barrier((first, far_own))
    second_here, first_here, far_own = to_place(second, 2), to_place(first, 1), to_chip(far_own)
    return total(own, second_here, first_here, far_own).astype(jnp.bfloat16)


def by_permutes(tokens, expert_ids, route_weights, expert_slot, w_gate, w_up, w_down):
    own = pack(tokens, expert_ids, route_weights, expert_slot, w_gate, w_up, w_down)
    hidden = hidden_units(gather_blocks(own), w_gate, w_up, expert_slot.shape[0])
    matrix = w_down.reshape(-1, w_down.shape[-1])
    rows = tokens.shape[0]
    groups = (EARLY * rows, LATE * rows) * 2
    return reduce_blocks(*down(hidden, matrix, groups))


def by_collectives(tokens, expert_ids, route_weights, expert_slot, w_gate, w_up, w_down):
    members, width, _ = w_gate.shape
    experts = expert_slot.shape[0]
    packed = pack(tokens, expert_ids, route_weights, expert_slot)
    gathered = lax.all_gather(packed, ("node", "local"), axis=0, tiled=True)
    rows = gathered[:, :width]
    tail = gathered[:, width : width + 3 * experts].astype(jnp.float32)
    weights = tail.reshape(-1, 3, experts).sum(axis=1)
    mine = lax.dynamic_slice_in_dim(weights, lax.axis_index("node") * members, members, axis=1)
    gate = jnp.einsum("td,edh->eth", rows, w_gate, preferred_element_type=jnp.float32)
    up = jnp.einsum("td,edh->eth", rows, w_up, preferred_element_type=jnp.float32)
    hidden = (jax.nn.silu(gate) * up * mine.T[..., None]).astype(jnp.bfloat16)
    result = jnp.einsum("eth,ehd->td", hidden, w_down, preferred_element_type=jnp.float32)
    return lax.psum_scatter(
        result.astype(jnp.bfloat16), ("node", "local"), scatter_dimension=0, tiled=True
    )


def per_device(*args):
    small = (lax.axis_size("node"), lax.axis_size("local")) == (2 * CHIPS, PLACES)
    return (by_permutes if small else by_collectives)(*args)


def solution(mesh):
    rows = P(("parts", "node", "local"), None)
    in_specs = (
        rows,
        rows,
        rows,
        P(),
        P("node", None, "local"),
        P("node", None, "local"),
        P("node", "local", None),
    )
    return jax.shard_map(
        per_device, mesh=mesh, in_specs=in_specs, out_specs=rows, check_vma=False
    )
```
